32 devices in a mesh: fsdp: 4 (over y, x), ctx: 8 (over z, core).
Axes of the slice: x: 2, y: 2, z: 4, core: 2. Of those that a mesh axis runs over, the one named last changes fastest.
Arguments:
- tokens: bfloat16 [4, 1024, 768], P('fsdp', 'ctx'), may hold values from -6 to 6
- cotangent: bfloat16 [4, 1024, 768], P('fsdp', 'ctx'), may hold values from -6 to 6
- encoder: bfloat16 [4, 512, 768], P('fsdp', 'ctx'), may hold values from -6 to 6
- expert_ids: int32 [4, 1024, 1], P('fsdp', 'ctx'), may hold values from 0 to 7
- block_order: int32 [16], replicated, may hold values from 0 to 15, as said below
- bucket_table: int32 [1024], replicated, may hold values from 0 to 31, as said below
- first_gain: bfloat16 [768], P('fsdp'), may hold values from 0.099609375 to 1.8984375
- second_gain: bfloat16 [768], P('fsdp'), may hold values from 0.099609375 to 1.8984375
- third_gain: bfloat16 [768], P('fsdp'), may hold values from 0.099609375 to 1.8984375
- position_bias: bfloat16 [32, 12], P('fsdp'), may hold values from -6 to 6
- query_weight: bfloat16 [768, 768], P('fsdp'), may hold values from -0.21875 to 0.21875
- key_weight: bfloat16 [768, 768], P('fsdp'), may hold values from -0.21875 to 0.21875
- value_weight: bfloat16 [768, 768], P('fsdp'), may hold values from -0.21875 to 0.21875
- out_weight: bfloat16 [768, 768], P('fsdp'), may hold values from -1.75 to 1.75
- cross_query: bfloat16 [768, 768], P('fsdp'), may hold values from -0.21875 to 0.21875
- cross_key: bfloat16 [768, 768], P('fsdp'), may hold values from -0.21875 to 0.21875
- cross_value: bfloat16 [768, 768], P('fsdp'), may hold values from -0.21875 to 0.21875
- cross_out: bfloat16 [768, 768], P('fsdp'), may hold values from -1.75 to 1.75
- router_weight: bfloat16 [768, 8], P('fsdp'), may hold values from -0.15625 to 0.15625
- expert_in: bfloat16 [8, 768, 3072], P('ctx', None, 'fsdp'), may hold values from -0.21875 to 0.21875
- expert_out: bfloat16 [8, 3072, 768], P('ctx', 'fsdp'), may hold values from -1.25 to 1.25
Outputs:
- mixed_out: bfloat16 [4, 1024, 768], P('fsdp', 'ctx')
- tokens_grad: float32 [4, 1024, 768], P('fsdp', 'ctx')
- grad_first_gain: float32 [768], P('fsdp')
- grad_second_gain: float32 [768], P('fsdp')
- grad_third_gain: float32 [768], P('fsdp')
- grad_position_bias: float32 [32, 12], P('fsdp')
- grad_query_weight: float32 [768, 768], P('fsdp')
- grad_key_weight: float32 [768, 768], P('fsdp')
- grad_value_weight: float32 [768, 768], P('fsdp')
- grad_out_weight: float32 [768, 768], P('fsdp')
- grad_cross_query: float32 [768, 768], P('fsdp')
- grad_cross_key: float32 [768, 768], P('fsdp')
- grad_cross_value: float32 [768, 768], P('fsdp')
- grad_cross_out: float32 [768, 768], P('fsdp')
- grad_router_weight: float32 [768, 8], P('fsdp')
- grad_expert_in: float32 [8, 768, 3072], P('ctx', None, 'fsdp')
- grad_expert_out: float32 [8, 3072, 768], P('ctx', 'fsdp')
The draws below stay inside these ranges and needn't reach their ends.
Inputs may be any that keep to these rules, and one draw needn't show every extreme that they name: `block_order`: entries 2c and 2c + 1 are k and 15 - k for some k; every value appears once. `bucket_table`: entry d is d for d < 16 and never falls as d grows; every distance from 128 on has bucket 32 - 1.
All inputs are finite; a program needn't handle non-finite values.
Results may differ from the reference program's by a relative error of at most 0.024.
Values may be sent and summed in bfloat16 or wider, within the bound.
No kernel may reach another device: no remote copies, remote signals or barrier semaphores. Data moves between devices by JAX's collectives and lax.ppermute only.
A program may use at most 256 MiB of HBM per device.

```python
import math
import jax
import jax.numpy as jnp
from jax import lax

D = 768
HEADS = 12
HEAD_DIM = 64
FF = 3072
BUCKETS = 32
SEQS = 1
SPAN = 128
LEN = 1024
ENC = 512
SEQ_ALL = 4
HALF = 64
BLOCKS = 16
EXPERTS = 8
CAPACITY = 20
N_FSDP = 4
N_CTX = 8


def draw_block_order(key, part):
    key = jax.random.fold_in(key, 11)
    dealing = jax.random.permutation(key, BLOCKS // 2).astype(jnp.int32)
    return jnp.stack([dealing, BLOCKS - 1 - dealing], axis=1).reshape(BLOCKS).astype(jnp.int32)


def draw_bucket_table(key, part):
    key = jax.random.fold_in(key, 17)
    half_count = BUCKETS // 2
    log_starts = [math.ceil(half_count * 8.0 ** ((bucket - half_count) / half_count) - 1e-09) for bucket in range(half_count + 1, BUCKETS)]
    jitter = jax.random.randint(key, (half_count - 1,), 0, 2).astype(jnp.int32)
    bounds = jnp.array(log_starts, dtype=jnp.int32) + jitter
    distance = jnp.arange(LEN, dtype=jnp.int32)
    upper_bucket = half_count + jnp.sum((distance[:, None] >= bounds[None, :]).astype(jnp.int32), axis=1)
    return jnp.where(distance < half_count, distance, upper_bucket).astype(jnp.int32)


def steps_of(rng, dims, split, low, top_value):
    def one(position, shards_of):
        heights = jax.random.uniform(jax.random.fold_in(jax.random.fold_in(rng, 6), position), (shards_of,), jnp.float32, low / len(split), top_value / len(split))
        return jnp.repeat(jnp.exp(heights), dims[position] // shards_of).reshape((-1,) + (1,) * (len(dims) - position - 1))

    factor_of = one(*split[0])
    for cut in split[1:]:
        factor_of = factor_of * one(*cut)
    return factor_of


def different_ones(stream_key, rows, count, top, lift):
    sequence = jax.random.permutation(jax.random.fold_in(stream_key, 1), count)
    boost = sequence
    for power in range(3):
        boost = boost * boost // count
    boost = boost * lift // count
    chance = jax.random.randint(jax.random.fold_in(stream_key, 2), (rows, count), 0, 4096) + boost
    holders = jax.random.permutation(jax.random.fold_in(stream_key, 3), rows)[jnp.arange(count) % rows]
    chance = jnp.where(jnp.arange(rows)[:, None] == holders[None, :], 1 << 14, chance)
    score = chance * count + jnp.arange(count)
    return lax.top_k(score.astype(jnp.int32), top)[1].astype(jnp.int32)


def scatter_about(rng, extent, width, most, split=(), kind=jnp.bfloat16):
    factor_of = steps_of(rng, extent, split, -0.22, 0.18) if split else 1.0
    result = jax.random.normal(rng, extent, jnp.float32) * width * factor_of
    return jnp.minimum(jnp.maximum(result, -most), most).astype(kind)


def setup_inputs(seed: int = 0) -> dict:
    keys = jax.random.split(jax.random.key(seed), 22)
    return {
        "tokens": scatter_about(keys[0], (SEQ_ALL, LEN, D), 1.0, 6.0, ((0, 4), (1, 8))),
        "cotangent": scatter_about(keys[1], (SEQ_ALL, LEN, D), 1.0, 6.0, ((0, 4), (1, 8))),
        "encoder": scatter_about(keys[2], (SEQ_ALL, ENC, D), 1.0, 6.0, ((0, 4), (1, 8))),
        "expert_ids": different_ones(keys[3], SEQ_ALL * LEN, EXPERTS, 1, 1024).reshape((SEQ_ALL, LEN, 1)),
        "block_order": draw_block_order(jax.random.fold_in(keys[21], 71), 0),
        "bucket_table": draw_bucket_table(jax.random.fold_in(keys[21], 71), 0),
        "first_gain": jnp.clip(1.0 + 0.18 * jax.random.normal(keys[6], (D,), jnp.float32), 0.099609375, 1.8984375).astype(jnp.bfloat16),
        "second_gain": jnp.clip(1.0 + 0.18 * jax.random.normal(keys[7], (D,), jnp.float32), 0.099609375, 1.8984375).astype(jnp.bfloat16),
        "third_gain": jnp.clip(1.0 + 0.18 * jax.random.normal(keys[8], (D,), jnp.float32), 0.099609375, 1.8984375).astype(jnp.bfloat16),
        "position_bias": scatter_about(keys[9], (BUCKETS, HEADS), 1.0, 6.0, ((0, 4),)),
        "query_weight": scatter_about(keys[10], (D, D), D ** -0.5, 0.21875, ((0, 4),)),
        "key_weight": scatter_about(keys[11], (D, D), D ** -0.5, 0.21875, ((0, 4),)),
        "value_weight": scatter_about(keys[12], (D, D), D ** -0.5, 0.21875, ((0, 4),)),
        "out_weight": scatter_about(keys[13], (D, D), (max(1, D * 16 // LEN)) ** -0.5, 1.75, ((0, 4),)),
        "cross_query": scatter_about(keys[14], (D, D), D ** -0.5, 0.21875, ((0, 4),)),
        "cross_key": scatter_about(keys[15], (D, D), D ** -0.5, 0.21875, ((0, 4),)),
        "cross_value": scatter_about(keys[16], (D, D), D ** -0.5, 0.21875, ((0, 4),)),
        "cross_out": scatter_about(keys[17], (D, D), (max(1, D * 8 // ENC)) ** -0.5, 1.75, ((0, 4),)),
        "router_weight": scatter_about(keys[18], (D, EXPERTS), 0.025, 0.15625, ((0, 4),)),
        "expert_in": scatter_about(keys[19], (EXPERTS, D, FF), D ** -0.5, 0.21875, ((0, 8), (2, 4))),
        "expert_out": scatter_about(keys[20], (EXPERTS, FF, D), (0.025 * EXPERTS), 1.25, ((0, 8), (1, 4))),
    }


epsilon = 1e-06
highest = lax.Precision.HIGHEST

@jax.custom_vjp
def low(v):
    return lax.optimization_barrier(v.astype(jnp.bfloat16)).astype(jnp.float32)

@jax.custom_vjp
def low_back(v):
    return v

def low_keep(v):
    return (low(v), None)

def low_pass(kept, grad):
    return (grad,)

def back_keep(v):
    return (v, None)

def back_low(kept, grad):
    return (low(grad),)
low.defvjp(low_keep, low_pass)
low_back.defvjp(back_keep, back_low)

def product(left_rows, right_rows):
    return jnp.dot(left_rows, right_rows, precision=highest, preferred_element_type=jnp.float32)

def rms_norm(values, norm_gain):
    inv_rms = lax.rsqrt(lax.optimization_barrier(jnp.mean(values * values, axis=-1, keepdims=True)) + epsilon)
    return values * inv_rms * norm_gain

def attention(queries, key_rows, value_rows, query_pos, key_pos, dist_bias):
    count = queries.shape[0]
    block_rows = math.gcd(count, 256)
    query_heads = queries.reshape(count // block_rows, block_rows, HEADS, HEAD_DIM)
    pos_blocks = query_pos.reshape(count // block_rows, block_rows)
    key_heads = key_rows.reshape(-1, HEADS, HEAD_DIM)
    value_heads = value_rows.reshape(-1, HEADS, HEAD_DIM)

    def one_block(pieces):
        query_block, pos_block = pieces
        raw_scores = jnp.einsum('qhd,khd->hqk', query_block, key_heads, precision=highest) * 0.125
        scores = low_back(raw_scores)
        if dist_bias is not None:
            distance = pos_block[:, None] - key_pos[None, :]
            bias_rows = jnp.take(dist_bias, jnp.maximum(distance, 0), axis=0)
            scores = scores + jnp.transpose(bias_rows, (2, 0, 1))
            scores = jnp.where(distance[None] >= 0, scores, -1e+30)
        weights = jax.nn.softmax(scores, axis=-1)
        mixed_rows = jnp.einsum('hqk,khd->qhd', low(weights), value_heads, precision=highest)
        return mixed_rows.reshape(block_rows, D)
    return lax.map(jax.checkpoint(one_block), (query_heads, pos_blocks)).reshape(count, D)

def layer(params, hidden, encoded, expert_row, flat_row, keep_row, positions, bucket_table):
    first_gain, second_gain, third_gain, position_bias, query_weight, key_weight, value_weight, out_weight, cross_query, cross_key, cross_value, cross_out, router_weight, expert_in, expert_out = params
    dist_bias = position_bias[bucket_table]
    normed = low(rms_norm(hidden, first_gain))
    queries = low(low_back(product(normed, query_weight)))
    key_rows = low(low_back(product(normed, key_weight)))
    value_rows = low(low_back(product(normed, value_weight)))
    attended = low(low_back(attention(queries, key_rows, value_rows, positions, positions, dist_bias)))
    first_sum = hidden + low_back(product(attended, out_weight))
    normed_two = low(rms_norm(first_sum, second_gain))
    cross_rows = low(low_back(product(normed_two, cross_query)))
    cross_keys = low(low_back(product(encoded, cross_key)))
    cross_values = low(low_back(product(encoded, cross_value)))
    cross_mixed = low(low_back(attention(cross_rows, cross_keys, cross_values, positions, positions, None)))
    second_sum = first_sum + low_back(product(cross_mixed, cross_out))
    normed_three = low(rms_norm(second_sum, third_gain))
    logits = low_back(product(normed_three, router_weight))
    chosen = (expert_row[:, None] == jnp.arange(EXPERTS, dtype=jnp.int32)[None, :]).astype(jnp.float32)
    gate_value = lax.optimization_barrier(jnp.sum(jax.nn.softmax(logits, axis=-1) * chosen, axis=-1))
    slot_rows = N_CTX * CAPACITY
    sent_rows = low_back(normed_three) * keep_row[:, None]
    buffer_rows = jnp.zeros((EXPERTS * slot_rows, D), jnp.float32).at[flat_row].add(sent_rows, mode='drop')
    buffer_rows = buffer_rows.reshape(EXPERTS, slot_rows, D)
    inner = low_back(jnp.einsum('erd,edf->erf', buffer_rows, expert_in, precision=highest))
    activated = low(jax.nn.gelu(inner))
    expert_rows = low(low_back(jnp.einsum('erf,efd->erd', activated, expert_out, precision=highest)))
    returned = jnp.take(expert_rows.reshape(EXPERTS * slot_rows, D), jnp.minimum(flat_row, EXPERTS * slot_rows - 1), axis=0)
    return second_sum + (gate_value * keep_row)[:, None] * returned

def reference(tokens, cotangent, encoder, expert_ids, block_order, bucket_table, first_gain, second_gain, third_gain, position_bias, query_weight, key_weight, value_weight, out_weight, cross_query, cross_key, cross_value, cross_out, router_weight, expert_in, expert_out):
    params = tuple((weight.astype(jnp.float32) for weight in (first_gain, second_gain, third_gain, position_bias, query_weight, key_weight, value_weight, out_weight, cross_query, cross_key, cross_value, cross_out, router_weight, expert_in, expert_out)))
    stored = jnp.arange(LEN, dtype=jnp.int32)
    positions = block_order[stored // HALF] * HALF + stored % HALF
    routes = expert_ids[:, :, 0]
    grouped = routes.reshape(N_FSDP, SEQS, N_CTX, SPAN).transpose(0, 2, 1, 3).reshape(N_FSDP, N_CTX, SEQS * SPAN)
    one_hot = (grouped[..., None] == jnp.arange(EXPERTS, dtype=jnp.int32)).astype(jnp.int32)
    earlier = jnp.cumsum(one_hot, axis=2) - one_hot
    slot_rank = lax.optimization_barrier(jnp.sum(earlier * one_hot, axis=-1))
    slot_rank = slot_rank.reshape(N_FSDP, N_CTX, SEQS, SPAN).transpose(0, 2, 1, 3).reshape(SEQ_ALL, LEN)
    kept_flag = slot_rank < CAPACITY
    slot_rows = N_CTX * CAPACITY
    owner_rank = stored // SPAN
    flat_index = jnp.where(kept_flag, routes * slot_rows + owner_rank[None, :] * CAPACITY + slot_rank, EXPERTS * slot_rows).astype(jnp.int32)
    keep_mask = kept_flag.astype(jnp.float32)

    def one_sequence(running, inputs):
        hidden, encoded, upstream, expert_row, flat_row, keep_row = inputs

        def forward(weights, hidden_in):
            return layer(weights, hidden_in, encoded, expert_row, flat_row, keep_row, positions, bucket_table)
        output, pullback = jax.vjp(forward, params, hidden)
        weight_grads, hidden_grad = pullback(upstream)
        running = jax.tree.map(jnp.add, running, weight_grads)
        return (running, (output.astype(jnp.bfloat16), hidden_grad))
    start_grads = jax.tree.map(jnp.zeros_like, params)
    totals, outputs = lax.scan(one_sequence, start_grads, (tokens.astype(jnp.float32), encoder.astype(jnp.float32), cotangent.astype(jnp.float32), routes, flat_index, keep_mask))
    mixed_out, tokens_grad = outputs
    grad_one, grad_two, grad_three, grad_bias, grad_query, grad_key, grad_value, grad_out, grad_cq, grad_ck, grad_cv, grad_co, grad_router, grad_in, grad_outer = totals
    return (mixed_out, tokens_grad, grad_one, grad_two, grad_three, grad_bias, grad_query, grad_key, grad_value, grad_out, grad_cq, grad_ck, grad_cv, grad_co, grad_router, grad_in, grad_outer)
```

```python
import math
from functools import partial

import jax
import jax.numpy as jnp
from jax import lax
from jax.experimental import pallas as pl
from jax.experimental.pallas import tpu as pltpu
from jax.sharding import PartitionSpec as P

HEADS = 12
HEAD_DIM = 64
BUCKETS = 32
GROUP = 4
OWN_HEADS = HEADS // GROUP
EPSILON = 1e-06
MASKED = -1e30
LOW = jnp.bfloat16
WIDE = jnp.float32
VMEM_LIMIT = 56 * 1024 * 1024
NT = (((1,), (1,)), ((), ()))
TN = (((0,), (0,)), ((), ()))


def swap_fsdp(rows, k):
    size = lax.axis_size("fsdp")
    return lax.ppermute(rows, "fsdp", [(i, i ^ k) for i in range(size)])


def swap_core(rows):
    size = lax.axis_size("ctx")
    return lax.ppermute(rows, "ctx", [(i, i ^ 1) for i in range(size)])


def swap_group(rows, k):
    size = lax.axis_size("ctx")
    return lax.ppermute(rows, "ctx", [(i, i ^ (2 * k)) for i in range(size)])


def shift_rest(rows, r):
    size = lax.axis_size("ctx")
    step = 2 * GROUP * r
    return lax.ppermute(rows, "ctx", [(i, (i + step) % size) for i in range(size)])


def rest_count():
    return lax.axis_size("ctx") // (2 * GROUP)


def block_at(blocks, index):
    return lax.dynamic_index_in_dim(blocks, index, 0, keepdims=False)


def in_order(parts, index):
    parts = list(parts)
    bit = 1
    while bit < len(parts):
        flag = (index & bit) != 0
        parts = [jnp.where(flag, parts[i ^ bit], parts[i]) for i in range(len(parts))]
        bit *= 2
    return parts


def gather_rows(rows):
    own = [rows] + [swap_group(rows, k) for k in range(1, GROUP)]
    other = [swap_core(piece) for piece in own]
    near = jnp.concatenate(own + other, axis=0)
    return jnp.concatenate([near] + [shift_rest(near, r) for r in range(1, rest_count())], axis=0)


def gather_fsdp(rows):
    return [rows] + [swap_fsdp(rows, k) for k in range(1, lax.axis_size("fsdp"))]


def reduce_fsdp(blocks, index):
    total = block_at(blocks, index).astype(WIDE)
    for k in range(1, blocks.shape[0]):
        total = total + swap_fsdp(block_at(blocks, index ^ k), k).astype(WIDE)
    return total


def reduce_group(blocks):
    total = blocks[0].astype(WIDE)
    for k in range(1, GROUP):
        total = total + swap_group(blocks[k], k).astype(WIDE)
    return total


def sum_rest(values):
    size = lax.axis_size("ctx")
    if rest_count() == 1:
        return values
    near = 2 * GROUP
    groups = [list(range(i, size, near)) for i in range(near)]
    return lax.psum(values, "ctx", axis_index_groups=groups)


def place_kernel(turned, index_ref, *refs):
    count = (len(refs) - 1) // 2
    own, other, out = refs[:count], refs[count : 2 * count], refs[-1]
    core = index_ref[2 * count]
    first = pl.program_id(0) < turned
    for k in range(count):
        spot = jnp.where(first, index_ref[count + k], index_ref[k])
        out[0, spot, core] = own[k][0]
        out[0, spot, 1 - core] = other[k][0]


def gather_weights(halves, turned, f_index, g_index, core):
    pieces = gather_fsdp(halves)
    others = [swap_core(piece) for piece in pieces]
    count = len(pieces)
    spots = [f_index ^ k for k in range(count)]
    indices = jnp.stack(spots + [g_index ^ spot for spot in spots] + [core]).astype(jnp.int32)
    number, rows, width = halves.shape
    whole = pl.pallas_call(
        partial(place_kernel, turned),
        out_shape=jax.ShapeDtypeStruct((number, count, 2, rows, width), halves.dtype),
        grid=(number,),
        in_specs=[pl.BlockSpec(memory_space=pltpu.SMEM)]
        + [pl.BlockSpec((1, rows, width), lambda i: (i, 0, 0))] * (2 * count),
        out_specs=pl.BlockSpec((1, count, 2, rows, width), lambda i: (i, 0, 0, 0, 0)),
        compiler_params=pltpu.CompilerParams(vmem_limit_bytes=VMEM_LIMIT),
        name="place_weights",
    )(indices, *pieces, *others)
    return whole.reshape(number, count * 2 * rows, width)


def head_lanes(head, width):
    first = head // 2 * 128
    return first, min(first + 128, width)


def only_head(rows, head):
    if rows.shape[-1] == HEAD_DIM:
        return rows
    lane = lax.broadcasted_iota(jnp.int32, rows.shape, rows.ndim - 1)
    return jnp.where(lane // HEAD_DIM == head % 2, rows, jnp.zeros_like(rows))


def bias_block(kind_ref, tile_ref, head, step, first_block, width):
    rows = []
    for half in range(2):
        columns = []
        for pair in range(width // 128):
            left = kind_ref[2 * step + half, first_block + 2 * pair]
            right = kind_ref[2 * step + half, first_block + 2 * pair + 1]
            columns.append(tile_ref[0, head, left] + tile_ref[1, head, right])
        rows.append(jnp.concatenate(columns, axis=1))
    return jnp.concatenate(rows, axis=0)


def chunk_scores(query_head, key_ref, lanes, first, width, head, step, kind_ref, tile_ref):
    keys = key_ref[pl.ds(first, width), lanes[0] : lanes[1]]
    scores = lax.dot_general(query_head, keys, NT, preferred_element_type=WIDE)
    if kind_ref is not None:
        scores = scores + bias_block(kind_ref, tile_ref, head, step, first // HEAD_DIM, width)
    return scores


def forward_body(step, kind_ref, tile_ref, query_ref, key_ref, value_ref, out_ref, log_ref):
    width = query_ref.shape[-1]
    key_count = key_ref.shape[0]
    chunk = math.gcd(key_count, 1024)
    rows = query_ref.shape[0]
    lane = lax.broadcasted_iota(jnp.int32, (rows, 128), 1)
    logs = jnp.zeros((rows, 128), WIDE)
    tile_out = None
    for head in range(width // HEAD_DIM):
        lanes = head_lanes(head, width)
        query_head = only_head(query_ref[:, lanes[0] : lanes[1]], head) * jnp.asarray(0.125, LOW)

        def one_chunk(index, running):
            top, total, mixed = running
            first = index * chunk
            scores = chunk_scores(
                query_head, key_ref, lanes, first, chunk, head, step, kind_ref, tile_ref
            )
            new_top = jnp.maximum(top, jnp.max(scores, axis=1, keepdims=True))
            weights = jnp.exp(scores - new_top)
            shrink = jnp.exp(top - new_top)
            total = total * shrink + jnp.sum(weights, axis=1, keepdims=True)
            values = value_ref[pl.ds(first, chunk), lanes[0] : lanes[1]]
            mixed = mixed * shrink + jnp.dot(
                weights.astype(LOW), values, preferred_element_type=WIDE
            )
            return new_top, total, mixed

        running = (
            jnp.full((rows, 1), -1e29, WIDE),
            jnp.zeros((rows, 1), WIDE),
            jnp.zeros((rows, lanes[1] - lanes[0]), WIDE),
        )
        if key_count == chunk:
            running = one_chunk(0, running)
        else:
            running = lax.fori_loop(0, key_count // chunk, one_chunk, running)
        top, total, mixed = running
        mixed = only_head(mixed / total, head)
        logs = jnp.where(lane == head, top + jnp.log(total), logs)
        tile_out = mixed if head % 2 == 0 else tile_out + mixed
        if head % 2 == 1 or head == width // HEAD_DIM - 1:
            out_ref[:, lanes[0] : lanes[1]] = tile_out.astype(LOW)
    log_ref[...] = logs


def backward_body(
    step, kind_ref, tile_ref, query_ref, up_ref, log_ref, key_ref, value_ref, dq_ref, dk_ref, dv_ref, sums
):
    width = query_ref.shape[-1]
    key_count = key_ref.shape[0]
    chunk = math.gcd(key_count, 1024)
    rows = query_ref.shape[0]
    tile_out = None
    for head in range(width // HEAD_DIM):
        lanes = head_lanes(head, width)
        query_head = only_head(query_ref[:, lanes[0] : lanes[1]], head) * jnp.asarray(0.125, LOW)
        up_head = only_head(up_ref[:, lanes[0] : lanes[1]], head)
        log_head = log_ref[:, head : head + 1]

        def probs_of(first):
            scores = chunk_scores(
                query_head, key_ref, lanes, first, chunk, head, step, kind_ref, tile_ref
            )
            probs = jnp.exp(scores - log_head)
            values = value_ref[pl.ds(first, chunk), lanes[0] : lanes[1]]
            prob_grad = lax.dot_general(up_head, values, NT, preferred_element_type=WIDE)
            return probs, prob_grad

        def finish(first, probs, prob_grad, delta):
            score_grad = probs * (prob_grad - delta)
            if sums is not None:
                for half in range(2):
                    for pair in range(chunk // 128):
                        block = first // HEAD_DIM + 2 * pair
                        left = kind_ref[2 * step + half, block]
                        right = kind_ref[2 * step + half, block + 1]
                        piece = score_grad[
                            half * HEAD_DIM : (half + 1) * HEAD_DIM, pair * 128 : (pair + 1) * 128
                        ]
                        sums[0, head, left] += piece
                        sums[1, head, right] += piece
            score_low = score_grad.astype(LOW)
            here = pl.ds(first, chunk)
            dk_ref[here, lanes[0] : lanes[1]] += lax.dot_general(
                score_low, query_head, TN, preferred_element_type=WIDE
            )
            dv_ref[here, lanes[0] : lanes[1]] += lax.dot_general(
                probs.astype(LOW), up_head, TN, preferred_element_type=WIDE
            )
            keys = key_ref[here, lanes[0] : lanes[1]]
            return jnp.dot(score_low, keys, preferred_element_type=WIDE)

        if key_count == chunk:
            probs, prob_grad = probs_of(0)
            delta = jnp.sum(probs * prob_grad, axis=1, keepdims=True)
            query_grad = finish(0, probs, prob_grad, delta)
        else:

            def add_delta(index, delta):
                probs, prob_grad = probs_of(index * chunk)
                return delta + jnp.sum(probs * prob_grad, axis=1, keepdims=True)

            delta = lax.fori_loop(0, key_count // chunk, add_delta, jnp.zeros((rows, 1), WIDE))

            def add_grad(index, total):
                probs, prob_grad = probs_of(index * chunk)
                return total + finish(index * chunk, probs, prob_grad, delta)

            query_grad = lax.fori_loop(
                0, key_count // chunk, add_grad, jnp.zeros((rows, lanes[1] - lanes[0]), WIDE)
            )
        query_grad = only_head(query_grad * 0.125, head)
        tile_out = query_grad if head % 2 == 0 else tile_out + query_grad
        if head % 2 == 1 or head == width // HEAD_DIM - 1:
            dq_ref[:, lanes[0] : lanes[1]] = tile_out.astype(LOW)


def self_forward_kernel(kind_ref, tile_ref, query_ref, key_ref, value_ref, out_ref, log_ref):
    forward_body(
        pl.program_id(0), kind_ref, tile_ref, query_ref, key_ref, value_ref, out_ref, log_ref
    )


def self_backward_kernel(
    kind_ref, tile_ref, query_ref, up_ref, log_ref, key_ref, value_ref, dq_ref, dk_out, dv_out, sums, dk_ref, dv_ref
):
    @pl.when(pl.program_id(0) == 0)
    def start():
        dk_ref[...] = jnp.zeros_like(dk_ref)
        dv_ref[...] = jnp.zeros_like(dv_ref)
        sums[...] = jnp.zeros_like(sums)

    backward_body(
        pl.program_id(0), kind_ref, tile_ref, query_ref, up_ref, log_ref, key_ref, value_ref, dq_ref, dk_ref, dv_ref, sums
    )

    @pl.when(pl.program_id(0) == pl.num_programs(0) - 1)
    def end():
        dk_out[...] = dk_ref[...].astype(LOW)
        dv_out[...] = dv_ref[...].astype(LOW)


def cross_forward_kernel(query_ref, key_ref, value_ref, out_ref, log_ref):
    forward_body(0, None, None, query_ref, key_ref, value_ref, out_ref, log_ref)


def cross_backward_kernel(
    query_ref, up_ref, log_ref, key_ref, value_ref, dq_ref, dk_out, dv_out, dk_ref, dv_ref
):
    dk_ref[...] = jnp.zeros_like(dk_ref)
    dv_ref[...] = jnp.zeros_like(dv_ref)
    backward_body(
        0, None, None, query_ref, up_ref, log_ref, key_ref, value_ref, dq_ref, dk_ref, dv_ref, None
    )
    dk_out[...] = dk_ref[...].astype(LOW)
    dv_out[...] = dv_ref[...].astype(LOW)


def cost_of(queries, keys, heads, products):
    return pl.CostEstimate(
        flops=2 * products * queries * keys * heads * HEAD_DIM,
        bytes_accessed=4 * (queries + 2 * keys) * heads * HEAD_DIM,
        transcendentals=queries * keys * heads,
    )


def whole_block(shape):
    return pl.BlockSpec(shape, lambda *index: (0,) * len(shape))


def row_block(rows, width):
    return pl.BlockSpec((rows, width), lambda i, *rest: (i, 0))


def lane_block(rows):
    return pl.BlockSpec((rows, 128), lambda i, *rest: (0, i))


def self_forward(kinds, tiles, queries, keys, values):
    count, width = queries.shape
    rows = 2 * HEAD_DIM
    return pl.pallas_call(
        self_forward_kernel,
        grid_spec=pltpu.PrefetchScalarGridSpec(
            num_scalar_prefetch=1,
            grid=(count // rows,),
            in_specs=[
                whole_block(tiles.shape),
                row_block(rows, width),
                whole_block(keys.shape),
                whole_block(values.shape),
            ],
            out_specs=[row_block(rows, width), row_block(rows, 128)],
        ),
        out_shape=[
            jax.ShapeDtypeStruct((count, width), LOW),
            jax.ShapeDtypeStruct((count, 128), WIDE),
        ],
        compiler_params=pltpu.CompilerParams(vmem_limit_bytes=VMEM_LIMIT),
        cost_estimate=cost_of(count, keys.shape[0], OWN_HEADS, 2),
        name="self_forward",
    )(kinds, tiles, queries, keys, values)


def self_backward(kinds, tiles, queries, up_rows, logs, keys, values):
    count, width = queries.shape
    rows = 2 * HEAD_DIM
    return pl.pallas_call(
        self_backward_kernel,
        grid_spec=pltpu.PrefetchScalarGridSpec(
            num_scalar_prefetch=1,
            grid=(count // rows,),
            in_specs=[
                whole_block(tiles.shape),
                row_block(rows, width),
                row_block(rows, width),
                row_block(rows, 128),
                whole_block(keys.shape),
                whole_block(values.shape),
            ],
            out_specs=[
                row_block(rows, width),
                whole_block(keys.shape),
                whole_block(values.shape),
                whole_block(tiles.shape),
            ],
            scratch_shapes=[pltpu.VMEM(keys.shape, WIDE), pltpu.VMEM(keys.shape, WIDE)],
        ),
        out_shape=[
            jax.ShapeDtypeStruct((count, width), LOW),
            jax.ShapeDtypeStruct(keys.shape, LOW),
            jax.ShapeDtypeStruct(keys.shape, LOW),
            jax.ShapeDtypeStruct(tiles.shape, WIDE),
        ],
        compiler_params=pltpu.CompilerParams(vmem_limit_bytes=VMEM_LIMIT),
        cost_estimate=cost_of(count, keys.shape[0], OWN_HEADS, 5),
        name="self_backward",
    )(kinds, tiles, queries, up_rows, logs, keys, values)


def cross_forward(queries, keys, values):
    count, width = queries.shape
    key_count = keys.shape[0]
    return pl.pallas_call(
        cross_forward_kernel,
        grid=(width // 128,),
        in_specs=[lane_block(count), lane_block(key_count), lane_block(key_count)],
        out_specs=[lane_block(count), lane_block(count)],
        out_shape=[
            jax.ShapeDtypeStruct((count, width), LOW),
            jax.ShapeDtypeStruct((count, width), WIDE),
        ],
        compiler_params=pltpu.CompilerParams(vmem_limit_bytes=VMEM_LIMIT),
        cost_estimate=cost_of(count, key_count, HEADS, 2),
        name="cross_forward",
    )(queries, keys, values)


def cross_backward(queries, up_rows, logs, keys, values):
    count, width = queries.shape
    key_count = keys.shape[0]
    return pl.pallas_call(
        cross_backward_kernel,
        grid=(width // 128,),
        in_specs=[lane_block(count)] * 3 + [lane_block(key_count)] * 2,
        out_specs=[lane_block(count), lane_block(key_count), lane_block(key_count)],
        scratch_shapes=[pltpu.VMEM((key_count, 128), WIDE), pltpu.VMEM((key_count, 128), WIDE)],
        out_shape=[
            jax.ShapeDtypeStruct((count, width), LOW),
            jax.ShapeDtypeStruct(keys.shape, LOW),
            jax.ShapeDtypeStruct(keys.shape, LOW),
        ],
        compiler_params=pltpu.CompilerParams(vmem_limit_bytes=VMEM_LIMIT),
        cost_estimate=cost_of(count, key_count, HEADS, 5),
        name="cross_backward",
    )(queries, up_rows, logs, keys, values)


def tiles_kernel(bound_ref, bias_ref, out_ref):
    shape = (HEAD_DIM, 2 * HEAD_DIM)
    lane = lax.broadcasted_iota(jnp.int32, shape, 1)
    row = lax.broadcasted_iota(jnp.int32, shape, 0)
    left = lane < HEAD_DIM
    offset = row - lane % HEAD_DIM
    for head in range(OWN_HEADS):
        far = jnp.full(shape, bias_ref[BUCKETS - 1, head], WIDE)
        tiles = [jnp.full(shape, MASKED, WIDE)]
        for apart in range(3):
            tile = tiles[0]
            for bucket in range(BUCKETS):
                reached = offset + apart * HEAD_DIM >= bound_ref[bucket]
                tile = jnp.where(reached, bias_ref[bucket, head], tile)
            tiles.append(tile)
        for kind, tile in enumerate(tiles + [far]):
            out_ref[0, head, kind] = jnp.where(left, tile, 0.0)
            out_ref[1, head, kind] = jnp.where(left, 0.0, tile)


def bias_tiles(lower_bounds, own_bias):
    shape = (2, OWN_HEADS, 5, HEAD_DIM, 2 * HEAD_DIM)
    return pl.pallas_call(
        tiles_kernel,
        out_shape=jax.ShapeDtypeStruct(shape, WIDE),
        in_specs=[pl.BlockSpec(memory_space=pltpu.SMEM)] * 2,
        out_specs=pl.BlockSpec(memory_space=pltpu.VMEM),
        name="bias_tiles",
    )(lower_bounds, own_bias)


def bucket_sums(sums, lower_bounds):
    tiles = sums[0, :, 1:, :, :HEAD_DIM] + sums[1, :, 1:, :, HEAD_DIM:]
    shape = (3, HEAD_DIM, HEAD_DIM, BUCKETS)
    distance = (
        lax.broadcasted_iota(jnp.int32, shape, 0) * HEAD_DIM
        + lax.broadcasted_iota(jnp.int32, shape, 1)
        - lax.broadcasted_iota(jnp.int32, shape, 2)
    )
    upper_bounds = jnp.concatenate([lower_bounds[1:], jnp.full((1,), 1 << 30, jnp.int32)])
    hot = ((distance >= lower_bounds) & (distance < upper_bounds)).astype(LOW)
    near = tiles[:, :3].reshape(OWN_HEADS, -1)
    high = near.astype(LOW)
    low = (near - high.astype(WIDE)).astype(LOW)
    both = jnp.dot(
        jnp.concatenate([high, low]), hot.reshape(-1, BUCKETS), preferred_element_type=WIDE
    )
    table = both[:OWN_HEADS] + both[OWN_HEADS:]
    far = jnp.sum(tiles[:, 3], axis=(1, 2))
    return table + jnp.where(jnp.arange(BUCKETS) == BUCKETS - 1, far[:, None], 0.0)


def rms_of(values):
    return lax.rsqrt(jnp.mean(values * values, axis=-1, keepdims=True) + EPSILON)


def norm_grad(values, inv_rms, gain, upstream):
    scaled = gain * upstream
    inner = jnp.mean(scaled * values, axis=-1, keepdims=True)
    return inv_rms * scaled - values * (inv_rms * inv_rms * inv_rms * inner)


def dot(left, right):
    return jnp.dot(left, right, preferred_element_type=WIDE)


def dot_nt(left, right):
    return lax.dot_general(left, right, NT, preferred_element_type=WIDE)


def dot_tn(left, right):
    return lax.dot_general(left, right, TN, preferred_element_type=WIDE)


def on_device(
    tokens,
    cotangent,
    encoder,
    expert_ids,
    block_order,
    bucket_table,
    first_gain,
    second_gain,
    third_gain,
    position_bias,
    query_weight,
    key_weight,
    value_weight,
    out_weight,
    cross_query,
    cross_key,
    cross_value,
    cross_out,
    router_weight,
    expert_in,
    expert_out,
):
    ctx_size = lax.axis_size("ctx")
    fsdp_size = lax.axis_size("fsdp")
    rests = rest_count()
    f_index = lax.axis_index("fsdp")
    ctx_index = lax.axis_index("ctx")
    core = ctx_index % 2
    group = (ctx_index // 2) % GROUP
    rest = ctx_index // (2 * GROUP)
    seq_count, span, width = tokens.shape
    shard = width // fsdp_size
    own_width = width // GROUP
    half_shard = shard // 2
    half_width = width // 2
    experts = expert_in.shape[0] * ctx_size
    capacity = (5 * seq_count * span + 4 * experts - 1) // (4 * experts)
    hidden_low = tokens.reshape(span, width)
    upstream = cotangent.reshape(span, width).astype(WIDE)

    small = jnp.concatenate(
        [
            first_gain[None],
            second_gain[None],
            third_gain[None],
            router_weight.T,
            jnp.pad(position_bias.reshape(1, -1), ((0, 0), (0, shard - position_bias.size))),
        ]
    )
    small = jnp.pad(small, ((0, -small.shape[0] % 16), (0, 0)))
    small_full = jnp.stack(in_order(gather_fsdp(small), f_index))
    rows_all = gather_rows(hidden_low)
    own_columns = [
        lax.dynamic_slice(
            weight, (core * half_shard, group * own_width), (half_shard, own_width)
        )
        for weight in (query_weight, key_weight, value_weight)
    ]
    own_qkv = gather_weights(
        jnp.concatenate(own_columns, axis=1)[None], 0, f_index, group, core
    )[0]
    halves = jnp.stack(
        [
            lax.dynamic_slice_in_dim(weight, core * half_shard, half_shard, 0)
            for weight in (out_weight, cross_query, cross_key, cross_value, cross_out)
        ]
    )
    dense = gather_weights(halves, 1, f_index, group, core)
    out_full, cross_q_full, cross_k_full, cross_v_full, cross_o_full = (dense[i] for i in range(5))
    encoder_all = gather_rows(encoder.reshape(-1, width))

    gain_one = small_full[:, 0].reshape(width).astype(WIDE)
    gain_two = small_full[:, 1].reshape(width).astype(WIDE)
    gain_three = small_full[:, 2].reshape(width).astype(WIDE)
    router_full = small_full[:, 3 : 3 + experts].transpose(1, 0, 2).reshape(experts, width)
    bias_full = small_full[:, 3 + experts, : position_bias.size].reshape(BUCKETS, HEADS)

    slots = jnp.arange(GROUP, dtype=jnp.int32)
    key_devices = (
        ((rest - jnp.arange(rests, dtype=jnp.int32)) % rests)[:, None, None] * (2 * GROUP)
        + (group ^ slots)[None, None, :] * 2
        + (core ^ jnp.arange(2, dtype=jnp.int32))[None, :, None]
    ).reshape(-1)
    key_blocks = (key_devices[:, None] * 2 + jnp.arange(2, dtype=jnp.int32)[None]).reshape(-1)
    block_count = block_order.shape[0]
    hits = key_blocks[:, None] == jnp.arange(block_count, dtype=jnp.int32)[None]
    key_places = jnp.sum(jnp.where(hits, block_order[None], 0), axis=1)
    query_places = key_places[: 2 * GROUP]
    kinds = jnp.clip(query_places[:, None] - key_places[None], -1, 3) + 1
    lower_bounds = jnp.sum(
        (bucket_table[:, None] < jnp.arange(BUCKETS, dtype=jnp.int32)[None]).astype(jnp.int32),
        axis=0,
    )
    own_bias = lax.dynamic_slice_in_dim(
        bias_full.astype(WIDE), group * OWN_HEADS, OWN_HEADS, 1
    )
    tiles = bias_tiles(lower_bounds, own_bias)

    routes = expert_ids.reshape(-1)
    chosen = routes[:, None] == jnp.arange(experts, dtype=jnp.int32)[None]
    order = jnp.arange(span)
    lower = (order[:, None] > order[None]).astype(LOW)
    earlier = dot(lower, chosen.astype(LOW))
    slot_rank = jnp.sum(jnp.where(chosen, earlier, 0.0), axis=1).astype(jnp.int32)
    block_rows = -(-2 * capacity // 8) * 8
    slot_rows = rests * GROUP * block_rows
    target = (
        (((routes // (2 * GROUP) - rest) % rests) * GROUP + (((routes // 2) % GROUP) ^ group))
        * block_rows
        + core * capacity
        + slot_rank
    )
    code = jnp.where(slot_rank < capacity, (routes % 2) * slot_rows + target, -1)
    own_code = jnp.broadcast_to(code.astype(WIDE)[:, None], (span, 128))
    other_code = swap_core(own_code)
    codes = jnp.concatenate([own_code[:, :1], other_code[:, :1]]).astype(jnp.int32)
    placing = (
        codes == core * slot_rows + jnp.arange(slot_rows, dtype=jnp.int32)[None]
    ).astype(LOW)
    chosen = chosen.astype(WIDE)

    wide_rows = rows_all.astype(WIDE)
    normed_all = (wide_rows * rms_of(wide_rows) * gain_one).astype(LOW)
    own_count = GROUP * span
    normed_own = normed_all[:own_count]
    queries = dot(normed_own, own_qkv[:, :own_width]).astype(LOW)
    key_rows = dot(normed_all, own_qkv[:, own_width : 2 * own_width]).astype(LOW)
    value_rows = dot(normed_all, own_qkv[:, 2 * own_width :]).astype(LOW)
    attended_own, self_logs = self_forward(kinds, tiles, queries, key_rows, value_rows)
    attended = jnp.concatenate(
        [attended_own[:span]]
        + [swap_group(attended_own[k * span : (k + 1) * span], k) for k in range(1, GROUP)],
        axis=1,
    )
    hidden = hidden_low.astype(WIDE)
    first_sum = hidden + dot(attended, out_full)
    inv_two = rms_of(first_sum)
    normed_two = (first_sum * inv_two * gain_two).astype(LOW)

    cross_keys = dot(encoder_all, cross_k_full).astype(LOW)
    cross_values = dot(encoder_all, cross_v_full).astype(LOW)
    cross_rows = dot(normed_two, cross_q_full).astype(LOW)
    cross_mixed, cross_logs = cross_forward(cross_rows, cross_keys, cross_values)
    second_sum = first_sum + dot(cross_mixed, cross_o_full)
    inv_three = rms_of(second_sum)
    normed_three = (second_sum * inv_three * gain_three).astype(LOW)

    logits = dot_nt(normed_three, router_full)
    router_probs = jax.nn.softmax(logits, axis=-1)
    gate_value = jnp.sum(router_probs * chosen, axis=-1, keepdims=True)
    scaled_up = (gate_value * upstream).astype(LOW)

    def dispatch(rows):
        both = jnp.concatenate([rows, swap_core(rows)])
        sent = dot_tn(placing, both).astype(LOW).reshape(rests, GROUP * block_rows, width)
        near = jnp.concatenate(
            [sent[0]] + [shift_rest(sent[r], r) for r in range(1, rests)]
        ).reshape(rests, GROUP, block_rows, width)
        arrived = jnp.concatenate(
            [near[:, 0]] + [swap_group(near[:, k], k) for k in range(1, GROUP)], axis=1
        ).reshape(slot_rows, width)
        return jnp.concatenate(gather_fsdp(arrived))

    def bring_back(rows):
        parts = rows.astype(LOW).reshape(fsdp_size, slot_rows, width)
        total = parts[0].astype(WIDE)
        for k in range(1, fsdp_size):
            total = total + swap_fsdp(parts[k], k).astype(WIDE)
        total = total.astype(LOW).reshape(rests, GROUP, block_rows, width)
        near = jnp.concatenate(
            [total[:, 0]] + [swap_group(total[:, k], k) for k in range(1, GROUP)], axis=1
        ).reshape(rests, GROUP * block_rows, width)
        home = jnp.concatenate(
            [near[0]] + [shift_rest(near[r], -r) for r in range(1, rests)]
        )
        both = dot(placing, home).astype(LOW)
        return both[:span].astype(WIDE) + swap_core(both[span:]).astype(WIDE)

    expert_rows_in = dispatch(normed_three)
    expert_up = dispatch(scaled_up)
    in_shard = expert_in[0]
    out_shard = expert_out[0]
    inner = dot(expert_rows_in, in_shard)
    gelu_value, gelu_pull = jax.vjp(jax.nn.gelu, inner)
    activated = gelu_value.astype(LOW)
    moe_rows = bring_back(dot(activated, out_shard))
    (inner_grad,) = gelu_pull(dot_nt(expert_up, out_shard))
    inner_low = inner_grad.astype(LOW)
    dispatch_grad = bring_back(dot_nt(inner_low, in_shard))
    grad_expert_out = dot_tn(activated, expert_up)[None]
    grad_expert_in = dot_tn(expert_rows_in, inner_low)[None]

    mixed_out = (second_sum + gate_value * moe_rows).astype(LOW).reshape(tokens.shape)
    gate_grad = jnp.sum(upstream * moe_rows, axis=-1, keepdims=True)
    logit_low = (gate_grad * gate_value * (chosen - router_probs)).astype(LOW)
    three_grad = dispatch_grad + dot(logit_low, router_full)
    second_grad = upstream + norm_grad(second_sum, inv_three, gain_three, three_grad)
    gain_three_part = jnp.sum(three_grad * second_sum * inv_three, axis=0, keepdims=True)
    router_part = dot_tn(logit_low, normed_three)
    spread = jnp.concatenate([router_part, gain_three_part])
    spread = jnp.pad(spread, ((0, -spread.shape[0] % 8), (0, 0)))
    spread = spread + swap_core(spread)
    bit = 1
    while bit < fsdp_size:
        spread = spread + swap_fsdp(spread, bit)
        bit *= 2
    bit = 1
    while bit < GROUP:
        spread = spread + swap_group(spread, bit)
        bit *= 2
    spread = sum_rest(spread)
    spread = lax.dynamic_slice_in_dim(spread, f_index * shard, shard, 1)
    grad_router = spread[: router_part.shape[0]].T
    grad_gain_three = spread[router_part.shape[0]]

    def own_half(values):
        return lax.dynamic_slice_in_dim(values, core * half_width, half_width, 1)

    def other_half(values):
        return lax.dynamic_slice_in_dim(values, (1 - core) * half_width, half_width, 1)

    def pair_grad(rows, grads):
        both_rows = jnp.concatenate([rows, swap_core(rows)])
        both_grads = jnp.concatenate([own_half(grads), swap_core(other_half(grads))])
        return dot_tn(both_rows, both_grads).astype(LOW)

    def shard_of(grad, index):
        return reduce_fsdp(grad.reshape(fsdp_size, shard, half_width), index)

    def finish_weights(parts):
        both = jnp.stack(parts).astype(LOW)
        half_rows, quarter_rows = shard // 2, shard // 4
        low_bit, high_bit = group & 1, group >> 1
        both = lax.dynamic_slice_in_dim(both, low_bit * half_rows, half_rows, 1).astype(
            WIDE
        ) + swap_group(
            lax.dynamic_slice_in_dim(both, (1 - low_bit) * half_rows, half_rows, 1), 1
        ).astype(WIDE)
        both = both.astype(LOW)
        both = lax.dynamic_slice_in_dim(both, high_bit * quarter_rows, quarter_rows, 1).astype(
            WIDE
        ) + swap_group(
            lax.dynamic_slice_in_dim(both, (1 - high_bit) * quarter_rows, quarter_rows, 1), 2
        ).astype(WIDE)
        own = sum_rest(both).astype(LOW)
        pieces = [own] + [swap_group(own, k) for k in range(1, GROUP)]
        others = [swap_core(piece) for piece in pieces]
        pieces = in_order(pieces, group)
        others = in_order(others, group)
        ordered = [0, 2, 1, 3]
        mine = jnp.concatenate([pieces[i] for i in ordered], axis=1)
        theirs = jnp.concatenate([others[i] for i in ordered], axis=1)
        left, right = in_order([mine, theirs], core)
        whole = jnp.concatenate([left, right], axis=2).astype(WIDE)
        return [whole[i] for i in range(len(parts))]

    branch_two = second_grad.astype(LOW)
    cross_up = dot_nt(branch_two, cross_o_full).astype(LOW)
    cross_q_low, cross_k_part, cross_v_part = cross_backward(
        cross_rows, cross_up, cross_logs, cross_keys, cross_values
    )
    two_grad = dot_nt(cross_q_low, cross_q_full)
    first_grad = second_grad + norm_grad(first_sum, inv_two, gain_two, two_grad)

    branch_one = first_grad.astype(LOW)
    self_up = dot_nt(branch_one, out_full).astype(LOW)
    up_own = jnp.concatenate(
        [self_up[:, :own_width]]
        + [
            swap_group(self_up[:, k * own_width : (k + 1) * own_width], k)
            for k in range(1, GROUP)
        ],
    )
    query_low, key_part, value_part, bias_parts = self_backward(
        kinds, tiles, queries, up_own, self_logs, key_rows, value_rows
    )

    def home_rows(part):
        near = part[: 2 * own_count].astype(WIDE)
        for r in range(1, rests):
            piece = part[r * 2 * own_count : (r + 1) * 2 * own_count]
            near = near + shift_rest(piece, -r).astype(WIDE)
        other = near[own_count:].astype(LOW)
        return (near[:own_count] + swap_core(other).astype(WIDE)).astype(LOW)

    qkv_low = jnp.concatenate([query_low, home_rows(key_part), home_rows(value_part)], axis=1)
    one_part = dot_nt(qkv_low, own_qkv).astype(LOW)
    one_grad = reduce_group(one_part.reshape(GROUP, span, width))
    tokens_grad = first_grad + norm_grad(hidden, rms_of(hidden), gain_one, one_grad)
    tokens_grad = tokens_grad.reshape(tokens.shape)

    cross_o_grad = shard_of(pair_grad(cross_mixed, branch_two), f_index)
    cross_q_grad = shard_of(pair_grad(normed_two, cross_q_low), f_index)

    def encoder_grad(part):
        theirs = swap_core(other_half(part)).reshape(rests, 2, -1, half_width)
        theirs = jnp.concatenate([theirs[:, 1:], theirs[:, :1]], axis=1)
        half = own_half(part).astype(WIDE) + theirs.reshape(-1, half_width).astype(WIDE)
        return dot_tn(encoder_all, half.astype(LOW)).astype(LOW)

    cross_k_grad = shard_of(encoder_grad(cross_k_part), f_index)
    cross_v_grad = shard_of(encoder_grad(cross_v_part), f_index)
    out_grad = shard_of(pair_grad(attended, branch_one), f_index ^ group)
    cross_q_total, cross_k_total, cross_v_total, cross_o_total = finish_weights(
        [cross_q_grad, cross_k_grad, cross_v_grad, cross_o_grad]
    )
    (out_total,) = finish_weights([out_grad])

    qkv_grad = dot_tn(normed_own, qkv_low).astype(LOW)
    qkv_grad = qkv_grad.reshape(fsdp_size, 2, half_shard, 3 * own_width)
    mine = lax.dynamic_index_in_dim(qkv_grad, core, 1, keepdims=False).astype(WIDE)
    theirs = lax.dynamic_index_in_dim(qkv_grad, 1 - core, 1, keepdims=False)
    qkv_grad = (mine + swap_core(theirs).astype(WIDE)).astype(LOW)
    qkv_shard = sum_rest(reduce_fsdp(qkv_grad, f_index)).astype(LOW)
    pieces = [qkv_shard] + [swap_group(qkv_shard, k) for k in range(1, GROUP)]
    others = [swap_core(piece) for piece in pieces]
    pieces = in_order(pieces, group)
    others = in_order(others, group)

    def columns_of(parts, which):
        return jnp.concatenate(
            [part[:, which * own_width : (which + 1) * own_width] for part in parts], axis=1
        )

    qkv_totals = []
    for which in range(3):
        top, bottom = in_order([columns_of(pieces, which), columns_of(others, which)], core)
        qkv_totals.append(jnp.concatenate([top, bottom]).astype(WIDE))
    query_total, key_total, value_total = qkv_totals

    grad_gain_one = sum(
        jnp.sum(weight.astype(WIDE) * total, axis=1)
        for weight, total in (
            (query_weight, query_total),
            (key_weight, key_total),
            (value_weight, value_total),
        )
    ) / first_gain.astype(WIDE)
    grad_gain_two = jnp.sum(cross_query.astype(WIDE) * cross_q_total, axis=1) / second_gain.astype(
        WIDE
    )

    table = bucket_sums(bias_parts, lower_bounds)
    table = jnp.pad(table, ((0, -table.shape[0] % 8), (0, 128 - BUCKETS)))
    table = table + swap_core(table)
    table = sum(gather_fsdp(table))
    table = sum_rest(table)
    tables = in_order([table] + [swap_group(table, k) for k in range(1, GROUP)], group)
    table_full = jnp.concatenate([one[:OWN_HEADS, :BUCKETS] for one in tables])
    bias_rows = BUCKETS // fsdp_size
    bias_total = lax.dynamic_slice_in_dim(table_full, f_index * bias_rows, bias_rows, 1).T

    return (
        mixed_out,
        tokens_grad,
        grad_gain_one,
        grad_gain_two,
        grad_gain_three,
        bias_total,
        query_total,
        key_total,
        value_total,
        out_total,
        cross_q_total,
        cross_k_total,
        cross_v_total,
        cross_o_total,
        grad_router,
        grad_expert_in,
        grad_expert_out,
    )


def solution(mesh):
    rows = P("fsdp", "ctx", None)
    vector = P("fsdp")
    matrix = P("fsdp", None)
    expert_specs = (P("ctx", None, "fsdp"), P("ctx", "fsdp", None))
    return jax.shard_map(
        on_device,
        mesh=mesh,
        in_specs=(rows,) * 4 + (P(),) * 2 + (vector,) * 3 + (matrix,) * 10 + expert_specs,
        out_specs=(rows,) * 2 + (vector,) * 3 + (matrix,) * 10 + expert_specs,
        check_vma=False,
    )
```

```python
import math
from functools import partial

import jax
import jax.numpy as jnp
from jax import lax
from jax.experimental import pallas as pl
from jax.experimental.pallas import tpu as pltpu
from jax.sharding import PartitionSpec as P

HEADS = 12
HEAD_DIM = 64
BUCKETS = 32
GROUP = 4
OWN_HEADS = HEADS // GROUP
EPSILON = 1e-06
MASKED = -1e30
LOW = jnp.bfloat16
WIDE = jnp.float32
VMEM_LIMIT = 56 * 1024 * 1024
NT = (((1,), (1,)), ((), ()))
TN = (((0,), (0,)), ((), ()))


def swap_fsdp(rows, k):
    size = lax.axis_size("fsdp")
    return lax.ppermute(rows, "fsdp", [(i, i ^ k) for i in range(size)])


def swap_core(rows):
    size = lax.axis_size("ctx")
    return lax.ppermute(rows, "ctx", [(i, i ^ 1) for i in range(size)])


def swap_group(rows, k):
    size = lax.axis_size("ctx")
    return lax.ppermute(rows, "ctx", [(i, i ^ (2 * k)) for i in range(size)])


def shift_rest(rows, r):
    size = lax.axis_size("ctx")
    step = 2 * GROUP * r
    return lax.ppermute(rows, "ctx", [(i, (i + step) % size) for i in range(size)])


def rest_count():
    return lax.axis_size("ctx") // (2 * GROUP)


def block_at(blocks, index):
    return lax.dynamic_index_in_dim(blocks, index, 0, keepdims=False)


def in_order(parts, index):
    parts = list(parts)
    bit = 1
    while bit < len(parts):
        flag = (index & bit) != 0
        parts = [jnp.where(flag, parts[i ^ bit], parts[i]) for i in range(len(parts))]
        bit *= 2
    return parts


def tie(*values):
    return lax.optimization_barrier(values)


def after(value, *earlier):
    return tie(value, *earlier)[0]


def gather_group(rows):
    return [rows] + [swap_group(rows, k) for k in range(1, GROUP)]


def gather_fsdp(rows):
    return [rows] + [swap_fsdp(rows, k) for k in range(1, lax.axis_size("fsdp"))]


def sum_rest(values):
    size = lax.axis_size("ctx")
    if rest_count() == 1:
        return values
    near = 2 * GROUP
    groups = [list(range(i, size, near)) for i in range(near)]
    return lax.psum(values, "ctx", axis_index_groups=groups)


def takes(us):
    return pl.CostEstimate(flops=int(us * 1e9), bytes_accessed=int(us * 3.5e6), transcendentals=0)


def vmem(count):
    return [pl.BlockSpec(memory_space=pltpu.VMEM)] * count


def smem():
    return pl.BlockSpec(memory_space=pltpu.SMEM)


def pack_kernel(index_ref, small_ref, *refs):
    group, core = index_ref[0], index_ref[1]
    ins, (qkv_ref, early_ref, late_ref) = refs[:-3], refs[-3:]
    rows = early_ref.shape[1]
    own = qkv_ref.shape[1] // 3
    shard = 2 * rows
    for choice in range(GROUP):

        @pl.when(group == choice)
        def take():
            for which in range(3):
                qkv_ref[:shard, which * own : (which + 1) * own] = ins[which][
                    :, choice * own : (choice + 1) * own
                ]

    qkv_ref[shard:] = jnp.zeros((small_ref.shape[0], 3 * own), LOW)
    qkv_ref[shard:, :shard] = small_ref[...]
    here = pl.ds(pl.multiple_of(core * rows, 16), rows)
    early = early_ref.shape[0]
    for i in range(early):
        early_ref[i] = ins[3 + i][here]
    for i in range(late_ref.shape[0]):
        late_ref[i] = ins[3 + early + i][here]


def pack_weights(small, weights, early, group, core):
    shard, width = weights[0].shape
    own = width // GROUP
    late = len(weights) - 3 - early
    return pl.pallas_call(
        pack_kernel,
        out_shape=[
            jax.ShapeDtypeStruct((shard + small.shape[0], 3 * own), LOW),
            jax.ShapeDtypeStruct((early, shard // 2, width), LOW),
            jax.ShapeDtypeStruct((late, shard // 2, width), LOW),
        ],
        in_specs=[smem()] + vmem(1 + len(weights)),
        out_specs=vmem(3),
        compiler_params=pltpu.CompilerParams(vmem_limit_bytes=VMEM_LIMIT),
        cost_estimate=takes(3),
        name="pack_weights",
    )(jnp.stack([group, core]).astype(jnp.int32), small, *weights)


def place_qkv_kernel(index_ref, *refs):
    pieces, (out, small) = refs[:-2], refs[-2:]
    rows = out.shape[1]
    for k in range(len(pieces)):
        out[index_ref[k]] = pieces[k][:rows]
        small[index_ref[k]] = pieces[k][rows:, :rows]


def place_qkv(pieces, extra, f_index):
    count = len(pieces)
    rows, width = pieces[0].shape
    rows = rows - extra
    whole, small = pl.pallas_call(
        place_qkv_kernel,
        out_shape=[
            jax.ShapeDtypeStruct((count, rows, width), LOW),
            jax.ShapeDtypeStruct((count, extra, rows), LOW),
        ],
        in_specs=[smem()] + vmem(count),
        out_specs=vmem(2),
        compiler_params=pltpu.CompilerParams(vmem_limit_bytes=VMEM_LIMIT),
        cost_estimate=takes(2.3),
        name="place_qkv",
    )(jnp.stack([f_index ^ k for k in range(count)]).astype(jnp.int32), *pieces)
    return whole.reshape(count * rows, width), small


def stack_kernel(turned, index_ref, *refs):
    count = len(refs) - 1
    out = refs[-1]
    for item in range(out.shape[0]):
        for k in range(count):
            spot = index_ref[count + k] if item < turned else index_ref[k]
            out[item, spot] = refs[k][item]


def stack_pieces(pieces, turned, f_index, g_index):
    count = len(pieces)
    spots = [f_index ^ k for k in range(count)]
    indices = jnp.stack(spots + [g_index ^ spot for spot in spots]).astype(jnp.int32)
    number, rows, width = pieces[0].shape
    return pl.pallas_call(
        partial(stack_kernel, turned),
        out_shape=jax.ShapeDtypeStruct((number, count, rows, width), LOW),
        in_specs=[smem()] + vmem(count),
        out_specs=vmem(1)[0],
        compiler_params=pltpu.CompilerParams(vmem_limit_bytes=VMEM_LIMIT),
        cost_estimate=takes(2.7),
        name="stack_pieces",
    )(indices, *pieces)


def weave_kernel(index_ref, mine_ref, theirs_ref, *outs):
    core = index_ref[0]
    for item, out in enumerate(outs):
        for block in range(out.shape[0]):
            out[block, core] = mine_ref[item, block]
            out[block, 1 - core] = theirs_ref[item, block]


def weave_halves(mine, theirs, core):
    number, count, rows, width = mine.shape
    whole = pl.pallas_call(
        weave_kernel,
        out_shape=[jax.ShapeDtypeStruct((count, 2, rows, width), LOW)] * number,
        in_specs=[smem()] + vmem(2),
        out_specs=vmem(number),
        compiler_params=pltpu.CompilerParams(vmem_limit_bytes=VMEM_LIMIT),
        cost_estimate=takes(4),
        name="weave_halves",
    )(core.reshape(1).astype(jnp.int32), mine, theirs)
    return [one.reshape(count * 2 * rows, width) for one in whole]


def expert_kernel(*refs):
    count = (len(refs) - 3) // 2
    pieces, in_ref, out_ref = refs[:count], refs[count], refs[count + 1]
    answers, middle = refs[count + 2 : 2 * count + 2], refs[-1]
    rows, width = pieces[0].shape[0], pieces[0].shape[1] // 2
    hidden = in_ref.shape[1]
    scale = math.sqrt(2 / math.pi)
    for k in range(count):
        inner = dot(pieces[k][:, :width], in_ref[...])
        square = inner * inner
        bent = jnp.tanh(scale * (inner + 0.044715 * (inner * square)))
        activated = (0.5 * inner * (1.0 + bent)).astype(LOW)
        slope = 0.5 * (1.0 + bent) + 0.5 * inner * (1.0 - bent * bent) * (
            scale * (1.0 + 3 * 0.044715 * square)
        )
        inner_low = (dot_nt(pieces[k][:, width:], out_ref[...]) * slope).astype(LOW)
        answers[k][:, :width] = dot(activated, out_ref[...]).astype(LOW)
        answers[k][:, width:] = dot_nt(inner_low, in_ref[...]).astype(LOW)
        here = slice(k * rows, (k + 1) * rows)
        middle[here, :hidden] = activated
        middle[here, hidden:] = inner_low


def run_experts(pieces, expert_in, expert_out):
    count = len(pieces)
    width, hidden = expert_in.shape
    rows = pieces[0].shape[0]
    results = pl.pallas_call(
        expert_kernel,
        out_shape=[jax.ShapeDtypeStruct((rows, 2 * width), LOW)] * count
        + [jax.ShapeDtypeStruct((count * rows, 2 * hidden), LOW)],
        in_specs=vmem(count + 2),
        out_specs=vmem(count + 1),
        compiler_params=pltpu.CompilerParams(vmem_limit_bytes=VMEM_LIMIT),
        cost_estimate=takes(8.2),
        name="experts",
    )(*pieces, expert_in, expert_out)
    return list(results[:count]), results[count]


def expert_grads_kernel(*refs):
    pieces, (middle, in_ref, out_ref) = refs[:-3], refs[-3:]
    width, hidden = in_ref.shape
    rows = jnp.concatenate([piece[...] for piece in pieces])
    in_ref[...] = dot_tn(rows[:, :width], middle[:, hidden:])
    out_ref[...] = dot_tn(middle[:, :hidden], rows[:, width:])


def expert_grads(pieces, middle):
    width = pieces[0].shape[1] // 2
    hidden = middle.shape[1] // 2
    return pl.pallas_call(
        expert_grads_kernel,
        out_shape=[
            jax.ShapeDtypeStruct((width, hidden), WIDE),
            jax.ShapeDtypeStruct((hidden, width), WIDE),
        ],
        in_specs=vmem(1 + len(pieces)),
        out_specs=vmem(2),
        compiler_params=pltpu.CompilerParams(vmem_limit_bytes=VMEM_LIMIT),
        cost_estimate=takes(5.7),
        name="expert_grads",
    )(*pieces, middle)


def home_kernel(rests, *refs):
    pieces, outs = refs[: len(refs) - GROUP], refs[len(refs) - GROUP :]
    block = outs[0].shape[0] // rests
    for k, out in enumerate(outs):
        for r in range(rests):
            here = slice((r * GROUP + k) * block, (r * GROUP + k + 1) * block)
            out[r * block : (r + 1) * block] = sum_low(
                pieces[0][here], [piece[here] for piece in pieces[1:]]
            )


def sum_home(pieces, rests):
    rows, width = pieces[0].shape
    return pl.pallas_call(
        partial(home_kernel, rests),
        out_shape=[jax.ShapeDtypeStruct((rows // GROUP, width), LOW)] * GROUP,
        in_specs=vmem(len(pieces)),
        out_specs=vmem(GROUP),
        compiler_params=pltpu.CompilerParams(vmem_limit_bytes=VMEM_LIMIT),
        cost_estimate=takes(2.4),
        name="sum_home",
    )(*pieces)


def grads_kernel(turns, extra_rows, index_ref, *refs):
    f_index, core, turn = index_ref[0], index_ref[1], index_ref[2]
    ins, spread_ref, keep, send = refs[: 2 * len(turns)], refs[-3], refs[-2], refs[-1]
    size, _, half = keep.shape
    shard = ins[0].shape[1] // size
    for item, turned in enumerate(turns):
        rows_ref, grad_ref = ins[2 * item], ins[2 * item + 1]
        for out, side in ((keep, core), (send, 1 - core)):
            grad = grad_ref[:, pl.ds(pl.multiple_of(side * half, 128), half)]
            product = dot_tn(rows_ref[...], grad).astype(LOW)
            for block in range(size):
                spot = block ^ f_index ^ (turn if turned else 0)
                out[spot, item * shard : (item + 1) * shard] = product[
                    block * shard : (block + 1) * shard
                ]
    first = len(turns) * shard
    for block in range(size):
        spot = block ^ f_index
        piece = spread_ref[:, block * shard : (block + 1) * shard].astype(LOW)
        keep[spot, first:] = jnp.zeros((extra_rows, half), LOW)
        send[spot, first:] = jnp.zeros((extra_rows, half), LOW)
        keep[spot, first : first + spread_ref.shape[0], :shard] = piece


def weight_grads(turns, pairs, spread, extra_rows, f_index, core, turn, size):
    width = pairs[0][0].shape[1]
    rows = len(turns) * (width // size) + extra_rows
    shape = jax.ShapeDtypeStruct((size, rows, width // 2), LOW)
    flat = [array for pair in pairs for array in pair] + [spread]
    return pl.pallas_call(
        partial(grads_kernel, turns, extra_rows),
        out_shape=[shape, shape],
        in_specs=[smem()] + vmem(len(flat)),
        out_specs=vmem(2),
        compiler_params=pltpu.CompilerParams(vmem_limit_bytes=VMEM_LIMIT),
        cost_estimate=takes(7.5),
        name="weight_grads",
    )(jnp.stack([f_index, core, turn]).astype(jnp.int32), *flat)


def add_low(left, right):
    return (left.astype(WIDE) + right.astype(WIDE)).astype(LOW)


def sum_low(first, others):
    total = first.astype(WIDE)
    for other in others:
        total = total + other.astype(WIDE)
    return total.astype(LOW)


def add_kernel(keep_ref, received_ref, *outs):
    for k, out in enumerate(outs):
        out[...] = add_low(keep_ref[k], received_ref[k])


def add_pieces(keep, received):
    size = keep.shape[0]
    return pl.pallas_call(
        add_kernel,
        out_shape=[jax.ShapeDtypeStruct(keep.shape[1:], LOW)] * size,
        in_specs=vmem(2),
        out_specs=vmem(size),
        compiler_params=pltpu.CompilerParams(vmem_limit_bytes=VMEM_LIMIT),
        cost_estimate=takes(4),
        name="add_pieces",
    )(keep, received)


def quarter_kernel(index_ref, *refs):
    pieces, outs = refs[: len(refs) - GROUP], refs[len(refs) - GROUP :]
    rows = outs[0].shape[0]
    for k, out in enumerate(outs):
        here = pl.ds(pl.multiple_of(index_ref[k] * rows, 16), rows)
        out[...] = sum_low(pieces[0][here], [piece[here] for piece in pieces[1:]])


def sum_quarters(pieces, group):
    rows, width = pieces[0].shape
    return pl.pallas_call(
        quarter_kernel,
        out_shape=[jax.ShapeDtypeStruct((rows // GROUP, width), LOW)] * GROUP,
        in_specs=[smem()] + vmem(len(pieces)),
        out_specs=vmem(GROUP),
        compiler_params=pltpu.CompilerParams(vmem_limit_bytes=VMEM_LIMIT),
        cost_estimate=takes(3),
        name="sum_quarters",
    )(jnp.stack([group ^ k for k in range(GROUP)]).astype(jnp.int32), *pieces)


def collect_kernel(index_ref, *refs):
    pieces, out = refs[:-1], refs[-1]
    for k in range(len(pieces)):
        out[index_ref[k]] = pieces[k][...]


def collect(pieces, spots):
    rows = pieces[0]
    return pl.pallas_call(
        collect_kernel,
        out_shape=jax.ShapeDtypeStruct((GROUP,) + rows.shape, rows.dtype),
        in_specs=[smem()] + vmem(GROUP),
        out_specs=vmem(1)[0],
        cost_estimate=takes(2),
        name="collect",
    )(jnp.stack(spots).astype(jnp.int32), *pieces)


def row_sums(values):
    ones = jnp.ones((8, values.shape[1]), WIDE)
    sums = lax.dot_general(
        ones, values, NT, precision=lax.Precision.HIGHEST, preferred_element_type=WIDE
    )
    return sums[:1]


def finish_kernel(index_ref, mine_ref, theirs_ref, weight_ref, gain_ref, *outs):
    core = index_ref[0]
    half = mine_ref.shape[1]
    shard = outs[0].shape[0]
    wholes, (router_ref, third_ref, second_ref) = outs[:-3], outs[-3:]
    for number, out in enumerate(wholes):
        here = slice(number * shard, (number + 1) * shard)
        out[:, pl.ds(pl.multiple_of(core * half, 128), half)] = mine_ref[here].astype(WIDE)
        out[:, pl.ds(pl.multiple_of((1 - core) * half, 128), half)] = theirs_ref[here].astype(WIDE)
    second_ref[...] = row_sums(weight_ref[...].astype(WIDE) * wholes[1][...]) / gain_ref[
        ...
    ].astype(WIDE)
    here = slice(len(wholes) * shard, None)
    spread = mine_ref[here].astype(WIDE) + theirs_ref[here].astype(WIDE)
    experts = router_ref.shape[0]
    router_ref[...] = spread[:experts, :shard]
    third_ref[...] = spread[experts : experts + 1, :shard]


def finish_weights(mine, theirs, weight, gain, core, experts):
    shard, width = weight.shape
    shapes = [(shard, width)] * 5 + [(experts, shard)] + [(1, shard)] * 2
    results = pl.pallas_call(
        finish_kernel,
        out_shape=[jax.ShapeDtypeStruct(shape, WIDE) for shape in shapes],
        in_specs=[smem()] + vmem(4),
        out_specs=vmem(len(shapes)),
        compiler_params=pltpu.CompilerParams(vmem_limit_bytes=VMEM_LIMIT),
        cost_estimate=takes(3),
        name="finish_weights",
    )(core.reshape(1).astype(jnp.int32), mine, theirs, weight, gain[None])
    return list(results[:5]) + [results[5].T] + [one[0] for one in results[6:]]


def qkv_grads_kernel(index_ref, rows_ref, grad_ref, table_ref, keep, send):
    f_index, core = index_ref[0], index_ref[1]
    size = keep.shape[0]
    extra = 16
    rows = keep.shape[1] - extra
    product = dot_tn(rows_ref[...], grad_ref[...])
    buckets = table_ref.shape[0] // size
    for block in range(size):
        spot = block ^ f_index
        top = product[2 * block * rows : (2 * block + 1) * rows].astype(LOW)
        bottom = product[(2 * block + 1) * rows : (2 * block + 2) * rows].astype(LOW)
        keep[spot, :rows] = jnp.where(core == 0, top, bottom)
        send[spot, :rows] = jnp.where(core == 0, bottom, top)
        keep[spot, rows:] = jnp.zeros((extra, keep.shape[2]), LOW)
        send[spot, rows:] = jnp.zeros((extra, keep.shape[2]), LOW)
        keep[spot, rows : rows + buckets, : table_ref.shape[1]] = table_ref[
            block * buckets : (block + 1) * buckets
        ].astype(LOW)


def qkv_finish_kernel(index_ref, mine_ref, theirs_ref, *refs):
    core = index_ref[0]
    weights, gain_ref, outs, bias_ref, gain_out = refs[:3], refs[3], refs[4:7], refs[7], refs[8]
    own = mine_ref.shape[2] // 3
    rows = outs[0].shape[0] // 2
    product = None
    for which in range(3):
        for source, side in ((mine_ref, core), (theirs_ref, 1 - core)):
            whole = jnp.concatenate(
                [
                    source[g, :rows, which * own : (which + 1) * own].astype(WIDE)
                    for g in range(GROUP)
                ],
                axis=1,
            )
            outs[which][pl.ds(pl.multiple_of(side * rows, 8), rows)] = whole
        one = weights[which][...].astype(WIDE) * outs[which][...]
        product = one if product is None else product + one
    gain_out[...] = row_sums(product) / gain_ref[...].astype(WIDE)
    buckets = bias_ref.shape[0]
    for g in range(GROUP):
        table = mine_ref[g, rows:, :128].astype(WIDE) + theirs_ref[g, rows:, :128].astype(WIDE)
        bias_ref[:, g * OWN_HEADS : (g + 1) * OWN_HEADS] = table[:buckets, :OWN_HEADS]


def qkv_weight_grads(rows, grads, table, f_index, core, size):
    width = rows.shape[1]
    half_shard = width // size // 2
    extra = 16
    shape = jax.ShapeDtypeStruct((size, half_shard + extra, grads.shape[1]), LOW)
    return pl.pallas_call(
        qkv_grads_kernel,
        out_shape=[shape, shape],
        in_specs=[smem()] + vmem(3),
        out_specs=vmem(2),
        compiler_params=pltpu.CompilerParams(vmem_limit_bytes=VMEM_LIMIT),
        cost_estimate=takes(3.1),
        name="qkv_grads",
    )(jnp.stack([f_index, core]).astype(jnp.int32), rows, grads, table)


def finish_qkv(mine, theirs, weights, gain, core, bias_shape):
    shard, width = weights[0].shape
    shapes = [(shard, width)] * 3 + [bias_shape, (1, shard)]
    results = pl.pallas_call(
        qkv_finish_kernel,
        out_shape=[jax.ShapeDtypeStruct(shape, WIDE) for shape in shapes],
        in_specs=[smem()] + vmem(6),
        out_specs=vmem(len(shapes)),
        compiler_params=pltpu.CompilerParams(vmem_limit_bytes=VMEM_LIMIT),
        cost_estimate=takes(2.6),
        name="qkv_finish",
    )(core.reshape(1).astype(jnp.int32), mine, theirs, *weights, gain[None])
    return list(results[:4]) + [results[4][0]]


def head_lanes(head, width):
    first = head // 2 * 128
    return first, min(first + 128, width)


def only_head(rows, head):
    if rows.shape[-1] == HEAD_DIM:
        return rows
    lane = lax.broadcasted_iota(jnp.int32, rows.shape, rows.ndim - 1)
    return jnp.where(lane // HEAD_DIM == head % 2, rows, jnp.zeros_like(rows))


def bias_block(kind_ref, tile_ref, head, step, first_block, width):
    rows = []
    for half in range(2):
        columns = []
        for pair in range(width // 128):
            left = kind_ref[2 * step + half, first_block + 2 * pair]
            right = kind_ref[2 * step + half, first_block + 2 * pair + 1]
            columns.append(tile_ref[0, head, left] + tile_ref[1, head, right])
        rows.append(jnp.concatenate(columns, axis=1))
    return jnp.concatenate(rows, axis=0)


def chunk_scores(query_head, key_ref, lanes, first, width, head, step, kind_ref, tile_ref):
    keys = key_ref[pl.ds(first, width), lanes[0] : lanes[1]]
    scores = lax.dot_general(query_head, keys, NT, preferred_element_type=WIDE)
    if kind_ref is not None:
        scores = scores + bias_block(kind_ref, tile_ref, head, step, first // HEAD_DIM, width)
    return scores


def forward_body(step, kind_ref, tile_ref, query_ref, key_ref, value_ref, out_ref, log_ref):
    width = query_ref.shape[-1]
    key_count = key_ref.shape[0]
    chunk = math.gcd(key_count, 1024)
    rows = query_ref.shape[0]
    lane = lax.broadcasted_iota(jnp.int32, (rows, 128), 1)
    logs = jnp.zeros((rows, 128), WIDE)
    tile_out = None
    for head in range(width // HEAD_DIM):
        lanes = head_lanes(head, width)
        query_head = only_head(query_ref[:, lanes[0] : lanes[1]], head) * jnp.asarray(0.125, LOW)

        def one_chunk(index, running):
            top, total, mixed = running
            first = index * chunk
            scores = chunk_scores(
                query_head, key_ref, lanes, first, chunk, head, step, kind_ref, tile_ref
            )
            new_top = jnp.maximum(top, jnp.max(scores, axis=1, keepdims=True))
            weights = jnp.exp(scores - new_top)
            shrink = jnp.exp(top - new_top)
            total = total * shrink + jnp.sum(weights, axis=1, keepdims=True)
            values = value_ref[pl.ds(first, chunk), lanes[0] : lanes[1]]
            mixed = mixed * shrink + jnp.dot(
                weights.astype(LOW), values, preferred_element_type=WIDE
            )
            return new_top, total, mixed

        running = (
            jnp.full((rows, 1), -1e29, WIDE),
            jnp.zeros((rows, 1), WIDE),
            jnp.zeros((rows, lanes[1] - lanes[0]), WIDE),
        )
        if key_count == chunk:
            running = one_chunk(0, running)
        else:
            running = lax.fori_loop(0, key_count // chunk, one_chunk, running)
        top, total, mixed = running
        mixed = only_head(mixed / total, head)
        logs = jnp.where(lane == head, top + jnp.log(total), logs)
        tile_out = mixed if head % 2 == 0 else tile_out + mixed
        if head % 2 == 1 or head == width // HEAD_DIM - 1:
            out_ref[:, lanes[0] : lanes[1]] = tile_out.astype(LOW)
    log_ref[...] = logs


def backward_body(
    step, kind_ref, tile_ref, query_ref, up_ref, log_ref, key_ref, value_ref, dq_ref, dk_ref, dv_ref, sums
):
    width = query_ref.shape[-1]
    key_count = key_ref.shape[0]
    chunk = math.gcd(key_count, 1024)
    rows = query_ref.shape[0]
    tile_out = None
    for head in range(width // HEAD_DIM):
        lanes = head_lanes(head, width)
        query_head = only_head(query_ref[:, lanes[0] : lanes[1]], head) * jnp.asarray(0.125, LOW)
        up_head = only_head(up_ref[:, lanes[0] : lanes[1]], head)
        log_head = log_ref[:, head : head + 1]

        def probs_of(first):
            scores = chunk_scores(
                query_head, key_ref, lanes, first, chunk, head, step, kind_ref, tile_ref
            )
            probs = jnp.exp(scores - log_head)
            values = value_ref[pl.ds(first, chunk), lanes[0] : lanes[1]]
            prob_grad = lax.dot_general(up_head, values, NT, preferred_element_type=WIDE)
            return probs, prob_grad

        def finish(first, probs, prob_grad, delta):
            score_grad = probs * (prob_grad - delta)
            if sums is not None:
                for half in range(2):
                    for pair in range(chunk // 128):
                        block = first // HEAD_DIM + 2 * pair
                        left = kind_ref[2 * step + half, block]
                        right = kind_ref[2 * step + half, block + 1]
                        piece = score_grad[
                            half * HEAD_DIM : (half + 1) * HEAD_DIM, pair * 128 : (pair + 1) * 128
                        ]
                        sums[0, head, left] += piece
                        sums[1, head, right] += piece
            score_low = score_grad.astype(LOW)
            here = pl.ds(first, chunk)
            dk_ref[here, lanes[0] : lanes[1]] += lax.dot_general(
                score_low, query_head, TN, preferred_element_type=WIDE
            )
            dv_ref[here, lanes[0] : lanes[1]] += lax.dot_general(
                probs.astype(LOW), up_head, TN, preferred_element_type=WIDE
            )
            keys = key_ref[here, lanes[0] : lanes[1]]
            return jnp.dot(score_low, keys, preferred_element_type=WIDE)

        if key_count == chunk:
            probs, prob_grad = probs_of(0)
            delta = jnp.sum(probs * prob_grad, axis=1, keepdims=True)
            query_grad = finish(0, probs, prob_grad, delta)
        else:

            def add_delta(index, delta):
                probs, prob_grad = probs_of(index * chunk)
                return delta + jnp.sum(probs * prob_grad, axis=1, keepdims=True)

            delta = lax.fori_loop(0, key_count // chunk, add_delta, jnp.zeros((rows, 1), WIDE))

            def add_grad(index, total):
                probs, prob_grad = probs_of(index * chunk)
                return total + finish(index * chunk, probs, prob_grad, delta)

            query_grad = lax.fori_loop(
                0, key_count // chunk, add_grad, jnp.zeros((rows, lanes[1] - lanes[0]), WIDE)
            )
        query_grad = only_head(query_grad * 0.125, head)
        tile_out = query_grad if head % 2 == 0 else tile_out + query_grad
        if head % 2 == 1 or head == width // HEAD_DIM - 1:
            dq_ref[:, lanes[0] : lanes[1]] = tile_out.astype(LOW)


def load_keys(own_ref, rest_ref, key_ref, value_ref):
    own, width = own_ref.shape[0], key_ref.shape[1]
    key_ref[:own] = own_ref[:, :width]
    key_ref[own:] = rest_ref[:, :width]
    value_ref[:own] = own_ref[:, width:]
    value_ref[own:] = rest_ref[:, width:]


def self_forward_kernel(kind_ref, tile_ref, query_ref, own_ref, rest_ref, *refs):
    outs, log_ref, out_ref, key_ref, value_ref = refs[:-4], refs[-4], refs[-3], refs[-2], refs[-1]

    @pl.when(pl.program_id(0) == 0)
    def start():
        load_keys(own_ref, rest_ref, key_ref, value_ref)

    forward_body(
        pl.program_id(0), kind_ref, tile_ref, query_ref, key_ref, value_ref, out_ref, log_ref
    )
    for k in range(len(outs)):

        @pl.when(pl.program_id(0) == k)
        def store():
            outs[k][...] = out_ref[...]


def self_backward_kernel(first, last, kind_ref, tile_ref, query_ref, up_ref, log_ref, own_ref, rest_ref, *refs):
    if first > 0:
        dk_start, dv_start, sums_start = refs[:3]
        refs = refs[3:]
    dq_ref, outs, (key_ref, value_ref, dk_ref, dv_ref) = refs[0], refs[1:4], refs[4:]
    sums = outs[2]

    @pl.when(pl.program_id(0) == 0)
    def start():
        load_keys(own_ref, rest_ref, key_ref, value_ref)
        if first > 0:
            dk_ref[...] = dk_start[...]
            dv_ref[...] = dv_start[...]
            sums[...] = sums_start[...]
        else:
            dk_ref[...] = jnp.zeros_like(dk_ref)
            dv_ref[...] = jnp.zeros_like(dv_ref)
            sums[...] = jnp.zeros_like(sums)

    backward_body(
        first + pl.program_id(0),
        kind_ref,
        tile_ref,
        query_ref,
        up_ref,
        log_ref,
        key_ref,
        value_ref,
        dq_ref,
        dk_ref,
        dv_ref,
        sums,
    )

    @pl.when(pl.program_id(0) == pl.num_programs(0) - 1)
    def end():
        if last:
            own, width = own_ref.shape[0], key_ref.shape[1]
            for out, here in ((outs[0], slice(0, own)), (outs[1], slice(own, None))):
                out[:, :width] = dk_ref[here].astype(LOW)
                out[:, width:] = dv_ref[here].astype(LOW)
        else:
            outs[0][...] = dk_ref[...]
            outs[1][...] = dv_ref[...]


def cross_forward_kernel(query_ref, key_ref, value_ref, out_ref, log_ref):
    forward_body(0, None, None, query_ref, key_ref, value_ref, out_ref, log_ref)


def cross_backward_kernel(
    query_ref, up_ref, log_ref, key_ref, value_ref, dq_ref, dk_out, dv_out, dk_ref, dv_ref
):
    dk_ref[...] = jnp.zeros_like(dk_ref)
    dv_ref[...] = jnp.zeros_like(dv_ref)
    backward_body(
        0, None, None, query_ref, up_ref, log_ref, key_ref, value_ref, dq_ref, dk_ref, dv_ref, None
    )
    dk_out[...] = dk_ref[...].astype(LOW)
    dv_out[...] = dv_ref[...].astype(LOW)


def whole_block(shape):
    return pl.BlockSpec(shape, lambda *index: (0,) * len(shape))


def row_block(rows, width):
    return pl.BlockSpec((rows, width), lambda i, *rest: (i, 0))


def lane_block(rows):
    return pl.BlockSpec((rows, 128), lambda i, *rest: (0, i))


def self_forward(kinds, tiles, queries, own, rest):
    count, width = queries.shape
    rows = 2 * HEAD_DIM
    keys = own.shape[0] + rest.shape[0]
    return pl.pallas_call(
        self_forward_kernel,
        grid_spec=pltpu.PrefetchScalarGridSpec(
            num_scalar_prefetch=1,
            grid=(count // rows,),
            in_specs=[
                whole_block(tiles.shape),
                row_block(rows, width),
                whole_block(own.shape),
                whole_block(rest.shape),
            ],
            out_specs=[whole_block((rows, width))] * (count // rows) + [row_block(rows, 128)],
            scratch_shapes=[
                pltpu.VMEM((rows, width), LOW),
                pltpu.VMEM((keys, width), LOW),
                pltpu.VMEM((keys, width), LOW),
            ],
        ),
        out_shape=[jax.ShapeDtypeStruct((rows, width), LOW)] * (count // rows)
        + [jax.ShapeDtypeStruct((count, 128), WIDE)],
        compiler_params=pltpu.CompilerParams(vmem_limit_bytes=VMEM_LIMIT),
        cost_estimate=takes(8.5),
        name="self_forward",
    )(kinds, tiles, queries, own, rest)


def self_backward(first, last, kinds, tiles, queries, up_rows, logs, own, rest, start=()):
    count, width = queries.shape
    rows = 2 * HEAD_DIM
    done = last == count // rows
    keys = own.shape[0] + rest.shape[0]
    if done:
        shapes = [jax.ShapeDtypeStruct(own.shape, LOW), jax.ShapeDtypeStruct(rest.shape, LOW)]
    else:
        shapes = [jax.ShapeDtypeStruct((keys, width), WIDE)] * 2
    shapes.append(jax.ShapeDtypeStruct(tiles.shape, WIDE))

    def rows_at(lanes):
        return pl.BlockSpec((rows, lanes), lambda i, *refs: (first + i, 0))

    return pl.pallas_call(
        partial(self_backward_kernel, first, done),
        grid_spec=pltpu.PrefetchScalarGridSpec(
            num_scalar_prefetch=1,
            grid=(last - first,),
            in_specs=[
                whole_block(tiles.shape),
                rows_at(width),
                rows_at(width),
                rows_at(128),
                whole_block(own.shape),
                whole_block(rest.shape),
            ]
            + [whole_block(array.shape) for array in start],
            out_specs=[row_block(rows, width)] + [whole_block(shape.shape) for shape in shapes],
            scratch_shapes=[pltpu.VMEM((keys, width), LOW)] * 2
            + [pltpu.VMEM((keys, width), WIDE)] * 2,
        ),
        out_shape=[jax.ShapeDtypeStruct(((last - first) * rows, width), LOW)] + shapes,
        compiler_params=pltpu.CompilerParams(vmem_limit_bytes=VMEM_LIMIT),
        cost_estimate=takes(9),
        name="self_backward",
    )(kinds, tiles, queries, up_rows, logs, own, rest, *start)


def cross_forward(queries, keys, values):
    count, width = queries.shape
    key_count = keys.shape[0]
    return pl.pallas_call(
        cross_forward_kernel,
        grid=(width // 128,),
        in_specs=[lane_block(count), lane_block(key_count), lane_block(key_count)],
        out_specs=[lane_block(count), lane_block(count)],
        out_shape=[
            jax.ShapeDtypeStruct((count, width), LOW),
            jax.ShapeDtypeStruct((count, width), WIDE),
        ],
        compiler_params=pltpu.CompilerParams(vmem_limit_bytes=VMEM_LIMIT),
        cost_estimate=takes(6.6),
        name="cross_forward",
    )(queries, keys, values)


def cross_backward(queries, up_rows, logs, keys, values):
    count, width = queries.shape
    key_count = keys.shape[0]
    return pl.pallas_call(
        cross_backward_kernel,
        grid=(width // 128,),
        in_specs=[lane_block(count)] * 3 + [lane_block(key_count)] * 2,
        out_specs=[lane_block(count), lane_block(key_count), lane_block(key_count)],
        scratch_shapes=[pltpu.VMEM((key_count, 128), WIDE), pltpu.VMEM((key_count, 128), WIDE)],
        out_shape=[
            jax.ShapeDtypeStruct((count, width), LOW),
            jax.ShapeDtypeStruct(keys.shape, LOW),
            jax.ShapeDtypeStruct(keys.shape, LOW),
        ],
        compiler_params=pltpu.CompilerParams(vmem_limit_bytes=VMEM_LIMIT),
        cost_estimate=takes(8.2),
        name="cross_backward",
    )(queries, up_rows, logs, keys, values)


def tiles_kernel(bound_ref, bias_ref, out_ref):
    shape = (HEAD_DIM, 2 * HEAD_DIM)
    lane = lax.broadcasted_iota(jnp.int32, shape, 1)
    row = lax.broadcasted_iota(jnp.int32, shape, 0)
    left = lane < HEAD_DIM
    offset = row - lane % HEAD_DIM
    for head in range(OWN_HEADS):
        far = jnp.full(shape, bias_ref[BUCKETS - 1, head], WIDE)
        tiles = [jnp.full(shape, MASKED, WIDE)]
        for apart in range(3):
            tile = tiles[0]
            for bucket in range(BUCKETS):
                reached = offset + apart * HEAD_DIM >= bound_ref[bucket]
                tile = jnp.where(reached, bias_ref[bucket, head], tile)
            tiles.append(tile)
        for kind, tile in enumerate(tiles + [far]):
            out_ref[0, head, kind] = jnp.where(left, tile, 0.0)
            out_ref[1, head, kind] = jnp.where(left, 0.0, tile)


def bias_tiles(lower_bounds, own_bias):
    shape = (2, OWN_HEADS, 5, HEAD_DIM, 2 * HEAD_DIM)
    return pl.pallas_call(
        tiles_kernel,
        out_shape=jax.ShapeDtypeStruct(shape, WIDE),
        in_specs=[pl.BlockSpec(memory_space=pltpu.SMEM)] * 2,
        out_specs=pl.BlockSpec(memory_space=pltpu.VMEM),
        cost_estimate=takes(2.7),
        name="bias_tiles",
    )(lower_bounds, own_bias)


def bucket_sums(sums, lower_bounds):
    tiles = sums[0, :, 1:, :, :HEAD_DIM] + sums[1, :, 1:, :, HEAD_DIM:]
    shape = (3, HEAD_DIM, HEAD_DIM, BUCKETS)
    distance = (
        lax.broadcasted_iota(jnp.int32, shape, 0) * HEAD_DIM
        + lax.broadcasted_iota(jnp.int32, shape, 1)
        - lax.broadcasted_iota(jnp.int32, shape, 2)
    )
    upper_bounds = jnp.concatenate([lower_bounds[1:], jnp.full((1,), 1 << 30, jnp.int32)])
    hot = ((distance >= lower_bounds) & (distance < upper_bounds)).astype(LOW)
    near = tiles[:, :3].reshape(OWN_HEADS, -1)
    high = near.astype(LOW)
    low = (near - high.astype(WIDE)).astype(LOW)
    both = jnp.dot(
        jnp.concatenate([high, low]), hot.reshape(-1, BUCKETS), preferred_element_type=WIDE
    )
    table = both[:OWN_HEADS] + both[OWN_HEADS:]
    far = jnp.sum(tiles[:, 3], axis=(1, 2))
    return table + jnp.where(jnp.arange(BUCKETS) == BUCKETS - 1, far[:, None], 0.0)


def rms_of(values):
    return lax.rsqrt(jnp.mean(values * values, axis=-1, keepdims=True) + EPSILON)


def norm_grad(values, inv_rms, gain, upstream):
    scaled = gain * upstream
    inner = jnp.mean(scaled * values, axis=-1, keepdims=True)
    return inv_rms * scaled - values * (inv_rms * inv_rms * inv_rms * inner)


def dot(left, right):
    return jnp.dot(left, right, preferred_element_type=WIDE)


def dot_nt(left, right):
    return lax.dot_general(left, right, NT, preferred_element_type=WIDE)


def dot_tn(left, right):
    return lax.dot_general(left, right, TN, preferred_element_type=WIDE)


def on_device(
    tokens,
    cotangent,
    encoder,
    expert_ids,
    block_order,
    bucket_table,
    first_gain,
    second_gain,
    third_gain,
    position_bias,
    query_weight,
    key_weight,
    value_weight,
    out_weight,
    cross_query,
    cross_key,
    cross_value,
    cross_out,
    router_weight,
    expert_in,
    expert_out,
):
    ctx_size = lax.axis_size("ctx")
    fsdp_size = lax.axis_size("fsdp")
    rests = rest_count()
    f_index = lax.axis_index("fsdp")
    ctx_index = lax.axis_index("ctx")
    core = ctx_index % 2
    group = (ctx_index // 2) % GROUP
    rest = ctx_index // (2 * GROUP)
    seq_count, span, width = tokens.shape
    shard = width // fsdp_size
    own_width = width // GROUP
    half_shard = shard // 2
    half_width = width // 2
    experts = expert_in.shape[0] * ctx_size
    capacity = (5 * seq_count * span + 4 * experts - 1) // (4 * experts)
    hidden_low = tokens.reshape(span, width)
    upstream = cotangent.reshape(span, width).astype(WIDE)

    small = jnp.concatenate(
        [
            first_gain[None],
            second_gain[None],
            third_gain[None],
            router_weight.T,
            jnp.pad(position_bias.reshape(1, -1), ((0, 0), (0, shard - position_bias.size))),
        ]
    )
    small = jnp.pad(small, ((0, -small.shape[0] % 16), (0, 0)))
    extra = small.shape[0]
    qkv_payload, early, late = pack_weights(
        small,
        (
            query_weight,
            key_weight,
            value_weight,
            out_weight,
            cross_key,
            cross_value,
            cross_query,
            cross_out,
        ),
        3,
        group,
        core,
    )
    first_hops = tie(*gather_group(hidden_low), *gather_fsdp(qkv_payload), early, late)
    own_rows = jnp.concatenate(first_hops[:GROUP])
    own_qkv, small_full = place_qkv(first_hops[GROUP : GROUP + fsdp_size], extra, f_index)
    early, late = first_hops[GROUP + fsdp_size :]
    early_x, early_y = swap_fsdp(early, 1), swap_fsdp(early, 2)
    expert_ids = after(expert_ids, qkv_payload)
    block_order, bucket_table, _ = tie(block_order, bucket_table, qkv_payload)

    gain_one = small_full[:, 0].reshape(width).astype(WIDE)
    gain_two = small_full[:, 1].reshape(width).astype(WIDE)
    gain_three = small_full[:, 2].reshape(width).astype(WIDE)
    router_full = small_full[:, 3 : 3 + experts].transpose(1, 0, 2).reshape(experts, width)
    bias_full = small_full[:, 3 + experts, : position_bias.size].reshape(BUCKETS, HEADS)

    slots = jnp.arange(GROUP, dtype=jnp.int32)
    key_devices = (
        ((rest - jnp.arange(rests, dtype=jnp.int32)) % rests)[:, None, None] * (2 * GROUP)
        + (group ^ slots)[None, None, :] * 2
        + (core ^ jnp.arange(2, dtype=jnp.int32))[None, :, None]
    ).reshape(-1)
    key_blocks = (key_devices[:, None] * 2 + jnp.arange(2, dtype=jnp.int32)[None]).reshape(-1)
    block_count = block_order.shape[0]
    hits = key_blocks[:, None] == jnp.arange(block_count, dtype=jnp.int32)[None]
    key_places = jnp.sum(jnp.where(hits, block_order[None], 0), axis=1)
    query_places = key_places[: 2 * GROUP]
    kinds = jnp.clip(query_places[:, None] - key_places[None], -1, 3) + 1
    lower_bounds = jnp.sum(
        (bucket_table[:, None] < jnp.arange(BUCKETS, dtype=jnp.int32)[None]).astype(jnp.int32),
        axis=0,
    )
    own_bias = lax.dynamic_slice_in_dim(
        bias_full.astype(WIDE), group * OWN_HEADS, OWN_HEADS, 1
    )
    tiles = bias_tiles(lower_bounds, own_bias)

    routes = expert_ids.reshape(-1)
    chosen = routes[:, None] == jnp.arange(experts, dtype=jnp.int32)[None]
    order = jnp.arange(span)
    lower = (order[:, None] > order[None]).astype(LOW)
    earlier = dot(lower, chosen.astype(LOW))
    slot_rank = jnp.sum(jnp.where(chosen, earlier, 0.0), axis=1).astype(jnp.int32)
    block_rows = -(-2 * capacity // 8) * 8
    slot_rows = rests * GROUP * block_rows
    target = (
        (((routes // (2 * GROUP) - rest) % rests) * GROUP + (((routes // 2) % GROUP) ^ group))
        * block_rows
        + core * capacity
        + slot_rank
    )
    code = jnp.where(slot_rank < capacity, (routes % 2) * slot_rows + target, -1)
    own_code = jnp.broadcast_to(code.astype(WIDE)[:, None], (span, 128))
    other_code = swap_core(own_code)
    codes = jnp.concatenate([own_code[:, :1], other_code[:, :1]]).astype(jnp.int32)
    placing = (
        codes == core * slot_rows + jnp.arange(slot_rows, dtype=jnp.int32)[None]
    ).astype(LOW)
    chosen = chosen.astype(WIDE)

    wide_rows = own_rows.astype(WIDE)
    normed_own = (wide_rows * rms_of(wide_rows) * gain_one).astype(LOW)
    own_count = GROUP * span
    queries = dot(normed_own, own_qkv[:, :own_width]).astype(LOW)
    pairs_own = dot(normed_own, own_qkv[:, own_width:]).astype(LOW)
    pairs_rest = swap_core(pairs_own)
    encoder_pieces = gather_group(after(encoder, early).reshape(-1, width))
    pairs_own, pairs_rest, early_x, early_y, *encoder_pieces = tie(
        pairs_own, pairs_rest, early_x, early_y, *encoder_pieces
    )
    early_xy = swap_fsdp(early_x, 2)
    late_x, late_y = swap_fsdp(late, 1), swap_fsdp(late, 2)
    if rests > 1:
        near = jnp.concatenate([pairs_own, pairs_rest])
        pairs_rest = jnp.concatenate(
            [pairs_rest] + [shift_rest(near, r) for r in range(1, rests)]
        )
    *attended_own, self_logs = self_forward(kinds, tiles, queries, pairs_own, pairs_rest)
    *attended_own, early_xy, late_x = tie(*attended_own, early_xy, late_x)
    attended = [attended_own[0]] + [swap_group(attended_own[k], k) for k in range(1, GROUP)]
    late_xy = swap_fsdp(late_x, 2)
    early_mine = stack_pieces((early, early_x, early_y, early_xy), 1, f_index, group)
    early_theirs = swap_core(early_mine)
    encoder_own = jnp.concatenate(encoder_pieces)
    encoder_other = swap_core(encoder_own)
    *attended, early_theirs, encoder_other, late_y = tie(
        *attended, early_theirs, encoder_other, late_y
    )
    out_full, cross_k_full, cross_v_full = weave_halves(early_mine, early_theirs, core)
    encoder_all = jnp.concatenate([encoder_own, encoder_other])
    if rests > 1:
        encoder_all = jnp.concatenate(
            [encoder_all] + [shift_rest(encoder_all, r) for r in range(1, rests)]
        )
    attended = jnp.concatenate(attended, axis=1)
    hidden = hidden_low.astype(WIDE)
    first_sum = hidden + dot(attended, out_full)
    inv_two = rms_of(first_sum)
    normed_two = (first_sum * inv_two * gain_two).astype(LOW)
    normed_two, late_xy = tie(normed_two, late_xy)
    late_mine = stack_pieces((late, late_x, late_y, late_xy), 0, f_index, group)
    late_theirs = swap_core(late_mine)

    cross_keys = dot(after(encoder_all, late_mine), cross_k_full).astype(LOW)
    cross_values = dot(encoder_all, cross_v_full).astype(LOW)
    cross_q_full, cross_o_full = weave_halves(late_mine, late_theirs, core)
    cross_rows = dot(normed_two, cross_q_full).astype(LOW)
    cross_mixed, cross_logs = cross_forward(cross_rows, cross_keys, cross_values)
    second_sum = first_sum + dot(cross_mixed, cross_o_full)
    inv_three = rms_of(second_sum)
    normed_three = (second_sum * inv_three * gain_three).astype(LOW)

    logits = dot_nt(normed_three, router_full)
    router_probs = jax.nn.softmax(logits, axis=-1)
    gate_value = jnp.sum(router_probs * chosen, axis=-1, keepdims=True)
    scaled_up = (gate_value * upstream).astype(LOW)

    sides = jnp.concatenate([normed_three, scaled_up], axis=1)
    sides = jnp.concatenate([sides, swap_core(sides)])
    sent = dot_tn(placing, sides).astype(LOW).reshape(rests, GROUP * block_rows, 2 * width)
    near = jnp.concatenate(
        [sent[0]] + [shift_rest(sent[r], r) for r in range(1, rests)]
    ).reshape(rests, GROUP, block_rows, 2 * width)
    arrived = jnp.concatenate(
        [near[:, 0]] + [swap_group(near[:, k], k) for k in range(1, GROUP)], axis=1
    ).reshape(slot_rows, 2 * width)
    arrivals = tie(*gather_fsdp(arrived))
    answers, middle = run_experts(arrivals, expert_in[0], expert_out[0])
    answers = tie(answers[0], *[swap_fsdp(answers[k], k) for k in range(1, fsdp_size)])
    answers = sum_home(answers, rests)
    near = [answers[0]] + [swap_group(answers[k], k) for k in range(1, GROUP)]
    near = jnp.concatenate(
        [piece.reshape(rests, block_rows, 2 * width) for piece in near], axis=1
    )
    home = jnp.concatenate([near[0]] + [shift_rest(near[r], -r) for r in range(1, rests)])
    both = dot(placing, home).astype(LOW)
    both = both[:span].astype(WIDE) + swap_core(both[span:]).astype(WIDE)
    moe_rows, dispatch_grad = both[:, :width], both[:, width:]
    grad_expert_in, grad_expert_out = expert_grads(arrivals, middle)
    grad_expert_in, grad_expert_out = grad_expert_in[None], grad_expert_out[None]

    mixed_out = (second_sum + gate_value * moe_rows).astype(LOW).reshape(tokens.shape)
    gate_grad = jnp.sum(upstream * moe_rows, axis=-1, keepdims=True)
    logit_low = (gate_grad * gate_value * (chosen - router_probs)).astype(LOW)
    three_grad = dispatch_grad + dot(logit_low, router_full)
    second_grad = upstream + norm_grad(second_sum, inv_three, gain_three, three_grad)
    gain_three_part = jnp.sum(three_grad * second_sum * inv_three, axis=0, keepdims=True)
    router_part = dot_tn(logit_low, normed_three)
    spread = jnp.concatenate([router_part, gain_three_part])
    spread = jnp.pad(spread, ((0, -spread.shape[0] % 16), (0, 0)))

    branch_two = second_grad.astype(LOW)
    cross_up = dot_nt(branch_two, cross_o_full).astype(LOW)
    cross_q_low, cross_k_part, cross_v_part = cross_backward(
        cross_rows, cross_up, cross_logs, cross_keys, cross_values
    )
    two_grad = dot_nt(cross_q_low, cross_q_full)
    first_grad = second_grad + norm_grad(first_sum, inv_two, gain_two, two_grad)

    branch_one = first_grad.astype(LOW)
    self_up = dot_nt(branch_one, out_full).astype(LOW)
    branch_one, self_up = tie(branch_one, self_up)
    up_pieces = [self_up[:, :own_width]] + [
        swap_group(self_up[:, k * own_width : (k + 1) * own_width], k) for k in range(1, GROUP)
    ]
    extra_rows = -(-spread.shape[0] // 64) * 64
    keep, send = weight_grads(
        (False, False, False, False, True),
        (
            (cross_mixed, branch_two),
            (normed_two, cross_q_low),
            (encoder_all, cross_k_part),
            (encoder_all, cross_v_part),
            (attended, branch_one),
        ),
        spread,
        extra_rows,
        f_index,
        core,
        group,
        fsdp_size,
    )
    *up_pieces, received = tie(*up_pieces, swap_core(send))
    up_own = jnp.concatenate(up_pieces)
    parts = [add_low(keep[k], received[k]) for k in range(fsdp_size)]
    up_own, *parts[1:] = tie(up_own, *parts[1:])
    parts = [parts[0]] + [swap_fsdp(parts[k], k) for k in range(1, fsdp_size)]
    query_low, pair_own, pair_rest, bias_parts = self_backward(
        0, own_count // span, kinds, tiles, queries, up_own, self_logs, pairs_own, pairs_rest
    )
    query_low, pair_own, pair_rest, bias_parts, parts[1], parts[2] = tie(
        query_low, pair_own, pair_rest, bias_parts, parts[1], parts[2]
    )
    if rests > 1:
        near = jnp.concatenate([pair_own, pair_rest[:own_count]]).astype(WIDE)
        for r in range(1, rests):
            first = (2 * r - 1) * own_count
            piece = pair_rest[first : first + 2 * own_count]
            near = near + shift_rest(piece, -r).astype(WIDE)
        pair_own, pair_rest = near[:own_count].astype(LOW), near[own_count:].astype(LOW)
    pair_low = add_low(pair_own, swap_core(pair_rest))
    qkv_low = jnp.concatenate([query_low, pair_low], axis=1)
    one_part = dot_nt(qkv_low, own_qkv).astype(LOW)
    one_parts = one_part.reshape(GROUP, span, width)
    one_parts = [one_parts[0]] + [swap_group(one_parts[k], k) for k in range(1, GROUP)]

    table = jnp.pad(bucket_sums(bias_parts, lower_bounds).T, ((0, 0), (0, 128 - OWN_HEADS)))
    qkv_keep, qkv_send = qkv_weight_grads(normed_own, qkv_low, table, f_index, core, fsdp_size)
    qkv_send, parts[3:] = tie(swap_core(qkv_send), parts[3:])
    qkv_parts = add_pieces(qkv_keep, qkv_send)
    qkv_parts = [qkv_parts[0]] + [swap_fsdp(qkv_parts[k], k) for k in range(1, fsdp_size)]
    qkv_shard = sum_rest(sum_low(qkv_parts[0], qkv_parts[1:])).astype(LOW)
    *one_parts, parts[0] = tie(*one_parts, parts[0])
    one_grad = sum(one.astype(WIDE) for one in one_parts)
    tokens_grad = first_grad + norm_grad(hidden, rms_of(hidden), gain_one, one_grad)
    tokens_grad = tokens_grad.reshape(tokens.shape)
    quarters = sum_quarters(parts, group)
    quarters = [quarters[0]] + [swap_group(quarters[k], k) for k in range(1, GROUP)]
    dense_shard = sum_rest(sum_low(quarters[0], quarters[1:])).astype(LOW)
    spots = [group ^ k for k in range(GROUP)]
    qkv_mine = collect(gather_group(qkv_shard), spots)
    query_total, key_total, value_total, bias_total, grad_gain_one = finish_qkv(
        qkv_mine,
        swap_core(qkv_mine),
        (query_weight, key_weight, value_weight),
        first_gain,
        core,
        position_bias.shape,
    )
    dense_mine = collect(gather_group(dense_shard), spots).reshape(-1, half_width)
    (
        cross_o_total,
        cross_q_total,
        cross_k_total,
        cross_v_total,
        out_total,
        grad_router,
        grad_gain_three,
        grad_gain_two,
    ) = finish_weights(dense_mine, swap_core(dense_mine), cross_query, second_gain, core, experts)

    return (
        mixed_out,
        tokens_grad,
        grad_gain_one,
        grad_gain_two,
        grad_gain_three,
        bias_total,
        query_total,
        key_total,
        value_total,
        out_total,
        cross_q_total,
        cross_k_total,
        cross_v_total,
        cross_o_total,
        grad_router,
        grad_expert_in,
        grad_expert_out,
    )


def solution(mesh):
    rows = P("fsdp", "ctx", None)
    vector = P("fsdp")
    matrix = P("fsdp", None)
    expert_specs = (P("ctx", None, "fsdp"), P("ctx", "fsdp", None))
    return jax.shard_map(
        on_device,
        mesh=mesh,
        in_specs=(rows,) * 4 + (P(),) * 2 + (vector,) * 3 + (matrix,) * 10 + expert_specs,
        out_specs=(rows,) * 2 + (vector,) * 3 + (matrix,) * 10 + expert_specs,
        check_vma=False,
    )
```

```python
import math
from functools import partial

import jax
import jax.numpy as jnp
from jax import lax
from jax.experimental import pallas as pl
from jax.experimental.pallas import tpu as pltpu
from jax.sharding import PartitionSpec as P

HEADS = 12
HEAD_DIM = 64
BUCKETS = 32
GROUP = 4
OWN_HEADS = HEADS // GROUP
EPSILON = 1e-06
MASKED = -1e30
LOW = jnp.bfloat16
WIDE = jnp.float32
VMEM_LIMIT = 56 * 1024 * 1024
NT = (((1,), (1,)), ((), ()))
TN = (((0,), (0,)), ((), ()))


def swap_fsdp(rows, k):
    size = lax.axis_size("fsdp")
    return lax.ppermute(rows, "fsdp", [(i, i ^ k) for i in range(size)])


def swap_core(rows):
    size = lax.axis_size("ctx")
    return lax.ppermute(rows, "ctx", [(i, i ^ 1) for i in range(size)])


def swap_group(rows, k):
    size = lax.axis_size("ctx")
    return lax.ppermute(rows, "ctx", [(i, i ^ (2 * k)) for i in range(size)])


def shift_rest(rows, r):
    size = lax.axis_size("ctx")
    step = 2 * GROUP * r
    return lax.ppermute(rows, "ctx", [(i, (i + step) % size) for i in range(size)])


def rest_count():
    return lax.axis_size("ctx") // (2 * GROUP)


def block_at(blocks, index):
    return lax.dynamic_index_in_dim(blocks, index, 0, keepdims=False)


def in_order(parts, index):
    parts = list(parts)
    bit = 1
    while bit < len(parts):
        flag = (index & bit) != 0
        parts = [jnp.where(flag, parts[i ^ bit], parts[i]) for i in range(len(parts))]
        bit *= 2
    return parts


def tie(*values):
    return lax.optimization_barrier(values)


def after(value, *earlier):
    return tie(value, *earlier)[0]


def gather_group(rows):
    return [rows] + [swap_group(rows, k) for k in range(1, GROUP)]


def gather_fsdp(rows):
    return [rows] + [swap_fsdp(rows, k) for k in range(1, lax.axis_size("fsdp"))]


def sum_rest(values):
    size = lax.axis_size("ctx")
    if rest_count() == 1:
        return values
    near = 2 * GROUP
    groups = [list(range(i, size, near)) for i in range(near)]
    return lax.psum(values, "ctx", axis_index_groups=groups)


def takes(us):
    return pl.CostEstimate(flops=int(us * 1e9), bytes_accessed=int(us * 3.5e6), transcendentals=0)


def vmem(count):
    return [pl.BlockSpec(memory_space=pltpu.VMEM)] * count


def smem():
    return pl.BlockSpec(memory_space=pltpu.SMEM)


def pack_kernel(index_ref, small_ref, *refs):
    group, core = index_ref[0], index_ref[1]
    ins, (qkv_ref, early_ref, late_ref) = refs[:-3], refs[-3:]
    rows = early_ref.shape[1]
    own = qkv_ref.shape[1] // 3
    shard = 2 * rows
    for choice in range(GROUP):

        @pl.when(group == choice)
        def take():
            for which in range(3):
                qkv_ref[:shard, which * own : (which + 1) * own] = ins[which][
                    :, choice * own : (choice + 1) * own
                ]

    qkv_ref[shard:] = jnp.zeros((small_ref.shape[0], 3 * own), LOW)
    qkv_ref[shard:, :shard] = small_ref[...]
    here = pl.ds(pl.multiple_of(core * rows, 16), rows)
    early = early_ref.shape[0]
    for i in range(early):
        early_ref[i] = ins[3 + i][here]
    for i in range(late_ref.shape[0]):
        late_ref[i] = ins[3 + early + i][here]


def pack_weights(small, weights, early, group, core):
    shard, width = weights[0].shape
    own = width // GROUP
    late = len(weights) - 3 - early
    return pl.pallas_call(
        pack_kernel,
        out_shape=[
            jax.ShapeDtypeStruct((shard + small.shape[0], 3 * own), LOW),
            jax.ShapeDtypeStruct((early, shard // 2, width), LOW),
            jax.ShapeDtypeStruct((late, shard // 2, width), LOW),
        ],
        in_specs=[smem()] + vmem(1 + len(weights)),
        out_specs=vmem(3),
        compiler_params=pltpu.CompilerParams(vmem_limit_bytes=VMEM_LIMIT),
        cost_estimate=takes(3),
        name="pack_weights",
    )(jnp.stack([group, core]).astype(jnp.int32), small, *weights)


def place_qkv_kernel(index_ref, *refs):
    pieces, (out, small) = refs[:-2], refs[-2:]
    rows = out.shape[1]
    for k in range(len(pieces)):
        out[index_ref[k]] = pieces[k][:rows]
        small[index_ref[k]] = pieces[k][rows:, :rows]


def place_qkv(pieces, extra, f_index):
    count = len(pieces)
    rows, width = pieces[0].shape
    rows = rows - extra
    whole, small = pl.pallas_call(
        place_qkv_kernel,
        out_shape=[
            jax.ShapeDtypeStruct((count, rows, width), LOW),
            jax.ShapeDtypeStruct((count, extra, rows), LOW),
        ],
        in_specs=[smem()] + vmem(count),
        out_specs=vmem(2),
        compiler_params=pltpu.CompilerParams(vmem_limit_bytes=VMEM_LIMIT),
        cost_estimate=takes(2.3),
        name="place_qkv",
    )(jnp.stack([f_index ^ k for k in range(count)]).astype(jnp.int32), *pieces)
    return whole.reshape(count * rows, width), small


def stack_kernel(turned, index_ref, *refs):
    count = len(refs) - 1
    out = refs[-1]
    for item in range(out.shape[0]):
        for k in range(count):
            spot = index_ref[count + k] if item < turned else index_ref[k]
            out[item, spot] = refs[k][item]


def stack_pieces(pieces, turned, f_index, g_index):
    count = len(pieces)
    spots = [f_index ^ k for k in range(count)]
    indices = jnp.stack(spots + [g_index ^ spot for spot in spots]).astype(jnp.int32)
    number, rows, width = pieces[0].shape
    return pl.pallas_call(
        partial(stack_kernel, turned),
        out_shape=jax.ShapeDtypeStruct((number, count, rows, width), LOW),
        in_specs=[smem()] + vmem(count),
        out_specs=vmem(1)[0],
        compiler_params=pltpu.CompilerParams(vmem_limit_bytes=VMEM_LIMIT),
        cost_estimate=takes(2.7),
        name="stack_pieces",
    )(indices, *pieces)


def weave_kernel(index_ref, mine_ref, theirs_ref, *outs):
    core = index_ref[0]
    for item, out in enumerate(outs):
        for block in range(out.shape[0]):
            out[block, core] = mine_ref[item, block]
            out[block, 1 - core] = theirs_ref[item, block]


def weave_halves(mine, theirs, core):
    number, count, rows, width = mine.shape
    whole = pl.pallas_call(
        weave_kernel,
        out_shape=[jax.ShapeDtypeStruct((count, 2, rows, width), LOW)] * number,
        in_specs=[smem()] + vmem(2),
        out_specs=vmem(number),
        compiler_params=pltpu.CompilerParams(vmem_limit_bytes=VMEM_LIMIT),
        cost_estimate=takes(4),
        name="weave_halves",
    )(core.reshape(1).astype(jnp.int32), mine, theirs)
    return [one.reshape(count * 2 * rows, width) for one in whole]


def expert_kernel(*refs):
    count = (len(refs) - 3) // 2
    pieces, in_ref, out_ref = refs[:count], refs[count], refs[count + 1]
    answers, middle = refs[count + 2 : 2 * count + 2], refs[-1]
    rows, width = pieces[0].shape[0], pieces[0].shape[1] // 2
    hidden = in_ref.shape[1]
    scale = math.sqrt(2 / math.pi)
    for k in range(count):
        inner = dot(pieces[k][:, :width], in_ref[...])
        square = inner * inner
        bent = jnp.tanh(scale * (inner + 0.044715 * (inner * square)))
        activated = (0.5 * inner * (1.0 + bent)).astype(LOW)
        slope = 0.5 * (1.0 + bent) + 0.5 * inner * (1.0 - bent * bent) * (
            scale * (1.0 + 3 * 0.044715 * square)
        )
        inner_low = (dot_nt(pieces[k][:, width:], out_ref[...]) * slope).astype(LOW)
        answers[k][:, :width] = dot(activated, out_ref[...]).astype(LOW)
        answers[k][:, width:] = dot_nt(inner_low, in_ref[...]).astype(LOW)
        here = slice(k * rows, (k + 1) * rows)
        middle[here, :hidden] = activated
        middle[here, hidden:] = inner_low


def run_experts(pieces, expert_in, expert_out):
    count = len(pieces)
    width, hidden = expert_in.shape
    rows = pieces[0].shape[0]
    results = pl.pallas_call(
        expert_kernel,
        out_shape=[jax.ShapeDtypeStruct((rows, 2 * width), LOW)] * count
        + [jax.ShapeDtypeStruct((count * rows, 2 * hidden), LOW)],
        in_specs=vmem(count + 2),
        out_specs=vmem(count + 1),
        compiler_params=pltpu.CompilerParams(vmem_limit_bytes=VMEM_LIMIT),
        cost_estimate=takes(8.2),
        name="experts",
    )(*pieces, expert_in, expert_out)
    return list(results[:count]), results[count]


def expert_grads_kernel(*refs):
    pieces, (middle, in_ref, out_ref) = refs[:-3], refs[-3:]
    width, hidden = in_ref.shape
    rows = jnp.concatenate([piece[...] for piece in pieces])
    in_ref[...] = dot_tn(rows[:, :width], middle[:, hidden:])
    out_ref[...] = dot_tn(middle[:, :hidden], rows[:, width:])


def expert_grads(pieces, middle):
    width = pieces[0].shape[1] // 2
    hidden = middle.shape[1] // 2
    return pl.pallas_call(
        expert_grads_kernel,
        out_shape=[
            jax.ShapeDtypeStruct((width, hidden), WIDE),
            jax.ShapeDtypeStruct((hidden, width), WIDE),
        ],
        in_specs=vmem(1 + len(pieces)),
        out_specs=vmem(2),
        compiler_params=pltpu.CompilerParams(vmem_limit_bytes=VMEM_LIMIT),
        cost_estimate=takes(5.7),
        name="expert_grads",
    )(*pieces, middle)


def home_kernel(rests, *refs):
    pieces, outs = refs[: len(refs) - GROUP], refs[len(refs) - GROUP :]
    block = outs[0].shape[0] // rests
    for k, out in enumerate(outs):
        for r in range(rests):
            here = slice((r * GROUP + k) * block, (r * GROUP + k + 1) * block)
            out[r * block : (r + 1) * block] = sum_low(
                pieces[0][here], [piece[here] for piece in pieces[1:]]
            )


def sum_home(pieces, rests):
    rows, width = pieces[0].shape
    return pl.pallas_call(
        partial(home_kernel, rests),
        out_shape=[jax.ShapeDtypeStruct((rows // GROUP, width), LOW)] * GROUP,
        in_specs=vmem(len(pieces)),
        out_specs=vmem(GROUP),
        compiler_params=pltpu.CompilerParams(vmem_limit_bytes=VMEM_LIMIT),
        cost_estimate=takes(2.4),
        name="sum_home",
    )(*pieces)


def grads_kernel(turns, extra_rows, index_ref, *refs):
    f_index, core, turn = index_ref[0], index_ref[1], index_ref[2]
    ins, spread_ref, keep, send = refs[: 2 * len(turns)], refs[-3], refs[-2], refs[-1]
    size, _, half = keep.shape
    shard = ins[0].shape[1] // size
    for item, turned in enumerate(turns):
        rows_ref, grad_ref = ins[2 * item], ins[2 * item + 1]
        for out, side in ((keep, core), (send, 1 - core)):
            grad = grad_ref[:, pl.ds(pl.multiple_of(side * half, 128), half)]
            product = dot_tn(rows_ref[...], grad).astype(LOW)
            for block in range(size):
                spot = block ^ f_index ^ (turn if turned else 0)
                out[spot, item * shard : (item + 1) * shard] = product[
                    block * shard : (block + 1) * shard
                ]
    first = len(turns) * shard
    for block in range(size):
        spot = block ^ f_index
        piece = spread_ref[:, block * shard : (block + 1) * shard].astype(LOW)
        keep[spot, first:] = jnp.zeros((extra_rows, half), LOW)
        send[spot, first:] = jnp.zeros((extra_rows, half), LOW)
        keep[spot, first : first + spread_ref.shape[0], :shard] = piece


def weight_grads(turns, pairs, spread, extra_rows, f_index, core, turn, size):
    width = pairs[0][0].shape[1]
    rows = len(turns) * (width // size) + extra_rows
    shape = jax.ShapeDtypeStruct((size, rows, width // 2), LOW)
    flat = [array for pair in pairs for array in pair] + [spread]
    return pl.pallas_call(
        partial(grads_kernel, turns, extra_rows),
        out_shape=[shape, shape],
        in_specs=[smem()] + vmem(len(flat)),
        out_specs=vmem(2),
        compiler_params=pltpu.CompilerParams(vmem_limit_bytes=VMEM_LIMIT),
        cost_estimate=takes(7.5),
        name="weight_grads",
    )(jnp.stack([f_index, core, turn]).astype(jnp.int32), *flat)


def add_low(left, right):
    return (left.astype(WIDE) + right.astype(WIDE)).astype(LOW)


def sum_low(first, others):
    total = first.astype(WIDE)
    for other in others:
        total = total + other.astype(WIDE)
    return total.astype(LOW)


def quarter_kernel(index_ref, *refs):
    outs = refs[len(refs) - GROUP :]
    count = (len(refs) - GROUP) // 2
    rows = outs[0].shape[0] // 2
    for k, out in enumerate(outs):
        here = pl.ds(pl.multiple_of(index_ref[k] * rows, 16), rows)
        for half in range(2):
            pieces = refs[half * count : (half + 1) * count]
            out[half * rows : (half + 1) * rows] = sum_low(
                pieces[0][here], [piece[here] for piece in pieces[1:]]
            )


def sum_quarters(top, bottom, group):
    rows, width = top[0].shape
    pieces = list(top) + list(bottom)
    return pl.pallas_call(
        quarter_kernel,
        out_shape=[jax.ShapeDtypeStruct((2 * rows // GROUP, width), LOW)] * GROUP,
        in_specs=[smem()] + vmem(len(pieces)),
        out_specs=vmem(GROUP),
        compiler_params=pltpu.CompilerParams(vmem_limit_bytes=VMEM_LIMIT),
        cost_estimate=takes(3),
        name="sum_quarters",
    )(jnp.stack([group ^ k for k in range(GROUP)]).astype(jnp.int32), *pieces)


def collect_kernel(index_ref, *refs):
    pieces, out = refs[:-1], refs[-1]
    rows = out.shape[2]
    for k in range(len(pieces)):
        for half in range(out.shape[0]):
            out[half, index_ref[k]] = pieces[k][half * rows : (half + 1) * rows]


def collect(pieces, spots, halves):
    rows, width = pieces[0].shape
    return pl.pallas_call(
        collect_kernel,
        out_shape=jax.ShapeDtypeStruct((halves, GROUP, rows // halves, width), LOW),
        in_specs=[smem()] + vmem(GROUP),
        out_specs=vmem(1)[0],
        cost_estimate=takes(2),
        name="collect",
    )(jnp.stack(spots).astype(jnp.int32), *pieces)


def row_sums(values):
    ones = jnp.ones((8, values.shape[1]), WIDE)
    sums = lax.dot_general(
        ones, values, NT, precision=lax.Precision.HIGHEST, preferred_element_type=WIDE
    )
    return sums[:1]


def finish_kernel(index_ref, mine_ref, theirs_ref, weight_ref, gain_ref, *outs):
    core = index_ref[0]
    half = mine_ref.shape[1]
    shard = outs[0].shape[0]
    wholes, (router_ref, third_ref, second_ref) = outs[:-3], outs[-3:]
    for number, out in enumerate(wholes):
        here = slice(number * shard, (number + 1) * shard)
        out[:, pl.ds(pl.multiple_of(core * half, 128), half)] = mine_ref[here].astype(WIDE)
        out[:, pl.ds(pl.multiple_of((1 - core) * half, 128), half)] = theirs_ref[here].astype(WIDE)
    second_ref[...] = row_sums(weight_ref[...].astype(WIDE) * wholes[1][...]) / gain_ref[
        ...
    ].astype(WIDE)
    here = slice(len(wholes) * shard, None)
    spread = mine_ref[here].astype(WIDE) + theirs_ref[here].astype(WIDE)
    experts = router_ref.shape[0]
    router_ref[...] = spread[:experts, :shard]
    third_ref[...] = spread[experts : experts + 1, :shard]


def finish_weights(mine, theirs, weight, gain, core, experts):
    shard, width = weight.shape
    shapes = [(shard, width)] * 5 + [(experts, shard)] + [(1, shard)] * 2
    results = pl.pallas_call(
        finish_kernel,
        out_shape=[jax.ShapeDtypeStruct(shape, WIDE) for shape in shapes],
        in_specs=[smem()] + vmem(4),
        out_specs=vmem(len(shapes)),
        compiler_params=pltpu.CompilerParams(vmem_limit_bytes=VMEM_LIMIT),
        cost_estimate=takes(3),
        name="finish_weights",
    )(core.reshape(1).astype(jnp.int32), mine, theirs, weight, gain[None])
    return list(results[:5]) + [results[5].T] + [one[0] for one in results[6:]]


def key_grads_kernel(index_ref, rows_ref, query_ref, own_ref, rest_ref, weight_ref, *outs):
    f_index, core = index_ref[0], index_ref[1]
    ones, (keep, send) = outs[:-2], outs[-2:]
    grads = jnp.concatenate([query_ref[...], add_low(own_ref[...], rest_ref[...])], axis=1)
    count = grads.shape[0] // len(ones)
    for k, one in enumerate(ones):
        one[...] = dot_nt(grads[k * count : (k + 1) * count], weight_ref[...]).astype(LOW)
    size, rows, _ = keep.shape
    product = dot_tn(rows_ref[...], grads)
    for block in range(size):
        spot = block ^ f_index
        top = product[2 * block * rows : (2 * block + 1) * rows].astype(LOW)
        bottom = product[(2 * block + 1) * rows : (2 * block + 2) * rows].astype(LOW)
        keep[spot] = jnp.where(core == 0, top, bottom)
        send[spot] = jnp.where(core == 0, bottom, top)


def key_grads(rows, query, own, rest, weight, f_index, core, size):
    count, width = rows.shape
    shape = jax.ShapeDtypeStruct((size, width // size // 2, weight.shape[1]), LOW)
    results = pl.pallas_call(
        key_grads_kernel,
        out_shape=[jax.ShapeDtypeStruct((count // GROUP, width), LOW)] * GROUP + [shape] * 2,
        in_specs=[smem()] + vmem(5),
        out_specs=vmem(GROUP + 2),
        compiler_params=pltpu.CompilerParams(vmem_limit_bytes=VMEM_LIMIT),
        cost_estimate=takes(0.1),
        name="key_grads",
    )(jnp.stack([f_index, core]).astype(jnp.int32), rows, query, own, rest, weight)
    return list(results[:GROUP]), results[GROUP], results[GROUP + 1]


def add_qkv_kernel(index_ref, keep_ref, received_ref, table_ref, *outs):
    rows = keep_ref.shape[1]
    buckets = table_ref.shape[0] // len(outs)
    for k, out in enumerate(outs):
        out[:rows] = add_low(keep_ref[k], received_ref[k])
        here = pl.ds(pl.multiple_of((index_ref[0] ^ k) * buckets, 8), buckets)
        table = table_ref[here]
        spare = out.shape[1] - table.shape[1]
        table = jnp.concatenate([table, jnp.zeros((buckets, spare), WIDE)], axis=1)
        below = jnp.zeros((out.shape[0] - rows - buckets, out.shape[1]), WIDE)
        out[rows:] = jnp.concatenate([table, below]).astype(LOW)


def add_qkv(keep, received, table, f_index):
    size, rows, width = keep.shape
    return list(
        pl.pallas_call(
            add_qkv_kernel,
            out_shape=[jax.ShapeDtypeStruct((rows + 16, width), LOW)] * size,
            in_specs=[smem()] + vmem(3),
            out_specs=vmem(size),
            compiler_params=pltpu.CompilerParams(vmem_limit_bytes=VMEM_LIMIT),
            cost_estimate=takes(2),
            name="add_qkv",
        )(f_index.reshape(1).astype(jnp.int32), keep, received, table)
    )


def qkv_finish_kernel(index_ref, mine_ref, theirs_ref, *refs):
    core = index_ref[0]
    weights, gain_ref, outs, bias_ref, gain_out = refs[:3], refs[3], refs[4:7], refs[7], refs[8]
    own = mine_ref.shape[2] // 3
    rows = outs[0].shape[0] // 2
    product = None
    for which in range(3):
        for source, side in ((mine_ref, core), (theirs_ref, 1 - core)):
            whole = jnp.concatenate(
                [
                    source[g, :rows, which * own : (which + 1) * own].astype(WIDE)
                    for g in range(GROUP)
                ],
                axis=1,
            )
            outs[which][pl.ds(pl.multiple_of(side * rows, 8), rows)] = whole
        one = weights[which][...].astype(WIDE) * outs[which][...]
        product = one if product is None else product + one
    gain_out[...] = row_sums(product) / gain_ref[...].astype(WIDE)
    buckets = bias_ref.shape[0]
    for g in range(GROUP):
        table = mine_ref[g, rows:, :128].astype(WIDE) + theirs_ref[g, rows:, :128].astype(WIDE)
        bias_ref[:, g * OWN_HEADS : (g + 1) * OWN_HEADS] = table[:buckets, :OWN_HEADS]


def finish_qkv(mine, theirs, weights, gain, core, bias_shape):
    shard, width = weights[0].shape
    shapes = [(shard, width)] * 3 + [bias_shape, (1, shard)]
    results = pl.pallas_call(
        qkv_finish_kernel,
        out_shape=[jax.ShapeDtypeStruct(shape, WIDE) for shape in shapes],
        in_specs=[smem()] + vmem(6),
        out_specs=vmem(len(shapes)),
        compiler_params=pltpu.CompilerParams(vmem_limit_bytes=VMEM_LIMIT),
        cost_estimate=takes(2.6),
        name="qkv_finish",
    )(core.reshape(1).astype(jnp.int32), mine, theirs, *weights, gain[None])
    return list(results[:4]) + [results[4][0]]


def head_lanes(head, width):
    first = head // 2 * 128
    return first, min(first + 128, width)


def only_head(rows, head):
    if rows.shape[-1] == HEAD_DIM:
        return rows
    lane = lax.broadcasted_iota(jnp.int32, rows.shape, rows.ndim - 1)
    return jnp.where(lane // HEAD_DIM == head % 2, rows, jnp.zeros_like(rows))


def bias_block(kind_ref, tile_ref, head, step, first_block, width):
    rows = []
    for half in range(2):
        columns = []
        for pair in range(width // 128):
            left = kind_ref[2 * step + half, first_block + 2 * pair]
            right = kind_ref[2 * step + half, first_block + 2 * pair + 1]
            columns.append(tile_ref[0, head, left] + tile_ref[1, head, right])
        rows.append(jnp.concatenate(columns, axis=1))
    return jnp.concatenate(rows, axis=0)


def chunk_scores(query_head, key_ref, lanes, first, width, head, step, kind_ref, tile_ref):
    keys = key_ref[pl.ds(first, width), lanes[0] : lanes[1]]
    scores = lax.dot_general(query_head, keys, NT, preferred_element_type=WIDE)
    if kind_ref is not None:
        scores = scores + bias_block(kind_ref, tile_ref, head, step, first // HEAD_DIM, width)
    return scores


def forward_body(step, kind_ref, tile_ref, query_ref, key_ref, value_ref, out_ref, log_ref):
    width = query_ref.shape[-1]
    key_count = key_ref.shape[0]
    chunk = math.gcd(key_count, 1024)
    rows = query_ref.shape[0]
    lane = lax.broadcasted_iota(jnp.int32, (rows, 128), 1)
    logs = jnp.zeros((rows, 128), WIDE)
    tile_out = None
    for head in range(width // HEAD_DIM):
        lanes = head_lanes(head, width)
        query_head = only_head(query_ref[:, lanes[0] : lanes[1]], head) * jnp.asarray(0.125, LOW)

        def one_chunk(index, running):
            top, total, mixed = running
            first = index * chunk
            scores = chunk_scores(
                query_head, key_ref, lanes, first, chunk, head, step, kind_ref, tile_ref
            )
            new_top = jnp.maximum(top, jnp.max(scores, axis=1, keepdims=True))
            weights = jnp.exp(scores - new_top)
            shrink = jnp.exp(top - new_top)
            total = total * shrink + jnp.sum(weights, axis=1, keepdims=True)
            values = value_ref[pl.ds(first, chunk), lanes[0] : lanes[1]]
            mixed = mixed * shrink + jnp.dot(
                weights.astype(LOW), values, preferred_element_type=WIDE
            )
            return new_top, total, mixed

        running = (
            jnp.full((rows, 1), -1e29, WIDE),
            jnp.zeros((rows, 1), WIDE),
            jnp.zeros((rows, lanes[1] - lanes[0]), WIDE),
        )
        if key_count == chunk:
            running = one_chunk(0, running)
        else:
            running = lax.fori_loop(0, key_count // chunk, one_chunk, running)
        top, total, mixed = running
        mixed = only_head(mixed / total, head)
        logs = jnp.where(lane == head, top + jnp.log(total), logs)
        tile_out = mixed if head % 2 == 0 else tile_out + mixed
        if head % 2 == 1 or head == width // HEAD_DIM - 1:
            out_ref[:, lanes[0] : lanes[1]] = tile_out.astype(LOW)
    log_ref[...] = logs


def backward_body(
    step, kind_ref, tile_ref, query_ref, up_ref, log_ref, key_ref, value_ref, dq_ref, dk_ref, dv_ref, sums
):
    width = query_ref.shape[-1]
    key_count = key_ref.shape[0]
    chunk = math.gcd(key_count, 1024)
    rows = query_ref.shape[0]
    tile_out = None
    for head in range(width // HEAD_DIM):
        lanes = head_lanes(head, width)
        query_head = only_head(query_ref[:, lanes[0] : lanes[1]], head) * jnp.asarray(0.125, LOW)
        up_head = only_head(up_ref[:, lanes[0] : lanes[1]], head)
        log_head = log_ref[:, head : head + 1]

        def probs_of(first):
            scores = chunk_scores(
                query_head, key_ref, lanes, first, chunk, head, step, kind_ref, tile_ref
            )
            probs = jnp.exp(scores - log_head)
            values = value_ref[pl.ds(first, chunk), lanes[0] : lanes[1]]
            prob_grad = lax.dot_general(up_head, values, NT, preferred_element_type=WIDE)
            return probs, prob_grad

        def finish(first, probs, prob_grad, delta):
            score_grad = probs * (prob_grad - delta)
            if sums is not None:
                for half in range(2):
                    for pair in range(chunk // 128):
                        block = first // HEAD_DIM + 2 * pair
                        left = kind_ref[2 * step + half, block]
                        right = kind_ref[2 * step + half, block + 1]
                        piece = score_grad[
                            half * HEAD_DIM : (half + 1) * HEAD_DIM, pair * 128 : (pair + 1) * 128
                        ]
                        sums[0, head, left] += piece
                        sums[1, head, right] += piece
            score_low = score_grad.astype(LOW)
            here = pl.ds(first, chunk)
            dk_ref[here, lanes[0] : lanes[1]] += lax.dot_general(
                score_low, query_head, TN, preferred_element_type=WIDE
            )
            dv_ref[here, lanes[0] : lanes[1]] += lax.dot_general(
                probs.astype(LOW), up_head, TN, preferred_element_type=WIDE
            )
            keys = key_ref[here, lanes[0] : lanes[1]]
            return jnp.dot(score_low, keys, preferred_element_type=WIDE)

        if key_count == chunk:
            probs, prob_grad = probs_of(0)
            delta = jnp.sum(probs * prob_grad, axis=1, keepdims=True)
            query_grad = finish(0, probs, prob_grad, delta)
        else:

            def add_delta(index, delta):
                probs, prob_grad = probs_of(index * chunk)
                return delta + jnp.sum(probs * prob_grad, axis=1, keepdims=True)

            delta = lax.fori_loop(0, key_count // chunk, add_delta, jnp.zeros((rows, 1), WIDE))

            def add_grad(index, total):
                probs, prob_grad = probs_of(index * chunk)
                return total + finish(index * chunk, probs, prob_grad, delta)

            query_grad = lax.fori_loop(
                0, key_count // chunk, add_grad, jnp.zeros((rows, lanes[1] - lanes[0]), WIDE)
            )
        query_grad = only_head(query_grad * 0.125, head)
        tile_out = query_grad if head % 2 == 0 else tile_out + query_grad
        if head % 2 == 1 or head == width // HEAD_DIM - 1:
            dq_ref[:, lanes[0] : lanes[1]] = tile_out.astype(LOW)


def load_keys(own_ref, rest_ref, key_ref, value_ref):
    own, width = own_ref.shape[0], key_ref.shape[1]
    key_ref[:own] = own_ref[:, :width]
    key_ref[own:] = rest_ref[:, :width]
    value_ref[:own] = own_ref[:, width:]
    value_ref[own:] = rest_ref[:, width:]


def self_forward_kernel(kind_ref, tile_ref, query_ref, own_ref, rest_ref, *refs):
    outs, log_ref, out_ref, key_ref, value_ref = refs[:-4], refs[-4], refs[-3], refs[-2], refs[-1]

    @pl.when(pl.program_id(0) == 0)
    def start():
        load_keys(own_ref, rest_ref, key_ref, value_ref)

    forward_body(
        pl.program_id(0), kind_ref, tile_ref, query_ref, key_ref, value_ref, out_ref, log_ref
    )
    for k in range(len(outs)):

        @pl.when(pl.program_id(0) == k)
        def store():
            outs[k][...] = out_ref[...]


def self_backward_kernel(first, last, kind_ref, tile_ref, query_ref, up_ref, log_ref, own_ref, rest_ref, *refs):
    if first > 0:
        dk_start, dv_start, sums_start = refs[:3]
        refs = refs[3:]
    dq_ref, outs, (key_ref, value_ref, dk_ref, dv_ref) = refs[0], refs[1:4], refs[4:]
    sums = outs[2]

    @pl.when(pl.program_id(0) == 0)
    def start():
        load_keys(own_ref, rest_ref, key_ref, value_ref)
        if first > 0:
            dk_ref[...] = dk_start[...]
            dv_ref[...] = dv_start[...]
            sums[...] = sums_start[...]
        else:
            dk_ref[...] = jnp.zeros_like(dk_ref)
            dv_ref[...] = jnp.zeros_like(dv_ref)
            sums[...] = jnp.zeros_like(sums)

    backward_body(
        first + pl.program_id(0),
        kind_ref,
        tile_ref,
        query_ref,
        up_ref,
        log_ref,
        key_ref,
        value_ref,
        dq_ref,
        dk_ref,
        dv_ref,
        sums,
    )

    @pl.when(pl.program_id(0) == pl.num_programs(0) - 1)
    def end():
        if last:
            own, width = own_ref.shape[0], key_ref.shape[1]
            for out, here in ((outs[0], slice(0, own)), (outs[1], slice(own, None))):
                out[:, :width] = dk_ref[here].astype(LOW)
                out[:, width:] = dv_ref[here].astype(LOW)
        else:
            outs[0][...] = dk_ref[...]
            outs[1][...] = dv_ref[...]


def cross_forward_kernel(query_ref, key_ref, value_ref, out_ref, log_ref):
    forward_body(0, None, None, query_ref, key_ref, value_ref, out_ref, log_ref)


def cross_backward_kernel(
    query_ref, up_ref, log_ref, key_ref, value_ref, dq_ref, dk_out, dv_out, dk_ref, dv_ref
):
    dk_ref[...] = jnp.zeros_like(dk_ref)
    dv_ref[...] = jnp.zeros_like(dv_ref)
    backward_body(
        0, None, None, query_ref, up_ref, log_ref, key_ref, value_ref, dq_ref, dk_ref, dv_ref, None
    )
    dk_out[...] = dk_ref[...].astype(LOW)
    dv_out[...] = dv_ref[...].astype(LOW)


def whole_block(shape):
    return pl.BlockSpec(shape, lambda *index: (0,) * len(shape))


def row_block(rows, width):
    return pl.BlockSpec((rows, width), lambda i, *rest: (i, 0))


def lane_block(rows):
    return pl.BlockSpec((rows, 128), lambda i, *rest: (0, i))


def self_forward(kinds, tiles, queries, own, rest):
    count, width = queries.shape
    rows = 2 * HEAD_DIM
    keys = own.shape[0] + rest.shape[0]
    return pl.pallas_call(
        self_forward_kernel,
        grid_spec=pltpu.PrefetchScalarGridSpec(
            num_scalar_prefetch=1,
            grid=(count // rows,),
            in_specs=[
                whole_block(tiles.shape),
                row_block(rows, width),
                whole_block(own.shape),
                whole_block(rest.shape),
            ],
            out_specs=[whole_block((rows, width))] * (count // rows) + [row_block(rows, 128)],
            scratch_shapes=[
                pltpu.VMEM((rows, width), LOW),
                pltpu.VMEM((keys, width), LOW),
                pltpu.VMEM((keys, width), LOW),
            ],
        ),
        out_shape=[jax.ShapeDtypeStruct((rows, width), LOW)] * (count // rows)
        + [jax.ShapeDtypeStruct((count, 128), WIDE)],
        compiler_params=pltpu.CompilerParams(vmem_limit_bytes=VMEM_LIMIT),
        cost_estimate=takes(8.5),
        name="self_forward",
    )(kinds, tiles, queries, own, rest)


def self_backward(first, last, kinds, tiles, queries, up_rows, logs, own, rest, start=()):
    count, width = queries.shape
    rows = 2 * HEAD_DIM
    done = last == count // rows
    keys = own.shape[0] + rest.shape[0]
    if done:
        shapes = [jax.ShapeDtypeStruct(own.shape, LOW), jax.ShapeDtypeStruct(rest.shape, LOW)]
    else:
        shapes = [jax.ShapeDtypeStruct((keys, width), WIDE)] * 2
    shapes.append(jax.ShapeDtypeStruct(tiles.shape, WIDE))

    def rows_at(lanes):
        return pl.BlockSpec((rows, lanes), lambda i, *refs: (first + i, 0))

    return pl.pallas_call(
        partial(self_backward_kernel, first, done),
        grid_spec=pltpu.PrefetchScalarGridSpec(
            num_scalar_prefetch=1,
            grid=(last - first,),
            in_specs=[
                whole_block(tiles.shape),
                rows_at(width),
                rows_at(width),
                rows_at(128),
                whole_block(own.shape),
                whole_block(rest.shape),
            ]
            + [whole_block(array.shape) for array in start],
            out_specs=[row_block(rows, width)] + [whole_block(shape.shape) for shape in shapes],
            scratch_shapes=[pltpu.VMEM((keys, width), LOW)] * 2
            + [pltpu.VMEM((keys, width), WIDE)] * 2,
        ),
        out_shape=[jax.ShapeDtypeStruct(((last - first) * rows, width), LOW)] + shapes,
        compiler_params=pltpu.CompilerParams(vmem_limit_bytes=VMEM_LIMIT),
        cost_estimate=takes(9),
        name="self_backward",
    )(kinds, tiles, queries, up_rows, logs, own, rest, *start)


def cross_forward(queries, keys, values):
    count, width = queries.shape
    key_count = keys.shape[0]
    return pl.pallas_call(
        cross_forward_kernel,
        grid=(width // 128,),
        in_specs=[lane_block(count), lane_block(key_count), lane_block(key_count)],
        out_specs=[lane_block(count), lane_block(count)],
        out_shape=[
            jax.ShapeDtypeStruct((count, width), LOW),
            jax.ShapeDtypeStruct((count, width), WIDE),
        ],
        compiler_params=pltpu.CompilerParams(vmem_limit_bytes=VMEM_LIMIT),
        cost_estimate=takes(6.6),
        name="cross_forward",
    )(queries, keys, values)


def cross_backward(queries, up_rows, logs, keys, values):
    count, width = queries.shape
    key_count = keys.shape[0]
    return pl.pallas_call(
        cross_backward_kernel,
        grid=(width // 128,),
        in_specs=[lane_block(count)] * 3 + [lane_block(key_count)] * 2,
        out_specs=[lane_block(count), lane_block(key_count), lane_block(key_count)],
        scratch_shapes=[pltpu.VMEM((key_count, 128), WIDE), pltpu.VMEM((key_count, 128), WIDE)],
        out_shape=[
            jax.ShapeDtypeStruct((count, width), LOW),
            jax.ShapeDtypeStruct(keys.shape, LOW),
            jax.ShapeDtypeStruct(keys.shape, LOW),
        ],
        compiler_params=pltpu.CompilerParams(vmem_limit_bytes=VMEM_LIMIT),
        cost_estimate=takes(8.2),
        name="cross_backward",
    )(queries, up_rows, logs, keys, values)


def tiles_kernel(bound_ref, bias_ref, out_ref):
    shape = (HEAD_DIM, 2 * HEAD_DIM)
    lane = lax.broadcasted_iota(jnp.int32, shape, 1)
    row = lax.broadcasted_iota(jnp.int32, shape, 0)
    left = lane < HEAD_DIM
    offset = row - lane % HEAD_DIM
    for head in range(OWN_HEADS):
        far = jnp.full(shape, bias_ref[BUCKETS - 1, head], WIDE)
        tiles = [jnp.full(shape, MASKED, WIDE)]
        for apart in range(3):
            tile = tiles[0]
            for bucket in range(BUCKETS):
                reached = offset + apart * HEAD_DIM >= bound_ref[bucket]
                tile = jnp.where(reached, bias_ref[bucket, head], tile)
            tiles.append(tile)
        for kind, tile in enumerate(tiles + [far]):
            out_ref[0, head, kind] = jnp.where(left, tile, 0.0)
            out_ref[1, head, kind] = jnp.where(left, 0.0, tile)


def bias_tiles(lower_bounds, own_bias):
    shape = (2, OWN_HEADS, 5, HEAD_DIM, 2 * HEAD_DIM)
    return pl.pallas_call(
        tiles_kernel,
        out_shape=jax.ShapeDtypeStruct(shape, WIDE),
        in_specs=[pl.BlockSpec(memory_space=pltpu.SMEM)] * 2,
        out_specs=pl.BlockSpec(memory_space=pltpu.VMEM),
        cost_estimate=takes(2.7),
        name="bias_tiles",
    )(lower_bounds, own_bias)


def bucket_sums(sums, lower_bounds):
    tiles = sums[0, :, 1:, :, :HEAD_DIM] + sums[1, :, 1:, :, HEAD_DIM:]
    shape = (3, HEAD_DIM, HEAD_DIM, BUCKETS)
    distance = (
        lax.broadcasted_iota(jnp.int32, shape, 0) * HEAD_DIM
        + lax.broadcasted_iota(jnp.int32, shape, 1)
        - lax.broadcasted_iota(jnp.int32, shape, 2)
    )
    upper_bounds = jnp.concatenate([lower_bounds[1:], jnp.full((1,), 1 << 30, jnp.int32)])
    hot = ((distance >= lower_bounds) & (distance < upper_bounds)).astype(LOW)
    near = tiles[:, :3].reshape(OWN_HEADS, -1)
    high = near.astype(LOW)
    low = (near - high.astype(WIDE)).astype(LOW)
    both = jnp.dot(
        jnp.concatenate([high, low]), hot.reshape(-1, BUCKETS), preferred_element_type=WIDE
    )
    table = both[:OWN_HEADS] + both[OWN_HEADS:]
    far = jnp.sum(tiles[:, 3], axis=(1, 2))
    return table + jnp.where(jnp.arange(BUCKETS) == BUCKETS - 1, far[:, None], 0.0)


def rms_of(values):
    return lax.rsqrt(jnp.mean(values * values, axis=-1, keepdims=True) + EPSILON)


def norm_grad(values, inv_rms, gain, upstream):
    scaled = gain * upstream
    inner = jnp.mean(scaled * values, axis=-1, keepdims=True)
    return inv_rms * scaled - values * (inv_rms * inv_rms * inv_rms * inner)


def dot(left, right):
    return jnp.dot(left, right, preferred_element_type=WIDE)


def dot_nt(left, right):
    return lax.dot_general(left, right, NT, preferred_element_type=WIDE)


def dot_tn(left, right):
    return lax.dot_general(left, right, TN, preferred_element_type=WIDE)


def on_device(
    tokens,
    cotangent,
    encoder,
    expert_ids,
    block_order,
    bucket_table,
    first_gain,
    second_gain,
    third_gain,
    position_bias,
    query_weight,
    key_weight,
    value_weight,
    out_weight,
    cross_query,
    cross_key,
    cross_value,
    cross_out,
    router_weight,
    expert_in,
    expert_out,
):
    ctx_size = lax.axis_size("ctx")
    fsdp_size = lax.axis_size("fsdp")
    rests = rest_count()
    f_index = lax.axis_index("fsdp")
    ctx_index = lax.axis_index("ctx")
    core = ctx_index % 2
    group = (ctx_index // 2) % GROUP
    rest = ctx_index // (2 * GROUP)
    seq_count, span, width = tokens.shape
    shard = width // fsdp_size
    own_width = width // GROUP
    half_shard = shard // 2
    half_width = width // 2
    experts = expert_in.shape[0] * ctx_size
    capacity = (5 * seq_count * span + 4 * experts - 1) // (4 * experts)
    hidden_low = tokens.reshape(span, width)
    upstream = cotangent.reshape(span, width).astype(WIDE)

    small = jnp.concatenate(
        [
            first_gain[None],
            second_gain[None],
            third_gain[None],
            router_weight.T,
            jnp.pad(position_bias.reshape(1, -1), ((0, 0), (0, shard - position_bias.size))),
        ]
    )
    small = jnp.pad(small, ((0, -small.shape[0] % 16), (0, 0)))
    extra = small.shape[0]
    qkv_payload, early, late = pack_weights(
        small,
        (
            query_weight,
            key_weight,
            value_weight,
            out_weight,
            cross_key,
            cross_value,
            cross_query,
            cross_out,
        ),
        3,
        group,
        core,
    )
    first_hops = tie(*gather_group(hidden_low), *gather_fsdp(qkv_payload), early, late)
    own_rows = jnp.concatenate(first_hops[:GROUP])
    own_qkv, small_full = place_qkv(first_hops[GROUP : GROUP + fsdp_size], extra, f_index)
    early, late = first_hops[GROUP + fsdp_size :]
    early_x, early_y = swap_fsdp(early, 1), swap_fsdp(early, 2)
    expert_ids = after(expert_ids, qkv_payload)
    block_order, bucket_table, _ = tie(block_order, bucket_table, qkv_payload)

    gain_one = small_full[:, 0].reshape(width).astype(WIDE)
    gain_two = small_full[:, 1].reshape(width).astype(WIDE)
    gain_three = small_full[:, 2].reshape(width).astype(WIDE)
    router_full = small_full[:, 3 : 3 + experts].transpose(1, 0, 2).reshape(experts, width)
    bias_full = small_full[:, 3 + experts, : position_bias.size].reshape(BUCKETS, HEADS)

    slots = jnp.arange(GROUP, dtype=jnp.int32)
    key_devices = (
        ((rest - jnp.arange(rests, dtype=jnp.int32)) % rests)[:, None, None] * (2 * GROUP)
        + (group ^ slots)[None, None, :] * 2
        + (core ^ jnp.arange(2, dtype=jnp.int32))[None, :, None]
    ).reshape(-1)
    key_blocks = (key_devices[:, None] * 2 + jnp.arange(2, dtype=jnp.int32)[None]).reshape(-1)
    block_count = block_order.shape[0]
    hits = key_blocks[:, None] == jnp.arange(block_count, dtype=jnp.int32)[None]
    key_places = jnp.sum(jnp.where(hits, block_order[None], 0), axis=1)
    query_places = key_places[: 2 * GROUP]
    kinds = jnp.clip(query_places[:, None] - key_places[None], -1, 3) + 1
    lower_bounds = jnp.sum(
        (bucket_table[:, None] < jnp.arange(BUCKETS, dtype=jnp.int32)[None]).astype(jnp.int32),
        axis=0,
    )
    own_bias = lax.dynamic_slice_in_dim(
        bias_full.astype(WIDE), group * OWN_HEADS, OWN_HEADS, 1
    )
    tiles = bias_tiles(lower_bounds, own_bias)

    routes = expert_ids.reshape(-1)
    chosen = routes[:, None] == jnp.arange(experts, dtype=jnp.int32)[None]
    order = jnp.arange(span)
    lower = (order[:, None] > order[None]).astype(LOW)
    earlier = dot(lower, chosen.astype(LOW))
    slot_rank = jnp.sum(jnp.where(chosen, earlier, 0.0), axis=1).astype(jnp.int32)
    block_rows = -(-2 * capacity // 8) * 8
    slot_rows = rests * GROUP * block_rows
    target = (
        (((routes // (2 * GROUP) - rest) % rests) * GROUP + (((routes // 2) % GROUP) ^ group))
        * block_rows
        + core * capacity
        + slot_rank
    )
    code = jnp.where(slot_rank < capacity, (routes % 2) * slot_rows + target, -1)
    own_code = jnp.broadcast_to(code.astype(WIDE)[:, None], (span, 128))
    other_code = swap_core(own_code)
    codes = jnp.concatenate([own_code[:, :1], other_code[:, :1]]).astype(jnp.int32)
    placing = (
        codes == core * slot_rows + jnp.arange(slot_rows, dtype=jnp.int32)[None]
    ).astype(LOW)
    chosen = chosen.astype(WIDE)

    wide_rows = own_rows.astype(WIDE)
    normed_own = (wide_rows * rms_of(wide_rows) * gain_one).astype(LOW)
    own_count = GROUP * span
    queries = dot(normed_own, own_qkv[:, :own_width]).astype(LOW)
    pairs_own = dot(normed_own, own_qkv[:, own_width:]).astype(LOW)
    pairs_rest = swap_core(pairs_own)
    encoder_pieces = gather_group(after(encoder, early).reshape(-1, width))
    pairs_own, pairs_rest, early_x, early_y = tie(pairs_own, pairs_rest, early_x, early_y)
    early_xy = swap_fsdp(early_x, 2)
    late_x, late_y = swap_fsdp(late, 1), swap_fsdp(late, 2)
    if rests > 1:
        near = jnp.concatenate([pairs_own, pairs_rest])
        pairs_rest = jnp.concatenate(
            [pairs_rest] + [shift_rest(near, r) for r in range(1, rests)]
        )
    *attended_own, self_logs = self_forward(kinds, tiles, queries, pairs_own, pairs_rest)
    attended_own, early_xy, late_x, encoder_pieces = tie(
        attended_own, early_xy, late_x, encoder_pieces
    )
    attended = [attended_own[0]] + [swap_group(attended_own[k], k) for k in range(1, GROUP)]
    late_xy = swap_fsdp(late_x, 2)
    early_mine = stack_pieces((early, early_x, early_y, early_xy), 1, f_index, group)
    early_theirs = swap_core(early_mine)
    encoder_own = jnp.concatenate(encoder_pieces)
    encoder_other = swap_core(encoder_own)
    *attended, early_theirs, encoder_other = tie(*attended, early_theirs, encoder_other)
    out_full, cross_k_full, cross_v_full = weave_halves(early_mine, early_theirs, core)
    encoder_all = jnp.concatenate([encoder_own, encoder_other])
    if rests > 1:
        encoder_all = jnp.concatenate(
            [encoder_all] + [shift_rest(encoder_all, r) for r in range(1, rests)]
        )
    attended = jnp.concatenate(attended, axis=1)
    hidden = hidden_low.astype(WIDE)
    first_sum = hidden + dot(attended, out_full)
    inv_two = rms_of(first_sum)
    normed_two = (first_sum * inv_two * gain_two).astype(LOW)
    normed_two, late_xy, late_y = tie(normed_two, late_xy, late_y)
    late_mine = stack_pieces((late, late_x, late_y, late_xy), 0, f_index, group)
    late_theirs = swap_core(late_mine)

    cross_keys = dot(after(encoder_all, late_mine), cross_k_full).astype(LOW)
    cross_values = dot(encoder_all, cross_v_full).astype(LOW)
    cross_q_full, cross_o_full = weave_halves(late_mine, late_theirs, core)
    cross_rows = dot(normed_two, cross_q_full).astype(LOW)
    cross_mixed, cross_logs = cross_forward(cross_rows, cross_keys, cross_values)
    second_sum = first_sum + dot(cross_mixed, cross_o_full)
    inv_three = rms_of(second_sum)
    normed_three = (second_sum * inv_three * gain_three).astype(LOW)

    logits = dot_nt(normed_three, router_full)
    router_probs = jax.nn.softmax(logits, axis=-1)
    gate_value = jnp.sum(router_probs * chosen, axis=-1, keepdims=True)
    scaled_up = (gate_value * upstream).astype(LOW)

    sides = jnp.concatenate([normed_three, scaled_up], axis=1)
    sides = jnp.concatenate([sides, swap_core(sides)])
    sent = dot_tn(placing, sides).astype(LOW).reshape(rests, GROUP * block_rows, 2 * width)
    near = jnp.concatenate(
        [sent[0]] + [shift_rest(sent[r], r) for r in range(1, rests)]
    ).reshape(rests, GROUP, block_rows, 2 * width)
    arrived = jnp.concatenate(
        [near[:, 0]] + [swap_group(near[:, k], k) for k in range(1, GROUP)], axis=1
    ).reshape(slot_rows, 2 * width)
    arrivals = tie(*gather_fsdp(arrived))
    answers, middle = run_experts(arrivals, expert_in[0], expert_out[0])
    answers = tie(answers[0], *[swap_fsdp(answers[k], k) for k in range(1, fsdp_size)])
    answers = sum_home(answers, rests)
    near = [answers[0]] + [swap_group(answers[k], k) for k in range(1, GROUP)]
    near = jnp.concatenate(
        [piece.reshape(rests, block_rows, 2 * width) for piece in near], axis=1
    )
    home = jnp.concatenate([near[0]] + [shift_rest(near[r], -r) for r in range(1, rests)])
    both = dot(placing, home).astype(LOW)
    both = both[:span].astype(WIDE) + swap_core(both[span:]).astype(WIDE)
    moe_rows, dispatch_grad = both[:, :width], both[:, width:]
    grad_expert_in, grad_expert_out = expert_grads(arrivals, middle)
    grad_expert_in, grad_expert_out = grad_expert_in[None], grad_expert_out[None]

    mixed_out = (second_sum + gate_value * moe_rows).astype(LOW).reshape(tokens.shape)
    gate_grad = jnp.sum(upstream * moe_rows, axis=-1, keepdims=True)
    logit_low = (gate_grad * gate_value * (chosen - router_probs)).astype(LOW)
    three_grad = dispatch_grad + dot(logit_low, router_full)
    second_grad = upstream + norm_grad(second_sum, inv_three, gain_three, three_grad)
    gain_three_part = jnp.sum(three_grad * second_sum * inv_three, axis=0, keepdims=True)
    router_part = dot_tn(logit_low, normed_three)
    spread = jnp.concatenate([router_part, gain_three_part])
    spread = jnp.pad(spread, ((0, -spread.shape[0] % 16), (0, 0)))

    branch_two = second_grad.astype(LOW)
    cross_up = dot_nt(branch_two, cross_o_full).astype(LOW)
    cross_q_low, cross_k_part, cross_v_part = cross_backward(
        cross_rows, cross_up, cross_logs, cross_keys, cross_values
    )
    two_grad = dot_nt(cross_q_low, cross_q_full)
    first_grad = second_grad + norm_grad(first_sum, inv_two, gain_two, two_grad)

    branch_one = first_grad.astype(LOW)
    self_up = dot_nt(branch_one, out_full).astype(LOW)
    branch_one, self_up = tie(branch_one, self_up)
    up_pieces = [self_up[:, :own_width]] + [
        swap_group(self_up[:, k * own_width : (k + 1) * own_width], k) for k in range(1, GROUP)
    ]
    extra_rows = -(-spread.shape[0] // 64) * 64
    keep, send = weight_grads(
        (False, False, False, False, True),
        (
            (cross_mixed, branch_two),
            (normed_two, cross_q_low),
            (encoder_all, cross_k_part),
            (encoder_all, cross_v_part),
            (attended, branch_one),
        ),
        spread,
        extra_rows,
        f_index,
        core,
        group,
        fsdp_size,
    )
    *up_pieces, received = tie(*up_pieces, swap_core(send))
    up_own = jnp.concatenate(up_pieces)
    middle = keep.shape[1] // 2
    top = [add_low(keep[k, :middle], received[k, :middle]) for k in range(fsdp_size)]
    bottom = [add_low(keep[k, middle:], received[k, middle:]) for k in range(fsdp_size)]
    up_own, top[1:], bottom[1:] = tie(up_own, top[1:], bottom[1:])
    top = [top[0]] + [swap_fsdp(top[k], k) for k in range(1, fsdp_size)]
    query_low, pair_own, pair_rest, bias_parts = self_backward(
        0, own_count // span, kinds, tiles, queries, up_own, self_logs, pairs_own, pairs_rest
    )
    query_low, pair_own, pair_rest, bias_parts, top, bottom = tie(
        query_low, pair_own, pair_rest, bias_parts, top, bottom
    )
    bottom = [bottom[0]] + [swap_fsdp(bottom[k], k) for k in range(1, fsdp_size)]
    if rests > 1:
        near = jnp.concatenate([pair_own, pair_rest[:own_count]]).astype(WIDE)
        for r in range(1, rests):
            first = (2 * r - 1) * own_count
            piece = pair_rest[first : first + 2 * own_count]
            near = near + shift_rest(piece, -r).astype(WIDE)
        pair_own, pair_rest = near[:own_count].astype(LOW), near[own_count:].astype(LOW)
    one_parts, qkv_keep, qkv_send = key_grads(
        normed_own, query_low, pair_own, swap_core(pair_rest), own_qkv, f_index, core, fsdp_size
    )
    one_parts = [one_parts[0]] + [swap_group(one_parts[k], k) for k in range(1, GROUP)]
    qkv_send, bottom, bias_parts, one_parts[1] = tie(
        swap_core(qkv_send), bottom, bias_parts, one_parts[1]
    )
    quarters = sum_quarters(top, bottom, group)
    quarters = [quarters[0]] + [swap_group(quarters[k], k) for k in range(1, GROUP)]

    table = jnp.pad(bucket_sums(bias_parts, lower_bounds).T, ((0, 0), (0, 128 - OWN_HEADS)))
    qkv_parts = add_qkv(qkv_keep, qkv_send, table, f_index)
    qkv_parts = [qkv_parts[0]] + [swap_fsdp(qkv_parts[k], k) for k in range(1, fsdp_size)]
    qkv_parts, one_parts, quarters = tie(qkv_parts, one_parts, quarters)
    dense_shard = sum_rest(sum_low(quarters[0], quarters[1:])).astype(LOW)
    one_grad = sum(one.astype(WIDE) for one in one_parts)
    tokens_grad = first_grad + norm_grad(hidden, rms_of(hidden), gain_one, one_grad)
    tokens_grad = tokens_grad.reshape(tokens.shape)
    qkv_shard = sum_rest(sum_low(qkv_parts[0], qkv_parts[1:])).astype(LOW)
    spots = [group ^ k for k in range(GROUP)]
    qkv_mine = collect(gather_group(qkv_shard), spots, 1)[0]
    query_total, key_total, value_total, bias_total, grad_gain_one = finish_qkv(
        qkv_mine,
        swap_core(qkv_mine),
        (query_weight, key_weight, value_weight),
        first_gain,
        core,
        position_bias.shape,
    )
    dense_mine = collect(gather_group(dense_shard), spots, 2).reshape(-1, half_width)
    (
        cross_o_total,
        cross_q_total,
        cross_k_total,
        cross_v_total,
        out_total,
        grad_router,
        grad_gain_three,
        grad_gain_two,
    ) = finish_weights(dense_mine, swap_core(dense_mine), cross_query, second_gain, core, experts)

    return (
        mixed_out,
        tokens_grad,
        grad_gain_one,
        grad_gain_two,
        grad_gain_three,
        bias_total,
        query_total,
        key_total,
        value_total,
        out_total,
        cross_q_total,
        cross_k_total,
        cross_v_total,
        cross_o_total,
        grad_router,
        grad_expert_in,
        grad_expert_out,
    )


def solution(mesh):
    rows = P("fsdp", "ctx", None)
    vector = P("fsdp")
    matrix = P("fsdp", None)
    expert_specs = (P("ctx", None, "fsdp"), P("ctx", "fsdp", None))
    return jax.shard_map(
        on_device,
        mesh=mesh,
        in_specs=(rows,) * 4 + (P(),) * 2 + (vector,) * 3 + (matrix,) * 10 + expert_specs,
        out_specs=(rows,) * 2 + (vector,) * 3 + (matrix,) * 10 + expert_specs,
        check_vma=False,
    )
```

```python
import math
from functools import partial

import jax
import jax.numpy as jnp
from jax import lax
from jax.experimental import pallas as pl
from jax.experimental.pallas import tpu as pltpu
from jax.sharding import PartitionSpec as P

HEADS = 12
HEAD_DIM = 64
BUCKETS = 32
GROUP = 4
OWN_HEADS = HEADS // GROUP
EPSILON = 1e-06
MASKED = -1e30
LOW = jnp.bfloat16
WIDE = jnp.float32
VMEM_LIMIT = 56 * 1024 * 1024
NT = (((1,), (1,)), ((), ()))
TN = (((0,), (0,)), ((), ()))


def swap_fsdp(rows, k):
    size = lax.axis_size("fsdp")
    return lax.ppermute(rows, "fsdp", [(i, i ^ k) for i in range(size)])


def swap_core(rows):
    size = lax.axis_size("ctx")
    return lax.ppermute(rows, "ctx", [(i, i ^ 1) for i in range(size)])


def swap_group(rows, k):
    size = lax.axis_size("ctx")
    return lax.ppermute(rows, "ctx", [(i, i ^ (2 * k)) for i in range(size)])


def shift_rest(rows, r):
    size = lax.axis_size("ctx")
    step = 2 * GROUP * r
    return lax.ppermute(rows, "ctx", [(i, (i + step) % size) for i in range(size)])


def rest_count():
    return lax.axis_size("ctx") // (2 * GROUP)


def block_at(blocks, index):
    return lax.dynamic_index_in_dim(blocks, index, 0, keepdims=False)


def in_order(parts, index):
    parts = list(parts)
    bit = 1
    while bit < len(parts):
        flag = (index & bit) != 0
        parts = [jnp.where(flag, parts[i ^ bit], parts[i]) for i in range(len(parts))]
        bit *= 2
    return parts


def tie(*values):
    return lax.optimization_barrier(values)


def after(value, *earlier):
    return tie(value, *earlier)[0]


def gather_group(rows):
    return [rows] + [swap_group(rows, k) for k in range(1, GROUP)]


def gather_fsdp(rows):
    return [rows] + [swap_fsdp(rows, k) for k in range(1, lax.axis_size("fsdp"))]


def sum_rest(values):
    size = lax.axis_size("ctx")
    if rest_count() == 1:
        return values
    near = 2 * GROUP
    groups = [list(range(i, size, near)) for i in range(near)]
    return lax.psum(values, "ctx", axis_index_groups=groups)


def takes(us):
    return pl.CostEstimate(flops=int(us * 1e9), bytes_accessed=int(us * 3.5e6), transcendentals=0)


def vmem(count):
    return [pl.BlockSpec(memory_space=pltpu.VMEM)] * count


def smem():
    return pl.BlockSpec(memory_space=pltpu.SMEM)


def small_rows(small):
    return -(-(8 + small[1].shape[0] + small[2].shape[0]) // 16) * 16


def pack_kernel(index_ref, gain_ref, router_ref, bias_ref, *refs):
    group, core = index_ref[0], index_ref[1]
    ins, (qkv_ref, early_ref, late_ref) = refs[:-3], refs[-3:]
    rows = early_ref.shape[1]
    own = qkv_ref.shape[1] // 3
    shard = 2 * rows
    for choice in range(GROUP):

        @pl.when(group == choice)
        def take():
            for which in range(3):
                qkv_ref[:shard, which * own : (which + 1) * own] = ins[which][
                    :, choice * own : (choice + 1) * own
                ]

    def widened(rows, count):
        rows = rows.astype(WIDE)
        if rows.shape[1] < shard:
            spare = jnp.zeros((rows.shape[0], shard - rows.shape[1]), WIDE)
            rows = jnp.concatenate([rows, spare], axis=1)
        if rows.shape[0] < count:
            rows = jnp.concatenate([rows, jnp.zeros((count - rows.shape[0], shard), WIDE)])
        return rows

    experts = router_ref.shape[0]
    extra = qkv_ref.shape[0] - shard
    small = jnp.concatenate(
        [
            widened(gain_ref[...], 8),
            router_ref[...].astype(WIDE),
            widened(bias_ref[...], extra - 8 - experts),
        ]
    )
    qkv_ref[shard:] = jnp.zeros((extra, 3 * own), LOW)
    qkv_ref[shard:, :shard] = small.astype(LOW)
    here = pl.ds(pl.multiple_of(core * rows, 16), rows)
    early = early_ref.shape[0]
    for i in range(early):
        early_ref[i] = ins[3 + i][here]
    for i in range(late_ref.shape[0]):
        late_ref[i] = ins[3 + early + i][here]


def pack_weights(small, weights, early, group, core):
    shard, width = weights[0].shape
    own = width // GROUP
    late = len(weights) - 3 - early
    return pl.pallas_call(
        pack_kernel,
        out_shape=[
            jax.ShapeDtypeStruct((shard + small_rows(small), 3 * own), LOW),
            jax.ShapeDtypeStruct((early, shard // 2, width), LOW),
            jax.ShapeDtypeStruct((late, shard // 2, width), LOW),
        ],
        in_specs=[smem()] + vmem(3 + len(weights)),
        out_specs=vmem(3),
        compiler_params=pltpu.CompilerParams(vmem_limit_bytes=VMEM_LIMIT),
        cost_estimate=takes(3),
        name="pack_weights",
    )(jnp.stack([group, core]).astype(jnp.int32), *small, *weights)


def place_qkv_kernel(index_ref, *refs):
    pieces, (out, small) = refs[:-2], refs[-2:]
    rows = out.shape[1]
    for k in range(len(pieces)):
        out[index_ref[k]] = pieces[k][:rows]
        small[index_ref[k]] = pieces[k][rows:, :rows]


def place_qkv(pieces, extra, f_index):
    count = len(pieces)
    rows, width = pieces[0].shape
    rows = rows - extra
    whole, small = pl.pallas_call(
        place_qkv_kernel,
        out_shape=[
            jax.ShapeDtypeStruct((count, rows, width), LOW),
            jax.ShapeDtypeStruct((count, extra, rows), LOW),
        ],
        in_specs=[smem()] + vmem(count),
        out_specs=vmem(2),
        compiler_params=pltpu.CompilerParams(vmem_limit_bytes=VMEM_LIMIT),
        cost_estimate=takes(2.3),
        name="place_qkv",
    )(jnp.stack([f_index ^ k for k in range(count)]).astype(jnp.int32), *pieces)
    return whole.reshape(count * rows, width), small


def stack_kernel(turned, index_ref, *refs):
    count = len(refs) - 1
    out = refs[-1]
    for item in range(out.shape[0]):
        for k in range(count):
            spot = index_ref[count + k] if item < turned else index_ref[k]
            out[item, spot] = refs[k][item]


def stack_pieces(pieces, turned, f_index, g_index):
    count = len(pieces)
    spots = [f_index ^ k for k in range(count)]
    indices = jnp.stack(spots + [g_index ^ spot for spot in spots]).astype(jnp.int32)
    number, rows, width = pieces[0].shape
    return pl.pallas_call(
        partial(stack_kernel, turned),
        out_shape=jax.ShapeDtypeStruct((number, count, rows, width), LOW),
        in_specs=[smem()] + vmem(count),
        out_specs=vmem(1)[0],
        compiler_params=pltpu.CompilerParams(vmem_limit_bytes=VMEM_LIMIT),
        cost_estimate=takes(2.7),
        name="stack_pieces",
    )(indices, *pieces)


def weave_kernel(index_ref, mine_ref, theirs_ref, *outs):
    core = index_ref[0]
    for item, out in enumerate(outs):
        for block in range(out.shape[0]):
            out[block, core] = mine_ref[item, block]
            out[block, 1 - core] = theirs_ref[item, block]


def weave_halves(mine, theirs, core):
    number, count, rows, width = mine.shape
    whole = pl.pallas_call(
        weave_kernel,
        out_shape=[jax.ShapeDtypeStruct((count, 2, rows, width), LOW)] * number,
        in_specs=[smem()] + vmem(2),
        out_specs=vmem(number),
        compiler_params=pltpu.CompilerParams(vmem_limit_bytes=VMEM_LIMIT),
        cost_estimate=takes(4),
        name="weave_halves",
    )(core.reshape(1).astype(jnp.int32), mine, theirs)
    return [one.reshape(count * 2 * rows, width) for one in whole]


def expert_kernel(*refs):
    count = (len(refs) - 3) // 2
    pieces, in_ref, out_ref = refs[:count], refs[count], refs[count + 1]
    answers, middle = refs[count + 2 : 2 * count + 2], refs[-1]
    rows, width = pieces[0].shape[0], pieces[0].shape[1] // 2
    hidden = in_ref.shape[1]
    scale = math.sqrt(2 / math.pi)
    for k in range(count):
        inner = dot(pieces[k][:, :width], in_ref[...])
        square = inner * inner
        bent = jnp.tanh(scale * (inner + 0.044715 * (inner * square)))
        activated = (0.5 * inner * (1.0 + bent)).astype(LOW)
        slope = 0.5 * (1.0 + bent) + 0.5 * inner * (1.0 - bent * bent) * (
            scale * (1.0 + 3 * 0.044715 * square)
        )
        inner_low = (dot_nt(pieces[k][:, width:], out_ref[...]) * slope).astype(LOW)
        answers[k][:, :width] = dot(activated, out_ref[...]).astype(LOW)
        answers[k][:, width:] = dot_nt(inner_low, in_ref[...]).astype(LOW)
        here = slice(k * rows, (k + 1) * rows)
        middle[here, :hidden] = activated
        middle[here, hidden:] = inner_low


def run_experts(pieces, expert_in, expert_out):
    count = len(pieces)
    width, hidden = expert_in.shape
    rows = pieces[0].shape[0]
    results = pl.pallas_call(
        expert_kernel,
        out_shape=[jax.ShapeDtypeStruct((rows, 2 * width), LOW)] * count
        + [jax.ShapeDtypeStruct((count * rows, 2 * hidden), LOW)],
        in_specs=vmem(count + 2),
        out_specs=vmem(count + 1),
        compiler_params=pltpu.CompilerParams(vmem_limit_bytes=VMEM_LIMIT),
        cost_estimate=takes(4.1),
        name="experts",
    )(*pieces, expert_in, expert_out)
    return list(results[:count]), results[count]


def expert_grads_kernel(count, *refs):
    pieces, middles, (in_ref, out_ref) = refs[:count], refs[count:-2], refs[-2:]
    width, hidden = in_ref.shape
    rows = jnp.concatenate([piece[...] for piece in pieces])
    middle = jnp.concatenate([one[...] for one in middles])
    in_ref[...] = dot_tn(rows[:, :width], middle[:, hidden:])
    out_ref[...] = dot_tn(middle[:, :hidden], rows[:, width:])


def expert_grads(pieces, middles):
    width = pieces[0].shape[1] // 2
    hidden = middles[0].shape[1] // 2
    return pl.pallas_call(
        partial(expert_grads_kernel, len(pieces)),
        out_shape=[
            jax.ShapeDtypeStruct((width, hidden), WIDE),
            jax.ShapeDtypeStruct((hidden, width), WIDE),
        ],
        in_specs=vmem(len(pieces) + len(middles)),
        out_specs=vmem(2),
        compiler_params=pltpu.CompilerParams(vmem_limit_bytes=VMEM_LIMIT),
        cost_estimate=takes(5.7),
        name="expert_grads",
    )(*pieces, *middles)


def home_kernel(rests, *refs):
    pieces, outs = refs[: len(refs) - GROUP], refs[len(refs) - GROUP :]
    block = outs[0].shape[0] // rests
    for k, out in enumerate(outs):
        for r in range(rests):
            here = slice((r * GROUP + k) * block, (r * GROUP + k + 1) * block)
            out[r * block : (r + 1) * block] = sum_low(
                pieces[0][here], [piece[here] for piece in pieces[1:]]
            )


def sum_home(pieces, rests):
    rows, width = pieces[0].shape
    return pl.pallas_call(
        partial(home_kernel, rests),
        out_shape=[jax.ShapeDtypeStruct((rows // GROUP, width), LOW)] * GROUP,
        in_specs=vmem(len(pieces)),
        out_specs=vmem(GROUP),
        compiler_params=pltpu.CompilerParams(vmem_limit_bytes=VMEM_LIMIT),
        cost_estimate=takes(2.4),
        name="sum_home",
    )(*pieces)


def grads_kernel(turns, extra_rows, index_ref, *refs):
    f_index, core, turn = index_ref[0], index_ref[1], index_ref[2]
    ins, spread_ref, keep, send = refs[: 2 * len(turns)], refs[-3], refs[-2], refs[-1]
    size, _, half = keep.shape
    shard = ins[0].shape[1] // size
    for item, turned in enumerate(turns):
        rows_ref, grad_ref = ins[2 * item], ins[2 * item + 1]
        for out, side in ((keep, core), (send, 1 - core)):
            grad = grad_ref[:, pl.ds(pl.multiple_of(side * half, 128), half)]
            product = dot_tn(rows_ref[...], grad).astype(LOW)
            for block in range(size):
                spot = block ^ f_index ^ (turn if turned else 0)
                out[spot, item * shard : (item + 1) * shard] = product[
                    block * shard : (block + 1) * shard
                ]
    first = len(turns) * shard
    for block in range(size):
        spot = block ^ f_index
        piece = spread_ref[:, block * shard : (block + 1) * shard].astype(LOW)
        keep[spot, first:] = jnp.zeros((extra_rows, half), LOW)
        send[spot, first:] = jnp.zeros((extra_rows, half), LOW)
        keep[spot, first : first + spread_ref.shape[0], :shard] = piece


def weight_grads(turns, pairs, spread, extra_rows, f_index, core, turn, size):
    width = pairs[0][0].shape[1]
    rows = len(turns) * (width // size) + extra_rows
    shape = jax.ShapeDtypeStruct((size, rows, width // 2), LOW)
    flat = [array for pair in pairs for array in pair] + [spread]
    return pl.pallas_call(
        partial(grads_kernel, turns, extra_rows),
        out_shape=[shape, shape],
        in_specs=[smem()] + vmem(len(flat)),
        out_specs=vmem(2),
        compiler_params=pltpu.CompilerParams(vmem_limit_bytes=VMEM_LIMIT),
        cost_estimate=takes(7.5),
        name="weight_grads",
    )(jnp.stack([f_index, core, turn]).astype(jnp.int32), *flat)


def add_low(left, right):
    return (left.astype(WIDE) + right.astype(WIDE)).astype(LOW)


def sum_low(first, others):
    total = first.astype(WIDE)
    for other in others:
        total = total + other.astype(WIDE)
    return total.astype(LOW)


def quarter_kernel(index_ref, *refs):
    outs = refs[len(refs) - GROUP :]
    count = (len(refs) - GROUP) // 2
    rows = outs[0].shape[0] // 2
    for k, out in enumerate(outs):
        here = pl.ds(pl.multiple_of(index_ref[k] * rows, 16), rows)
        for half in range(2):
            pieces = refs[half * count : (half + 1) * count]
            out[half * rows : (half + 1) * rows] = sum_low(
                pieces[0][here], [piece[here] for piece in pieces[1:]]
            )


def sum_quarters(top, bottom, group):
    rows, width = top[0].shape
    pieces = list(top) + list(bottom)
    return pl.pallas_call(
        quarter_kernel,
        out_shape=[jax.ShapeDtypeStruct((2 * rows // GROUP, width), LOW)] * GROUP,
        in_specs=[smem()] + vmem(len(pieces)),
        out_specs=vmem(GROUP),
        compiler_params=pltpu.CompilerParams(vmem_limit_bytes=VMEM_LIMIT),
        cost_estimate=takes(3),
        name="sum_quarters",
    )(jnp.stack([group ^ k for k in range(GROUP)]).astype(jnp.int32), *pieces)


def collect_kernel(index_ref, *refs):
    pieces, out = refs[:-1], refs[-1]
    for k in range(len(pieces)):
        out[index_ref[k]] = pieces[k][...]


def collect(pieces, spots):
    return pl.pallas_call(
        collect_kernel,
        out_shape=jax.ShapeDtypeStruct((GROUP,) + pieces[0].shape, LOW),
        in_specs=[smem()] + vmem(GROUP),
        out_specs=vmem(1)[0],
        cost_estimate=takes(2),
        name="collect",
    )(jnp.stack(spots).astype(jnp.int32), *pieces)


def row_sums(values):
    ones = jnp.ones((8, values.shape[1]), WIDE)
    sums = lax.dot_general(
        ones, values, NT, precision=lax.Precision.HIGHEST, preferred_element_type=WIDE
    )
    return sums[:1]


def finish_kernel(index_ref, *refs):
    mine_pieces, their_pieces = refs[:GROUP], refs[GROUP : 2 * GROUP]
    weight_ref, gain_ref, *outs, mine_ref, theirs_ref = refs[2 * GROUP :]
    core = index_ref[GROUP]
    quarter = mine_pieces[0].shape[0] // 2
    for out, pieces in ((mine_ref, mine_pieces), (theirs_ref, their_pieces)):
        for k in range(GROUP):
            for part in range(2):
                first = (part * GROUP + index_ref[k]) * quarter
                out[pl.ds(pl.multiple_of(first, 16), quarter)] = pieces[k][
                    part * quarter : (part + 1) * quarter
                ]
    half = mine_ref.shape[1]
    shard = outs[0].shape[0]
    wholes, (router_ref, third_ref, second_ref) = outs[:-3], outs[-3:]
    for number, out in enumerate(wholes):
        here = slice(number * shard, (number + 1) * shard)
        out[:, pl.ds(pl.multiple_of(core * half, 128), half)] = mine_ref[here].astype(WIDE)
        out[:, pl.ds(pl.multiple_of((1 - core) * half, 128), half)] = theirs_ref[here].astype(WIDE)
    second_ref[...] = row_sums(weight_ref[...].astype(WIDE) * wholes[1][...]) / gain_ref[
        ...
    ].astype(WIDE)
    here = slice(len(wholes) * shard, None)
    spread = mine_ref[here].astype(WIDE) + theirs_ref[here].astype(WIDE)
    experts = router_ref.shape[0]
    router_ref[...] = spread[:experts, :shard]
    third_ref[...] = spread[experts : experts + 1, :shard]


def finish_weights(mine, theirs, weight, gain, group, core, experts):
    shard, width = weight.shape
    rows, half = mine[0].shape
    shapes = [(shard, width)] * 5 + [(experts, shard)] + [(1, shard)] * 2
    results = pl.pallas_call(
        finish_kernel,
        out_shape=[jax.ShapeDtypeStruct(shape, WIDE) for shape in shapes],
        in_specs=[smem()] + vmem(2 * GROUP + 2),
        out_specs=vmem(len(shapes)),
        scratch_shapes=[pltpu.VMEM((GROUP * rows, half), LOW)] * 2,
        compiler_params=pltpu.CompilerParams(vmem_limit_bytes=VMEM_LIMIT),
        cost_estimate=takes(3),
        name="finish_weights",
    )(
        jnp.stack([group ^ k for k in range(GROUP)] + [core]).astype(jnp.int32),
        *mine,
        *theirs,
        weight,
        gain[None],
    )
    return list(results[:5]) + [results[5].T] + [one[0] for one in results[6:]]


def key_grads_kernel(index_ref, rows_ref, query_ref, own_ref, rest_ref, weight_ref, *outs):
    f_index, core = index_ref[0], index_ref[1]
    ones, (keep, send) = outs[:-2], outs[-2:]
    grads = jnp.concatenate([query_ref[...], add_low(own_ref[...], rest_ref[...])], axis=1)
    count = grads.shape[0] // len(ones)
    for k, one in enumerate(ones):
        one[...] = dot_nt(grads[k * count : (k + 1) * count], weight_ref[...]).astype(LOW)
    size, rows, _ = keep.shape
    product = dot_tn(rows_ref[...], grads)
    for block in range(size):
        spot = block ^ f_index
        top = product[2 * block * rows : (2 * block + 1) * rows].astype(LOW)
        bottom = product[(2 * block + 1) * rows : (2 * block + 2) * rows].astype(LOW)
        keep[spot] = jnp.where(core == 0, top, bottom)
        send[spot] = jnp.where(core == 0, bottom, top)


def key_grads(rows, query, own, rest, weight, f_index, core, size):
    count, width = rows.shape
    shape = jax.ShapeDtypeStruct((size, width // size // 2, weight.shape[1]), LOW)
    results = pl.pallas_call(
        key_grads_kernel,
        out_shape=[jax.ShapeDtypeStruct((count // GROUP, width), LOW)] * GROUP + [shape] * 2,
        in_specs=[smem()] + vmem(5),
        out_specs=vmem(GROUP + 2),
        compiler_params=pltpu.CompilerParams(vmem_limit_bytes=VMEM_LIMIT),
        cost_estimate=takes(0.1),
        name="key_grads",
    )(jnp.stack([f_index, core]).astype(jnp.int32), rows, query, own, rest, weight)
    return list(results[:GROUP]), results[GROUP], results[GROUP + 1]


def add_qkv_kernel(index_ref, keep_ref, received_ref, table_ref, *outs):
    rows = keep_ref.shape[1]
    buckets = table_ref.shape[0] // len(outs)
    for k, out in enumerate(outs):
        out[:rows] = add_low(keep_ref[k], received_ref[k])
        here = pl.ds(pl.multiple_of((index_ref[0] ^ k) * buckets, 8), buckets)
        table = table_ref[here]
        spare = out.shape[1] - table.shape[1]
        table = jnp.concatenate([table, jnp.zeros((buckets, spare), WIDE)], axis=1)
        below = jnp.zeros((out.shape[0] - rows - buckets, out.shape[1]), WIDE)
        out[rows:] = jnp.concatenate([table, below]).astype(LOW)


def add_qkv(keep, received, table, f_index):
    size, rows, width = keep.shape
    return list(
        pl.pallas_call(
            add_qkv_kernel,
            out_shape=[jax.ShapeDtypeStruct((rows + 16, width), LOW)] * size,
            in_specs=[smem()] + vmem(3),
            out_specs=vmem(size),
            compiler_params=pltpu.CompilerParams(vmem_limit_bytes=VMEM_LIMIT),
            cost_estimate=takes(2),
            name="add_qkv",
        )(f_index.reshape(1).astype(jnp.int32), keep, received, table)
    )


def qkv_finish_kernel(index_ref, mine_ref, theirs_ref, *refs):
    core = index_ref[0]
    weights, gain_ref, outs, bias_ref, gain_out = refs[:3], refs[3], refs[4:7], refs[7], refs[8]
    own = mine_ref.shape[2] // 3
    rows = outs[0].shape[0] // 2
    product = None
    for which in range(3):
        for source, side in ((mine_ref, core), (theirs_ref, 1 - core)):
            whole = jnp.concatenate(
                [
                    source[g, :rows, which * own : (which + 1) * own].astype(WIDE)
                    for g in range(GROUP)
                ],
                axis=1,
            )
            outs[which][pl.ds(pl.multiple_of(side * rows, 8), rows)] = whole
        one = weights[which][...].astype(WIDE) * outs[which][...]
        product = one if product is None else product + one
    gain_out[...] = row_sums(product) / gain_ref[...].astype(WIDE)
    buckets = bias_ref.shape[0]
    for g in range(GROUP):
        table = mine_ref[g, rows:, :128].astype(WIDE) + theirs_ref[g, rows:, :128].astype(WIDE)
        bias_ref[:, g * OWN_HEADS : (g + 1) * OWN_HEADS] = table[:buckets, :OWN_HEADS]


def finish_qkv(mine, theirs, weights, gain, core, bias_shape):
    shard, width = weights[0].shape
    shapes = [(shard, width)] * 3 + [bias_shape, (1, shard)]
    results = pl.pallas_call(
        qkv_finish_kernel,
        out_shape=[jax.ShapeDtypeStruct(shape, WIDE) for shape in shapes],
        in_specs=[smem()] + vmem(6),
        out_specs=vmem(len(shapes)),
        compiler_params=pltpu.CompilerParams(vmem_limit_bytes=VMEM_LIMIT),
        cost_estimate=takes(2.6),
        name="qkv_finish",
    )(core.reshape(1).astype(jnp.int32), mine, theirs, *weights, gain[None])
    return list(results[:4]) + [results[4][0]]


def head_lanes(head, width):
    first = head // 2 * 128
    return first, min(first + 128, width)


def only_head(rows, head):
    if rows.shape[-1] == HEAD_DIM:
        return rows
    lane = lax.broadcasted_iota(jnp.int32, rows.shape, rows.ndim - 1)
    return jnp.where(lane // HEAD_DIM == head % 2, rows, jnp.zeros_like(rows))


def bias_block(kind_ref, tile_ref, head, step, first_block, width):
    rows = []
    for half in range(2):
        columns = []
        for pair in range(width // 128):
            left = kind_ref[2 * step + half, first_block + 2 * pair]
            right = kind_ref[2 * step + half, first_block + 2 * pair + 1]
            columns.append(tile_ref[0, head, left] + tile_ref[1, head, right])
        rows.append(jnp.concatenate(columns, axis=1))
    return jnp.concatenate(rows, axis=0)


def chunk_scores(query_head, key_ref, lanes, first, width, head, step, kind_ref, tile_ref):
    keys = key_ref[pl.ds(first, width), lanes[0] : lanes[1]]
    scores = lax.dot_general(query_head, keys, NT, preferred_element_type=WIDE)
    if kind_ref is not None:
        scores = scores + bias_block(kind_ref, tile_ref, head, step, first // HEAD_DIM, width)
    return scores


def forward_body(step, kind_ref, tile_ref, query_ref, key_ref, value_ref, out_ref, log_ref):
    width = query_ref.shape[-1]
    key_count = key_ref.shape[0]
    chunk = math.gcd(key_count, 1024)
    rows = query_ref.shape[0]
    lane = lax.broadcasted_iota(jnp.int32, (rows, 128), 1)
    logs = jnp.zeros((rows, 128), WIDE)
    tile_out = None
    for head in range(width // HEAD_DIM):
        lanes = head_lanes(head, width)
        query_head = only_head(query_ref[:, lanes[0] : lanes[1]], head) * jnp.asarray(0.125, LOW)

        def one_chunk(index, running):
            top, total, mixed = running
            first = index * chunk
            scores = chunk_scores(
                query_head, key_ref, lanes, first, chunk, head, step, kind_ref, tile_ref
            )
            values = value_ref[pl.ds(first, chunk), lanes[0] : lanes[1]]
            if key_count == chunk:
                top = jnp.max(scores, axis=1, keepdims=True)
                weights = jnp.exp(scores - top)
                total = jnp.sum(weights, axis=1, keepdims=True)
                return top, total, jnp.dot(weights.astype(LOW), values, preferred_element_type=WIDE)
            new_top = jnp.maximum(top, jnp.max(scores, axis=1, keepdims=True))
            weights = jnp.exp(scores - new_top)
            shrink = jnp.exp(top - new_top)
            total = total * shrink + jnp.sum(weights, axis=1, keepdims=True)
            mixed = mixed * shrink + jnp.dot(
                weights.astype(LOW), values, preferred_element_type=WIDE
            )
            return new_top, total, mixed

        running = (
            jnp.full((rows, 1), -1e29, WIDE),
            jnp.zeros((rows, 1), WIDE),
            jnp.zeros((rows, lanes[1] - lanes[0]), WIDE),
        )
        if key_count == chunk:
            running = one_chunk(0, running)
        else:
            running = lax.fori_loop(0, key_count // chunk, one_chunk, running)
        top, total, mixed = running
        mixed = only_head(mixed / total, head)
        logs = jnp.where(lane == head, top + jnp.log(total), logs)
        tile_out = mixed if head % 2 == 0 else tile_out + mixed
        if head % 2 == 1 or head == width // HEAD_DIM - 1:
            out_ref[:, lanes[0] : lanes[1]] = tile_out.astype(LOW)
    log_ref[...] = logs


def backward_body(
    step, kind_ref, tile_ref, query_ref, up_ref, log_ref, key_ref, value_ref, dq_ref, dk_ref, dv_ref, sums
):
    width = query_ref.shape[-1]
    key_count = key_ref.shape[0]
    chunk = math.gcd(key_count, 1024)
    rows = query_ref.shape[0]
    tile_out = None
    for head in range(width // HEAD_DIM):
        lanes = head_lanes(head, width)
        query_head = only_head(query_ref[:, lanes[0] : lanes[1]], head) * jnp.asarray(0.125, LOW)
        up_head = only_head(up_ref[:, lanes[0] : lanes[1]], head)
        log_head = log_ref[:, head : head + 1]

        def probs_of(first):
            scores = chunk_scores(
                query_head, key_ref, lanes, first, chunk, head, step, kind_ref, tile_ref
            )
            probs = jnp.exp(scores - log_head)
            values = value_ref[pl.ds(first, chunk), lanes[0] : lanes[1]]
            prob_grad = lax.dot_general(up_head, values, NT, preferred_element_type=WIDE)
            return probs, prob_grad

        def finish(first, probs, prob_grad, delta):
            score_grad = probs * (prob_grad - delta)
            if sums is not None:
                for half in range(2):
                    for pair in range(chunk // 128):
                        block = first // HEAD_DIM + 2 * pair
                        left = kind_ref[2 * step + half, block]
                        right = kind_ref[2 * step + half, block + 1]
                        piece = score_grad[
                            half * HEAD_DIM : (half + 1) * HEAD_DIM, pair * 128 : (pair + 1) * 128
                        ]
                        sums[0, head, left] += piece
                        sums[1, head, right] += piece
            score_low = score_grad.astype(LOW)
            here = pl.ds(first, chunk)
            dk_ref[here, lanes[0] : lanes[1]] += lax.dot_general(
                score_low, query_head, TN, preferred_element_type=WIDE
            )
            dv_ref[here, lanes[0] : lanes[1]] += lax.dot_general(
                probs.astype(LOW), up_head, TN, preferred_element_type=WIDE
            )
            keys = key_ref[here, lanes[0] : lanes[1]]
            return jnp.dot(score_low, keys, preferred_element_type=WIDE)

        if key_count == chunk:
            probs, prob_grad = probs_of(0)
            delta = jnp.sum(probs * prob_grad, axis=1, keepdims=True)
            query_grad = finish(0, probs, prob_grad, delta)
        else:

            def add_delta(index, delta):
                probs, prob_grad = probs_of(index * chunk)
                return delta + jnp.sum(probs * prob_grad, axis=1, keepdims=True)

            delta = lax.fori_loop(0, key_count // chunk, add_delta, jnp.zeros((rows, 1), WIDE))

            def add_grad(index, total):
                probs, prob_grad = probs_of(index * chunk)
                return total + finish(index * chunk, probs, prob_grad, delta)

            query_grad = lax.fori_loop(
                0, key_count // chunk, add_grad, jnp.zeros((rows, lanes[1] - lanes[0]), WIDE)
            )
        query_grad = only_head(query_grad * 0.125, head)
        tile_out = query_grad if head % 2 == 0 else tile_out + query_grad
        if head % 2 == 1 or head == width // HEAD_DIM - 1:
            dq_ref[:, lanes[0] : lanes[1]] = tile_out.astype(LOW)


def load_keys(own_ref, rest_ref, key_ref, value_ref):
    own, width = own_ref.shape[0], key_ref.shape[1]
    key_ref[:own] = own_ref[:, :width]
    key_ref[own:] = rest_ref[:, :width]
    value_ref[:own] = own_ref[:, width:]
    value_ref[own:] = rest_ref[:, width:]


def self_forward_kernel(first, kind_ref, tile_ref, query_ref, own_ref, rest_ref, *refs):
    outs, log_ref, out_ref, key_ref, value_ref = refs[:-4], refs[-4], refs[-3], refs[-2], refs[-1]

    @pl.when(pl.program_id(0) == 0)
    def start():
        load_keys(own_ref, rest_ref, key_ref, value_ref)

    forward_body(
        first + pl.program_id(0), kind_ref, tile_ref, query_ref, key_ref, value_ref, out_ref, log_ref
    )
    for k in range(len(outs)):

        @pl.when(pl.program_id(0) == k)
        def store():
            outs[k][...] = out_ref[...]


def self_backward_kernel(first, last, kind_ref, tile_ref, query_ref, up_ref, log_ref, own_ref, rest_ref, *refs):
    if first > 0:
        dk_start, dv_start, sums_start = refs[:3]
        refs = refs[3:]
    dq_ref, outs, (key_ref, value_ref, dk_ref, dv_ref) = refs[0], refs[1:4], refs[4:]
    sums = outs[2]

    @pl.when(pl.program_id(0) == 0)
    def start():
        load_keys(own_ref, rest_ref, key_ref, value_ref)
        if first > 0:
            dk_ref[...] = dk_start[...]
            dv_ref[...] = dv_start[...]
            sums[...] = sums_start[...]
        else:
            dk_ref[...] = jnp.zeros_like(dk_ref)
            dv_ref[...] = jnp.zeros_like(dv_ref)
            sums[...] = jnp.zeros_like(sums)

    backward_body(
        first + pl.program_id(0),
        kind_ref,
        tile_ref,
        query_ref,
        up_ref,
        log_ref,
        key_ref,
        value_ref,
        dq_ref,
        dk_ref,
        dv_ref,
        sums,
    )

    @pl.when(pl.program_id(0) == pl.num_programs(0) - 1)
    def end():
        if last:
            own, width = own_ref.shape[0], key_ref.shape[1]
            for out, here in ((outs[0], slice(0, own)), (outs[1], slice(own, None))):
                out[:, :width] = dk_ref[here].astype(LOW)
                out[:, width:] = dv_ref[here].astype(LOW)
        else:
            outs[0][...] = dk_ref[...]
            outs[1][...] = dv_ref[...]


def cross_forward_kernel(query_ref, key_ref, value_ref, out_ref, log_ref):
    forward_body(0, None, None, query_ref, key_ref, value_ref, out_ref, log_ref)


def cross_backward_kernel(
    query_ref, up_ref, log_ref, key_ref, value_ref, dq_ref, dk_out, dv_out, dk_ref, dv_ref
):
    dk_ref[...] = jnp.zeros_like(dk_ref)
    dv_ref[...] = jnp.zeros_like(dv_ref)
    backward_body(
        0, None, None, query_ref, up_ref, log_ref, key_ref, value_ref, dq_ref, dk_ref, dv_ref, None
    )
    dk_out[...] = dk_ref[...].astype(LOW)
    dv_out[...] = dv_ref[...].astype(LOW)


def whole_block(shape):
    return pl.BlockSpec(shape, lambda *index: (0,) * len(shape))


def row_block(rows, width):
    return pl.BlockSpec((rows, width), lambda i, *rest: (i, 0))


def lane_block(rows):
    return pl.BlockSpec((rows, 128), lambda i, *rest: (0, i))


def self_forward(first, last, kinds, tiles, queries, own, rest):
    width = queries.shape[1]
    rows = 2 * HEAD_DIM
    keys = own.shape[0] + rest.shape[0]
    blocks = last - first
    return pl.pallas_call(
        partial(self_forward_kernel, first),
        grid_spec=pltpu.PrefetchScalarGridSpec(
            num_scalar_prefetch=1,
            grid=(blocks,),
            in_specs=[
                whole_block(tiles.shape),
                pl.BlockSpec((rows, width), lambda i, *refs: (first + i, 0)),
                whole_block(own.shape),
                whole_block(rest.shape),
            ],
            out_specs=[whole_block((rows, width))] * blocks + [row_block(rows, 128)],
            scratch_shapes=[
                pltpu.VMEM((rows, width), LOW),
                pltpu.VMEM((keys, width), LOW),
                pltpu.VMEM((keys, width), LOW),
            ],
        ),
        out_shape=[jax.ShapeDtypeStruct((rows, width), LOW)] * blocks
        + [jax.ShapeDtypeStruct((blocks * rows, 128), WIDE)],
        compiler_params=pltpu.CompilerParams(vmem_limit_bytes=VMEM_LIMIT),
        cost_estimate=takes(2.2 * blocks),
        name="self_forward",
    )(kinds, tiles, queries, own, rest)


def self_backward(first, last, kinds, tiles, queries, up_rows, logs, own, rest, start=()):
    count, width = queries.shape
    rows = 2 * HEAD_DIM
    done = last == count // rows
    keys = own.shape[0] + rest.shape[0]
    if done:
        shapes = [jax.ShapeDtypeStruct(own.shape, LOW), jax.ShapeDtypeStruct(rest.shape, LOW)]
    else:
        shapes = [jax.ShapeDtypeStruct((keys, width), WIDE)] * 2
    shapes.append(jax.ShapeDtypeStruct(tiles.shape, WIDE))

    def rows_at(lanes):
        return pl.BlockSpec((rows, lanes), lambda i, *refs: (first + i, 0))

    return pl.pallas_call(
        partial(self_backward_kernel, first, done),
        grid_spec=pltpu.PrefetchScalarGridSpec(
            num_scalar_prefetch=1,
            grid=(last - first,),
            in_specs=[
                whole_block(tiles.shape),
                rows_at(width),
                rows_at(width),
                rows_at(128),
                whole_block(own.shape),
                whole_block(rest.shape),
            ]
            + [whole_block(array.shape) for array in start],
            out_specs=[row_block(rows, width)] + [whole_block(shape.shape) for shape in shapes],
            scratch_shapes=[pltpu.VMEM((keys, width), LOW)] * 2
            + [pltpu.VMEM((keys, width), WIDE)] * 2,
        ),
        out_shape=[jax.ShapeDtypeStruct(((last - first) * rows, width), LOW)] + shapes,
        compiler_params=pltpu.CompilerParams(vmem_limit_bytes=VMEM_LIMIT),
        cost_estimate=takes(9),
        name="self_backward",
    )(kinds, tiles, queries, up_rows, logs, own, rest, *start)


def cross_forward(queries, keys, values):
    count, width = queries.shape
    key_count = keys.shape[0]
    return pl.pallas_call(
        cross_forward_kernel,
        in_specs=vmem(3),
        out_specs=vmem(2),
        out_shape=[
            jax.ShapeDtypeStruct((count, width), LOW),
            jax.ShapeDtypeStruct((count, 128), WIDE),
        ],
        compiler_params=pltpu.CompilerParams(vmem_limit_bytes=VMEM_LIMIT),
        cost_estimate=takes(6.6),
        name="cross_forward",
    )(queries, keys, values)


def cross_backward(queries, up_rows, logs, keys, values):
    count, width = queries.shape
    key_count = keys.shape[0]
    return pl.pallas_call(
        cross_backward_kernel,
        in_specs=vmem(5),
        out_specs=vmem(3),
        scratch_shapes=[pltpu.VMEM(keys.shape, WIDE), pltpu.VMEM(keys.shape, WIDE)],
        out_shape=[
            jax.ShapeDtypeStruct((count, width), LOW),
            jax.ShapeDtypeStruct(keys.shape, LOW),
            jax.ShapeDtypeStruct(keys.shape, LOW),
        ],
        compiler_params=pltpu.CompilerParams(vmem_limit_bytes=VMEM_LIMIT),
        cost_estimate=takes(8.2),
        name="cross_backward",
    )(queries, up_rows, logs, keys, values)


def tiles_kernel(bound_ref, bias_ref, out_ref):
    shape = (HEAD_DIM, 2 * HEAD_DIM)
    lane = lax.broadcasted_iota(jnp.int32, shape, 1)
    row = lax.broadcasted_iota(jnp.int32, shape, 0)
    left = lane < HEAD_DIM
    offset = row - lane % HEAD_DIM
    for head in range(OWN_HEADS):
        far = jnp.full(shape, bias_ref[BUCKETS - 1, head], WIDE)
        tiles = [jnp.full(shape, MASKED, WIDE)]
        for apart in range(3):
            tile = tiles[0]
            for bucket in range(BUCKETS):
                reached = offset + apart * HEAD_DIM >= bound_ref[bucket]
                tile = jnp.where(reached, bias_ref[bucket, head], tile)
            tiles.append(tile)
        for kind, tile in enumerate(tiles + [far]):
            out_ref[0, head, kind] = jnp.where(left, tile, 0.0)
            out_ref[1, head, kind] = jnp.where(left, 0.0, tile)


def bias_tiles(lower_bounds, own_bias):
    shape = (2, OWN_HEADS, 5, HEAD_DIM, 2 * HEAD_DIM)
    return pl.pallas_call(
        tiles_kernel,
        out_shape=jax.ShapeDtypeStruct(shape, WIDE),
        in_specs=[pl.BlockSpec(memory_space=pltpu.SMEM)] * 2,
        out_specs=pl.BlockSpec(memory_space=pltpu.VMEM),
        cost_estimate=takes(2.7),
        name="bias_tiles",
    )(lower_bounds, own_bias)


def bucket_sums(sums, lower_bounds):
    tiles = sums[0, :, 1:, :, :HEAD_DIM] + sums[1, :, 1:, :, HEAD_DIM:]
    shape = (3, HEAD_DIM, HEAD_DIM, BUCKETS)
    distance = (
        lax.broadcasted_iota(jnp.int32, shape, 0) * HEAD_DIM
        + lax.broadcasted_iota(jnp.int32, shape, 1)
        - lax.broadcasted_iota(jnp.int32, shape, 2)
    )
    upper_bounds = jnp.concatenate([lower_bounds[1:], jnp.full((1,), 1 << 30, jnp.int32)])
    hot = ((distance >= lower_bounds) & (distance < upper_bounds)).astype(LOW)
    near = tiles[:, :3].reshape(OWN_HEADS, -1)
    high = near.astype(LOW)
    low = (near - high.astype(WIDE)).astype(LOW)
    both = jnp.dot(
        jnp.concatenate([high, low]), hot.reshape(-1, BUCKETS), preferred_element_type=WIDE
    )
    table = both[:OWN_HEADS] + both[OWN_HEADS:]
    far = jnp.sum(tiles[:, 3], axis=(1, 2))
    return table + jnp.where(jnp.arange(BUCKETS) == BUCKETS - 1, far[:, None], 0.0)


def rms_of(values):
    return lax.rsqrt(jnp.mean(values * values, axis=-1, keepdims=True) + EPSILON)


def norm_grad(values, inv_rms, gain, upstream):
    scaled = gain * upstream
    inner = jnp.mean(scaled * values, axis=-1, keepdims=True)
    return inv_rms * scaled - values * (inv_rms * inv_rms * inv_rms * inner)


def dot(left, right):
    return jnp.dot(left, right, preferred_element_type=WIDE)


def dot_nt(left, right):
    return lax.dot_general(left, right, NT, preferred_element_type=WIDE)


def dot_tn(left, right):
    return lax.dot_general(left, right, TN, preferred_element_type=WIDE)


def on_device(
    tokens,
    cotangent,
    encoder,
    expert_ids,
    block_order,
    bucket_table,
    first_gain,
    second_gain,
    third_gain,
    position_bias,
    query_weight,
    key_weight,
    value_weight,
    out_weight,
    cross_query,
    cross_key,
    cross_value,
    cross_out,
    router_weight,
    expert_in,
    expert_out,
):
    ctx_size = lax.axis_size("ctx")
    fsdp_size = lax.axis_size("fsdp")
    rests = rest_count()
    f_index = lax.axis_index("fsdp")
    ctx_index = lax.axis_index("ctx")
    core = ctx_index % 2
    group = (ctx_index // 2) % GROUP
    rest = ctx_index // (2 * GROUP)
    seq_count, span, width = tokens.shape
    shard = width // fsdp_size
    own_width = width // GROUP
    half_shard = shard // 2
    half_width = width // 2
    experts = expert_in.shape[0] * ctx_size
    capacity = (5 * seq_count * span + 4 * experts - 1) // (4 * experts)
    hidden_low = tokens.reshape(span, width)
    upstream = cotangent.reshape(span, width).astype(WIDE)

    gains = jnp.concatenate([first_gain, second_gain, third_gain]).reshape(3, shard)
    small = (gains, router_weight.T, position_bias)
    extra = small_rows(small)
    qkv_payload, early, late = pack_weights(
        small,
        (
            query_weight,
            key_weight,
            value_weight,
            out_weight,
            cross_key,
            cross_value,
            cross_query,
            cross_out,
        ),
        3,
        group,
        core,
    )
    first_hops = tie(*gather_group(hidden_low), *gather_fsdp(qkv_payload), early, late)
    own_rows = jnp.concatenate(first_hops[:GROUP])
    own_qkv, small_full = place_qkv(first_hops[GROUP : GROUP + fsdp_size], extra, f_index)
    early, late = first_hops[GROUP + fsdp_size :]
    early_x, early_y = swap_fsdp(early, 1), swap_fsdp(early, 2)
    expert_ids = after(expert_ids, qkv_payload)
    block_order, bucket_table, _ = tie(block_order, bucket_table, qkv_payload)

    gain_one = small_full[:, 0].reshape(width).astype(WIDE)
    gain_two = small_full[:, 1].reshape(width).astype(WIDE)
    gain_three = small_full[:, 2].reshape(width).astype(WIDE)
    router_full = small_full[:, 8 : 8 + experts].transpose(1, 0, 2).reshape(experts, width)
    bias_full = small_full[:, 8 + experts : 8 + experts + position_bias.shape[0], :HEADS]
    bias_full = bias_full.reshape(BUCKETS, HEADS)

    slots = jnp.arange(GROUP, dtype=jnp.int32)
    key_devices = (
        ((rest - jnp.arange(rests, dtype=jnp.int32)) % rests)[:, None, None] * (2 * GROUP)
        + (group ^ slots)[None, None, :] * 2
        + (core ^ jnp.arange(2, dtype=jnp.int32))[None, :, None]
    ).reshape(-1)
    key_blocks = (key_devices[:, None] * 2 + jnp.arange(2, dtype=jnp.int32)[None]).reshape(-1)
    block_count = block_order.shape[0]
    hits = key_blocks[:, None] == jnp.arange(block_count, dtype=jnp.int32)[None]
    key_places = jnp.sum(jnp.where(hits, block_order[None], 0), axis=1)
    query_places = key_places[: 2 * GROUP]
    kinds = jnp.clip(query_places[:, None] - key_places[None], -1, 3) + 1
    lower_bounds = jnp.sum(
        (bucket_table[:, None] < jnp.arange(BUCKETS, dtype=jnp.int32)[None]).astype(jnp.int32),
        axis=0,
    )
    own_bias = lax.dynamic_slice_in_dim(
        bias_full.astype(WIDE), group * OWN_HEADS, OWN_HEADS, 1
    )
    tiles = bias_tiles(lower_bounds, own_bias)

    routes = expert_ids.reshape(-1)
    chosen = routes[:, None] == jnp.arange(experts, dtype=jnp.int32)[None]
    order = jnp.arange(span)
    lower = (order[:, None] > order[None]).astype(LOW)
    earlier = dot(lower, chosen.astype(LOW))
    slot_rank = jnp.sum(jnp.where(chosen, earlier, 0.0), axis=1).astype(jnp.int32)
    block_rows = -(-2 * capacity // 8) * 8
    slot_rows = rests * GROUP * block_rows
    target = (
        (((routes // (2 * GROUP) - rest) % rests) * GROUP + (((routes // 2) % GROUP) ^ group))
        * block_rows
        + core * capacity
        + slot_rank
    )
    code = jnp.where(slot_rank < capacity, (routes % 2) * slot_rows + target, -1)
    own_code = jnp.broadcast_to(code.astype(WIDE)[:, None], (span, 128))
    other_code = swap_core(own_code)
    codes = jnp.concatenate([own_code[:, :1], other_code[:, :1]]).astype(jnp.int32)
    placing = (
        codes == core * slot_rows + jnp.arange(slot_rows, dtype=jnp.int32)[None]
    ).astype(LOW)
    chosen = chosen.astype(WIDE)

    wide_rows = own_rows.astype(WIDE)
    normed_own = (wide_rows * rms_of(wide_rows) * gain_one).astype(LOW)
    own_count = GROUP * span
    queries = dot(normed_own, own_qkv[:, :own_width]).astype(LOW)
    pairs_own = dot(normed_own, own_qkv[:, own_width:]).astype(LOW)
    pairs_rest = swap_core(pairs_own)
    encoder_pieces = gather_group(after(encoder, early).reshape(-1, width))
    pairs_own, pairs_rest, early_x, early_y = tie(pairs_own, pairs_rest, early_x, early_y)
    early_xy = swap_fsdp(early_x, 2)
    late_x, late_y = swap_fsdp(late, 1), swap_fsdp(late, 2)
    if rests > 1:
        near = jnp.concatenate([pairs_own, pairs_rest])
        pairs_rest = jnp.concatenate(
            [pairs_rest] + [shift_rest(near, r) for r in range(1, rests)]
        )
    half_group = GROUP // 2
    *far, far_logs = self_forward(
        half_group, GROUP, kinds, tiles, queries, pairs_own, pairs_rest
    )
    pairs_own, *far = tie(pairs_own, *far)
    far = [swap_group(piece, half_group + k) for k, piece in enumerate(far)]
    *attended, near_logs = self_forward(
        0, half_group, kinds, tiles, queries, pairs_own, pairs_rest
    )
    attended, far, early_xy, late_x, encoder_pieces = tie(
        attended, far, early_xy, late_x, encoder_pieces
    )
    self_logs = jnp.concatenate([near_logs, far_logs])
    attended = [attended[0]] + [swap_group(attended[k], k) for k in range(1, half_group)] + far
    late_xy = swap_fsdp(late_x, 2)
    early_mine = stack_pieces((early, early_x, early_y, early_xy), 1, f_index, group)
    early_theirs = swap_core(early_mine)
    encoder_own = jnp.concatenate(encoder_pieces)
    encoder_other = swap_core(encoder_own)
    *attended, early_theirs, encoder_other = tie(*attended, early_theirs, encoder_other)
    out_full, cross_k_full, cross_v_full = weave_halves(early_mine, early_theirs, core)
    encoder_all = jnp.concatenate([encoder_own, encoder_other])
    if rests > 1:
        encoder_all = jnp.concatenate(
            [encoder_all] + [shift_rest(encoder_all, r) for r in range(1, rests)]
        )
    attended = jnp.concatenate(attended, axis=1)
    hidden = hidden_low.astype(WIDE)
    first_sum = hidden + dot(attended, out_full)
    inv_two = rms_of(first_sum)
    normed_two = (first_sum * inv_two * gain_two).astype(LOW)
    normed_two, late_xy, late_y = tie(normed_two, late_xy, late_y)
    late_mine = stack_pieces((late, late_x, late_y, late_xy), 0, f_index, group)
    late_theirs = swap_core(late_mine)

    cross_keys = dot(after(encoder_all, late_mine), cross_k_full).astype(LOW)
    cross_values = dot(encoder_all, cross_v_full).astype(LOW)
    cross_q_full, cross_o_full = weave_halves(late_mine, late_theirs, core)
    cross_rows = dot(normed_two, cross_q_full).astype(LOW)
    cross_mixed, cross_logs = cross_forward(cross_rows, cross_keys, cross_values)
    second_sum = first_sum + dot(cross_mixed, cross_o_full)
    inv_three = rms_of(second_sum)
    normed_three = (second_sum * inv_three * gain_three).astype(LOW)

    logits = dot_nt(normed_three, router_full)
    router_probs = jax.nn.softmax(logits, axis=-1)
    gate_value = jnp.sum(router_probs * chosen, axis=-1, keepdims=True)
    scaled_up = (gate_value * upstream).astype(LOW)

    sides = jnp.concatenate([normed_three, scaled_up], axis=1)
    sides = jnp.concatenate([sides, swap_core(sides)])
    sent = dot_tn(placing, sides).astype(LOW).reshape(rests, GROUP * block_rows, 2 * width)
    near = jnp.concatenate(
        [sent[0]] + [shift_rest(sent[r], r) for r in range(1, rests)]
    ).reshape(rests, GROUP, block_rows, 2 * width)
    arrived = jnp.concatenate(
        [near[:, 0]] + [swap_group(near[:, k], k) for k in range(1, GROUP)], axis=1
    ).reshape(slot_rows, 2 * width)
    arrivals = list(gather_fsdp(arrived))
    near_count = fsdp_size // 2
    answers, middle = run_experts(arrivals[:near_count], expert_in[0], expert_out[0])
    answers, middle, arrivals[near_count:] = tie(answers, middle, arrivals[near_count:])
    more_answers, more_middle = run_experts(arrivals[near_count:], expert_in[0], expert_out[0])
    answers = answers + more_answers
    answers = tie(answers[0], *[swap_fsdp(answers[k], k) for k in range(1, fsdp_size)])
    answers = sum_home(answers, rests)
    near = [answers[0]] + [swap_group(answers[k], k) for k in range(1, GROUP)]
    near = jnp.concatenate(
        [piece.reshape(rests, block_rows, 2 * width) for piece in near], axis=1
    )
    home = jnp.concatenate([near[0]] + [shift_rest(near[r], -r) for r in range(1, rests)])
    both = dot(placing, home).astype(LOW)
    both = both[:span].astype(WIDE) + swap_core(both[span:]).astype(WIDE)
    moe_rows, dispatch_grad = both[:, :width], both[:, width:]
    grad_expert_in, grad_expert_out = expert_grads(arrivals, (middle, more_middle))
    grad_expert_in, grad_expert_out = grad_expert_in[None], grad_expert_out[None]

    mixed_out = (second_sum + gate_value * moe_rows).astype(LOW).reshape(tokens.shape)
    gate_grad = jnp.sum(upstream * moe_rows, axis=-1, keepdims=True)
    logit_low = (gate_grad * gate_value * (chosen - router_probs)).astype(LOW)
    three_grad = dispatch_grad + dot(logit_low, router_full)
    second_grad = upstream + norm_grad(second_sum, inv_three, gain_three, three_grad)
    gain_three_part = jnp.sum(three_grad * second_sum * inv_three, axis=0, keepdims=True)
    router_part = dot_tn(logit_low, normed_three)
    spread = jnp.concatenate([router_part, gain_three_part])
    spread = jnp.pad(spread, ((0, -spread.shape[0] % 16), (0, 0)))

    branch_two = second_grad.astype(LOW)
    cross_up = dot_nt(branch_two, cross_o_full).astype(LOW)
    cross_q_low, cross_k_part, cross_v_part = cross_backward(
        cross_rows, cross_up, cross_logs, cross_keys, cross_values
    )
    two_grad = dot_nt(cross_q_low, cross_q_full)
    first_grad = second_grad + norm_grad(first_sum, inv_two, gain_two, two_grad)

    branch_one = first_grad.astype(LOW)
    self_up = dot_nt(branch_one, out_full).astype(LOW)
    branch_one, self_up = tie(branch_one, self_up)
    up_pieces = [self_up[:, :own_width]] + [
        swap_group(self_up[:, k * own_width : (k + 1) * own_width], k) for k in range(1, GROUP)
    ]
    extra_rows = -(-spread.shape[0] // 64) * 64
    keep, send = weight_grads(
        (False, False, False, False, True),
        (
            (cross_mixed, branch_two),
            (normed_two, cross_q_low),
            (encoder_all, cross_k_part),
            (encoder_all, cross_v_part),
            (attended, branch_one),
        ),
        spread,
        extra_rows,
        f_index,
        core,
        group,
        fsdp_size,
    )
    *up_pieces, received = tie(*up_pieces, swap_core(send))
    up_own = jnp.concatenate(up_pieces)
    middle = keep.shape[1] // 2
    top = [add_low(keep[k, :middle], received[k, :middle]) for k in range(fsdp_size)]
    up_own, top[1:] = tie(up_own, top[1:])
    top = [top[0]] + [swap_fsdp(top[k], k) for k in range(1, fsdp_size)]
    query_low, pair_own, pair_rest, bias_parts = self_backward(
        0, own_count // span, kinds, tiles, queries, up_own, self_logs, pairs_own, pairs_rest
    )
    query_low, pair_own, pair_rest, bias_parts, top, keep, received = tie(
        query_low, pair_own, pair_rest, bias_parts, top, keep, received
    )
    bottom = [add_low(keep[k, middle:], received[k, middle:]) for k in range(fsdp_size)]
    bottom = [bottom[0]] + [swap_fsdp(bottom[k], k) for k in range(1, fsdp_size)]
    if rests > 1:
        near = jnp.concatenate([pair_own, pair_rest[:own_count]]).astype(WIDE)
        for r in range(1, rests):
            first = (2 * r - 1) * own_count
            piece = pair_rest[first : first + 2 * own_count]
            near = near + shift_rest(piece, -r).astype(WIDE)
        pair_own, pair_rest = near[:own_count].astype(LOW), near[own_count:].astype(LOW)
    one_parts, qkv_keep, qkv_send = key_grads(
        normed_own, query_low, pair_own, swap_core(pair_rest), own_qkv, f_index, core, fsdp_size
    )
    one_parts = [one_parts[0]] + [swap_group(one_parts[k], k) for k in range(1, GROUP)]
    qkv_send, bottom, bias_parts, one_parts[1] = tie(
        swap_core(qkv_send), bottom, bias_parts, one_parts[1]
    )
    qkv_send, *quarters = tie(qkv_send, *sum_quarters(top, bottom, group))
    quarters = [quarters[0]] + [swap_group(quarters[k], k) for k in range(1, GROUP)]

    table = jnp.pad(bucket_sums(bias_parts, lower_bounds).T, ((0, 0), (0, 128 - OWN_HEADS)))
    qkv_parts = add_qkv(qkv_keep, qkv_send, table, f_index)
    qkv_parts = [qkv_parts[0]] + [swap_fsdp(qkv_parts[k], k) for k in range(1, fsdp_size)]
    qkv_parts, one_parts, quarters, grad_expert_in, grad_expert_out = tie(
        qkv_parts, one_parts, quarters, grad_expert_in, grad_expert_out
    )
    dense_shard = sum_rest(sum_low(quarters[0], quarters[1:])).astype(LOW)
    one_grad = sum(one.astype(WIDE) for one in one_parts)
    tokens_grad = first_grad + norm_grad(hidden, rms_of(hidden), gain_one, one_grad)
    tokens_grad = tokens_grad.reshape(tokens.shape)
    qkv_shard = sum_rest(sum_low(qkv_parts[0], qkv_parts[1:])).astype(LOW)
    spots = [group ^ k for k in range(GROUP)]
    qkv_mine = collect(gather_group(qkv_shard), spots)
    query_total, key_total, value_total, bias_total, grad_gain_one = finish_qkv(
        qkv_mine,
        swap_core(qkv_mine),
        (query_weight, key_weight, value_weight),
        first_gain,
        core,
        position_bias.shape,
    )
    dense_pieces, query_total, tokens_grad = tie(
        gather_group(dense_shard), query_total, tokens_grad
    )
    (
        cross_o_total,
        cross_q_total,
        cross_k_total,
        cross_v_total,
        out_total,
        grad_router,
        grad_gain_three,
        grad_gain_two,
    ) = finish_weights(
        dense_pieces,
        [swap_core(piece) for piece in dense_pieces],
        cross_query,
        second_gain,
        group,
        core,
        experts,
    )

    return (
        mixed_out,
        tokens_grad,
        grad_gain_one,
        grad_gain_two,
        grad_gain_three,
        bias_total,
        query_total,
        key_total,
        value_total,
        out_total,
        cross_q_total,
        cross_k_total,
        cross_v_total,
        cross_o_total,
        grad_router,
        grad_expert_in,
        grad_expert_out,
    )


def solution(mesh):
    rows = P("fsdp", "ctx", None)
    vector = P("fsdp")
    matrix = P("fsdp", None)
    expert_specs = (P("ctx", None, "fsdp"), P("ctx", "fsdp", None))
    return jax.shard_map(
        on_device,
        mesh=mesh,
        in_specs=(rows,) * 4 + (P(),) * 2 + (vector,) * 3 + (matrix,) * 10 + expert_specs,
        out_specs=(rows,) * 2 + (vector,) * 3 + (matrix,) * 10 + expert_specs,
        check_vma=False,
    )
```

```python
import math
from functools import partial

import jax
import jax.numpy as jnp
from jax import lax
from jax.experimental import pallas as pl
from jax.experimental.pallas import tpu as pltpu
from jax.sharding import PartitionSpec as P

HEADS = 12
HEAD_DIM = 64
BUCKETS = 32
GROUP = 4
OWN_HEADS = HEADS // GROUP
EPSILON = 1e-06
MASKED = -1e30
LOW = jnp.bfloat16
WIDE = jnp.float32
VMEM_LIMIT = 56 * 1024 * 1024
NT = (((1,), (1,)), ((), ()))
TN = (((0,), (0,)), ((), ()))


def swap_fsdp(rows, k):
    size = lax.axis_size("fsdp")
    return lax.ppermute(rows, "fsdp", [(i, i ^ k) for i in range(size)])


def swap_core(rows):
    size = lax.axis_size("ctx")
    return lax.ppermute(rows, "ctx", [(i, i ^ 1) for i in range(size)])


def swap_group(rows, k):
    size = lax.axis_size("ctx")
    return lax.ppermute(rows, "ctx", [(i, i ^ (2 * k)) for i in range(size)])


def shift_rest(rows, r):
    size = lax.axis_size("ctx")
    step = 2 * GROUP * r
    return lax.ppermute(rows, "ctx", [(i, (i + step) % size) for i in range(size)])


def rest_count():
    return lax.axis_size("ctx") // (2 * GROUP)


def block_at(blocks, index):
    return lax.dynamic_index_in_dim(blocks, index, 0, keepdims=False)


def in_order(parts, index):
    parts = list(parts)
    bit = 1
    while bit < len(parts):
        flag = (index & bit) != 0
        parts = [jnp.where(flag, parts[i ^ bit], parts[i]) for i in range(len(parts))]
        bit *= 2
    return parts


def tie(*values):
    return lax.optimization_barrier(values)


def after(value, *earlier):
    return tie(value, *earlier)[0]


def gather_group(rows):
    return [rows] + [swap_group(rows, k) for k in range(1, GROUP)]


def gather_fsdp(rows):
    return [rows] + [swap_fsdp(rows, k) for k in range(1, lax.axis_size("fsdp"))]


def sum_rest(values):
    size = lax.axis_size("ctx")
    if rest_count() == 1:
        return values
    near = 2 * GROUP
    groups = [list(range(i, size, near)) for i in range(near)]
    return lax.psum(values, "ctx", axis_index_groups=groups)


def takes(us):
    return pl.CostEstimate(flops=int(us * 1e9), bytes_accessed=int(us * 3.5e6), transcendentals=0)


def vmem(count):
    return [pl.BlockSpec(memory_space=pltpu.VMEM)] * count


def smem():
    return pl.BlockSpec(memory_space=pltpu.SMEM)


def small_rows(small):
    return -(-(8 + small[1].shape[0] + small[2].shape[0]) // 16) * 16


def pack_kernel(index_ref, gain_ref, router_ref, bias_ref, *refs):
    group, core = index_ref[0], index_ref[1]
    ins, (qkv_ref, early_ref, late_ref) = refs[:-3], refs[-3:]
    rows = early_ref.shape[1]
    own = qkv_ref.shape[1] // 3
    shard = 2 * rows
    for choice in range(GROUP):

        @pl.when(group == choice)
        def take():
            for which in range(3):
                qkv_ref[:shard, which * own : (which + 1) * own] = ins[which][
                    :, choice * own : (choice + 1) * own
                ]

    def widened(rows, count):
        rows = rows.astype(WIDE)
        if rows.shape[1] < shard:
            spare = jnp.zeros((rows.shape[0], shard - rows.shape[1]), WIDE)
            rows = jnp.concatenate([rows, spare], axis=1)
        if rows.shape[0] < count:
            rows = jnp.concatenate([rows, jnp.zeros((count - rows.shape[0], shard), WIDE)])
        return rows

    experts = router_ref.shape[0]
    extra = qkv_ref.shape[0] - shard
    small = jnp.concatenate(
        [
            widened(gain_ref[...], 8),
            router_ref[...].astype(WIDE),
            widened(bias_ref[...], extra - 8 - experts),
        ]
    )
    qkv_ref[shard:] = jnp.zeros((extra, 3 * own), LOW)
    qkv_ref[shard:, :shard] = small.astype(LOW)
    here = pl.ds(pl.multiple_of(core * rows, 16), rows)
    early = early_ref.shape[0]
    for i in range(early):
        early_ref[i] = ins[3 + i][here]
    for i in range(late_ref.shape[0]):
        late_ref[i] = ins[3 + early + i][here]


def pack_weights(small, weights, early, group, core):
    shard, width = weights[0].shape
    own = width // GROUP
    late = len(weights) - 3 - early
    return pl.pallas_call(
        pack_kernel,
        out_shape=[
            jax.ShapeDtypeStruct((shard + small_rows(small), 3 * own), LOW),
            jax.ShapeDtypeStruct((early, shard // 2, width), LOW),
            jax.ShapeDtypeStruct((late, shard // 2, width), LOW),
        ],
        in_specs=[smem()] + vmem(3 + len(weights)),
        out_specs=vmem(3),
        compiler_params=pltpu.CompilerParams(vmem_limit_bytes=VMEM_LIMIT),
        cost_estimate=takes(3),
        name="pack_weights",
    )(jnp.stack([group, core]).astype(jnp.int32), *small, *weights)


def place_qkv_kernel(index_ref, *refs):
    pieces, (out, small) = refs[:-2], refs[-2:]
    rows = out.shape[1]
    for k in range(len(pieces)):
        out[index_ref[k]] = pieces[k][:rows]
        small[index_ref[k]] = pieces[k][rows:, :rows]


def place_qkv(pieces, extra, f_index):
    count = len(pieces)
    rows, width = pieces[0].shape
    rows = rows - extra
    whole, small = pl.pallas_call(
        place_qkv_kernel,
        out_shape=[
            jax.ShapeDtypeStruct((count, rows, width), LOW),
            jax.ShapeDtypeStruct((count, extra, rows), LOW),
        ],
        in_specs=[smem()] + vmem(count),
        out_specs=vmem(2),
        compiler_params=pltpu.CompilerParams(vmem_limit_bytes=VMEM_LIMIT),
        cost_estimate=takes(2.3),
        name="place_qkv",
    )(jnp.stack([f_index ^ k for k in range(count)]).astype(jnp.int32), *pieces)
    return whole.reshape(count * rows, width), small


def stack_kernel(turned, index_ref, *refs):
    count = len(refs) - 1
    out = refs[-1]
    for item in range(out.shape[0]):
        for k in range(count):
            spot = index_ref[count + k] if item < turned else index_ref[k]
            out[item, spot] = refs[k][item]


def stack_pieces(pieces, turned, f_index, g_index):
    count = len(pieces)
    spots = [f_index ^ k for k in range(count)]
    indices = jnp.stack(spots + [g_index ^ spot for spot in spots]).astype(jnp.int32)
    number, rows, width = pieces[0].shape
    return pl.pallas_call(
        partial(stack_kernel, turned),
        out_shape=jax.ShapeDtypeStruct((number, count, rows, width), LOW),
        in_specs=[smem()] + vmem(count),
        out_specs=vmem(1)[0],
        compiler_params=pltpu.CompilerParams(vmem_limit_bytes=VMEM_LIMIT),
        cost_estimate=takes(2.7),
        name="stack_pieces",
    )(indices, *pieces)


def weave_kernel(index_ref, mine_ref, theirs_ref, *outs):
    core = index_ref[0]
    for item, out in enumerate(outs):
        for block in range(out.shape[0]):
            out[block, core] = mine_ref[item, block]
            out[block, 1 - core] = theirs_ref[item, block]


def weave_halves(mine, theirs, core):
    number, count, rows, width = mine.shape
    whole = pl.pallas_call(
        weave_kernel,
        out_shape=[jax.ShapeDtypeStruct((count, 2, rows, width), LOW)] * number,
        in_specs=[smem()] + vmem(2),
        out_specs=vmem(number),
        compiler_params=pltpu.CompilerParams(vmem_limit_bytes=VMEM_LIMIT),
        cost_estimate=takes(4),
        name="weave_halves",
    )(core.reshape(1).astype(jnp.int32), mine, theirs)
    return [one.reshape(count * 2 * rows, width) for one in whole]


def expert_kernel(*refs):
    count = (len(refs) - 3) // 2
    pieces, in_ref, out_ref = refs[:count], refs[count], refs[count + 1]
    answers, middle = refs[count + 2 : 2 * count + 2], refs[-1]
    rows, width = pieces[0].shape[0], pieces[0].shape[1] // 2
    hidden = in_ref.shape[1]
    scale = math.sqrt(2 / math.pi)
    for k in range(count):
        inner = dot(pieces[k][:, :width], in_ref[...])
        square = inner * inner
        bent = jnp.tanh(scale * (inner + 0.044715 * (inner * square)))
        activated = (0.5 * inner * (1.0 + bent)).astype(LOW)
        slope = 0.5 * (1.0 + bent) + 0.5 * inner * (1.0 - bent * bent) * (
            scale * (1.0 + 3 * 0.044715 * square)
        )
        inner_low = (dot_nt(pieces[k][:, width:], out_ref[...]) * slope).astype(LOW)
        answers[k][:, :width] = dot(activated, out_ref[...]).astype(LOW)
        answers[k][:, width:] = dot_nt(inner_low, in_ref[...]).astype(LOW)
        here = slice(k * rows, (k + 1) * rows)
        middle[here, :hidden] = activated
        middle[here, hidden:] = inner_low


def run_experts(pieces, expert_in, expert_out):
    count = len(pieces)
    width, hidden = expert_in.shape
    rows = pieces[0].shape[0]
    results = pl.pallas_call(
        expert_kernel,
        out_shape=[jax.ShapeDtypeStruct((rows, 2 * width), LOW)] * count
        + [jax.ShapeDtypeStruct((count * rows, 2 * hidden), LOW)],
        in_specs=vmem(count + 2),
        out_specs=vmem(count + 1),
        compiler_params=pltpu.CompilerParams(vmem_limit_bytes=VMEM_LIMIT),
        cost_estimate=takes(4.1),
        name="experts",
    )(*pieces, expert_in, expert_out)
    return list(results[:count]), results[count]


def expert_grads_kernel(count, *refs):
    pieces, middles, (in_ref, out_ref) = refs[:count], refs[count:-2], refs[-2:]
    width, hidden = in_ref.shape
    rows = jnp.concatenate([piece[...] for piece in pieces])
    middle = jnp.concatenate([one[...] for one in middles])
    in_ref[...] = dot_tn(rows[:, :width], middle[:, hidden:])
    out_ref[...] = dot_tn(middle[:, :hidden], rows[:, width:])


def expert_grads(pieces, middles):
    width = pieces[0].shape[1] // 2
    hidden = middles[0].shape[1] // 2
    return pl.pallas_call(
        partial(expert_grads_kernel, len(pieces)),
        out_shape=[
            jax.ShapeDtypeStruct((width, hidden), WIDE),
            jax.ShapeDtypeStruct((hidden, width), WIDE),
        ],
        in_specs=vmem(len(pieces) + len(middles)),
        out_specs=vmem(2),
        compiler_params=pltpu.CompilerParams(vmem_limit_bytes=VMEM_LIMIT),
        cost_estimate=takes(5.7),
        name="expert_grads",
    )(*pieces, *middles)


def home_kernel(rests, *refs):
    pieces, outs = refs[: len(refs) - GROUP], refs[len(refs) - GROUP :]
    block = outs[0].shape[0] // rests
    total = pieces[0][...].astype(WIDE)
    for piece in pieces[1:]:
        total = total + piece[...].astype(WIDE)
    for k, out in enumerate(outs):
        rows = [
            total[(r * GROUP + k) * block : (r * GROUP + k + 1) * block] for r in range(rests)
        ]
        out[...] = (rows[0] if rests == 1 else jnp.concatenate(rows)).astype(LOW)


def sum_home(pieces, rests):
    rows, width = pieces[0].shape
    return pl.pallas_call(
        partial(home_kernel, rests),
        out_shape=[jax.ShapeDtypeStruct((rows // GROUP, width), LOW)] * GROUP,
        in_specs=vmem(len(pieces)),
        out_specs=vmem(GROUP),
        compiler_params=pltpu.CompilerParams(vmem_limit_bytes=VMEM_LIMIT),
        cost_estimate=takes(2.4),
        name="sum_home",
    )(*pieces)


def grads_kernel(turns, extra_rows, index_ref, *refs):
    f_index, core, turn = index_ref[0], index_ref[1], index_ref[2]
    ins, spread_ref, keep, send = refs[: 2 * len(turns)], refs[-3], refs[-2], refs[-1]
    size, _, half = keep.shape
    shard = ins[0].shape[1] // size
    for item, turned in enumerate(turns):
        rows_ref, grad_ref = ins[2 * item], ins[2 * item + 1]
        for out, side in ((keep, core), (send, 1 - core)):
            grad = grad_ref[:, pl.ds(pl.multiple_of(side * half, 128), half)]
            product = dot_tn(rows_ref[...], grad).astype(LOW)
            for block in range(size):
                spot = block ^ f_index ^ (turn if turned else 0)
                out[spot, item * shard : (item + 1) * shard] = product[
                    block * shard : (block + 1) * shard
                ]
    first = len(turns) * shard
    for block in range(size):
        spot = block ^ f_index
        piece = spread_ref[:, block * shard : (block + 1) * shard].astype(LOW)
        keep[spot, first:] = jnp.zeros((extra_rows, half), LOW)
        send[spot, first:] = jnp.zeros((extra_rows, half), LOW)
        keep[spot, first : first + spread_ref.shape[0], :shard] = piece


def weight_grads(turns, pairs, spread, extra_rows, f_index, core, turn, size):
    width = pairs[0][0].shape[1]
    rows = len(turns) * (width // size) + extra_rows
    shape = jax.ShapeDtypeStruct((size, rows, width // 2), LOW)
    flat = [array for pair in pairs for array in pair] + [spread]
    return pl.pallas_call(
        partial(grads_kernel, turns, extra_rows),
        out_shape=[shape, shape],
        in_specs=[smem()] + vmem(len(flat)),
        out_specs=vmem(2),
        compiler_params=pltpu.CompilerParams(vmem_limit_bytes=VMEM_LIMIT),
        cost_estimate=takes(7.5),
        name="weight_grads",
    )(jnp.stack([f_index, core, turn]).astype(jnp.int32), *flat)


def add_low(left, right):
    return (left.astype(WIDE) + right.astype(WIDE)).astype(LOW)


def sum_low(first, others):
    total = first.astype(WIDE)
    for other in others:
        total = total + other.astype(WIDE)
    return total.astype(LOW)


def quarter_kernel(index_ref, *refs):
    outs = refs[len(refs) - GROUP :]
    count = (len(refs) - GROUP) // 2
    rows = outs[0].shape[0] // 2
    for k, out in enumerate(outs):
        here = pl.ds(pl.multiple_of(index_ref[k] * rows, 16), rows)
        for half in range(2):
            pieces = refs[half * count : (half + 1) * count]
            out[half * rows : (half + 1) * rows] = sum_low(
                pieces[0][here], [piece[here] for piece in pieces[1:]]
            )


def sum_quarters(top, bottom, group):
    rows, width = top[0].shape
    pieces = list(top) + list(bottom)
    return pl.pallas_call(
        quarter_kernel,
        out_shape=[jax.ShapeDtypeStruct((2 * rows // GROUP, width), LOW)] * GROUP,
        in_specs=[smem()] + vmem(len(pieces)),
        out_specs=vmem(GROUP),
        compiler_params=pltpu.CompilerParams(vmem_limit_bytes=VMEM_LIMIT),
        cost_estimate=takes(3),
        name="sum_quarters",
    )(jnp.stack([group ^ k for k in range(GROUP)]).astype(jnp.int32), *pieces)


def collect_kernel(index_ref, *refs):
    pieces, out = refs[:-1], refs[-1]
    for k in range(len(pieces)):
        out[index_ref[k]] = pieces[k][...]


def collect(pieces, spots):
    return pl.pallas_call(
        collect_kernel,
        out_shape=jax.ShapeDtypeStruct((GROUP,) + pieces[0].shape, LOW),
        in_specs=[smem()] + vmem(GROUP),
        out_specs=vmem(1)[0],
        cost_estimate=takes(2),
        name="collect",
    )(jnp.stack(spots).astype(jnp.int32), *pieces)


def row_sums(values):
    ones = jnp.ones((8, values.shape[1]), WIDE)
    sums = lax.dot_general(
        ones, values, NT, precision=lax.Precision.HIGHEST, preferred_element_type=WIDE
    )
    return sums[:1]


def finish_kernel(index_ref, *refs):
    mine_pieces, their_pieces = refs[:GROUP], refs[GROUP : 2 * GROUP]
    weight_ref, gain_ref, *outs, mine_ref, theirs_ref = refs[2 * GROUP :]
    core = index_ref[GROUP]
    quarter = mine_pieces[0].shape[0] // 2
    for out, pieces in ((mine_ref, mine_pieces), (theirs_ref, their_pieces)):
        for k in range(GROUP):
            for part in range(2):
                first = (part * GROUP + index_ref[k]) * quarter
                out[pl.ds(pl.multiple_of(first, 16), quarter)] = pieces[k][
                    part * quarter : (part + 1) * quarter
                ]
    half = mine_ref.shape[1]
    shard = outs[0].shape[0]
    wholes, (router_ref, third_ref, second_ref) = outs[:-3], outs[-3:]
    for number, out in enumerate(wholes):
        here = slice(number * shard, (number + 1) * shard)
        out[:, pl.ds(pl.multiple_of(core * half, 128), half)] = mine_ref[here].astype(WIDE)
        out[:, pl.ds(pl.multiple_of((1 - core) * half, 128), half)] = theirs_ref[here].astype(WIDE)
    second_ref[...] = row_sums(weight_ref[...].astype(WIDE) * wholes[1][...]) / gain_ref[
        ...
    ].astype(WIDE)
    here = slice(len(wholes) * shard, None)
    spread = mine_ref[here].astype(WIDE) + theirs_ref[here].astype(WIDE)
    experts = router_ref.shape[0]
    router_ref[...] = spread[:experts, :shard]
    third_ref[...] = spread[experts : experts + 1, :shard]


def finish_weights(mine, theirs, weight, gain, group, core, experts):
    shard, width = weight.shape
    rows, half = mine[0].shape
    shapes = [(shard, width)] * 5 + [(experts, shard)] + [(1, shard)] * 2
    results = pl.pallas_call(
        finish_kernel,
        out_shape=[jax.ShapeDtypeStruct(shape, WIDE) for shape in shapes],
        in_specs=[smem()] + vmem(2 * GROUP + 2),
        out_specs=vmem(len(shapes)),
        scratch_shapes=[pltpu.VMEM((GROUP * rows, half), LOW)] * 2,
        compiler_params=pltpu.CompilerParams(vmem_limit_bytes=VMEM_LIMIT),
        cost_estimate=takes(3),
        name="finish_weights",
    )(
        jnp.stack([group ^ k for k in range(GROUP)] + [core]).astype(jnp.int32),
        *mine,
        *theirs,
        weight,
        gain[None],
    )
    return list(results[:5]) + [results[5].T] + [one[0] for one in results[6:]]


def key_grads_kernel(index_ref, rows_ref, query_ref, own_ref, rest_ref, weight_ref, *outs):
    f_index, core = index_ref[0], index_ref[1]
    ones, (keep, send) = outs[:-2], outs[-2:]
    grads = jnp.concatenate([query_ref[...], add_low(own_ref[...], rest_ref[...])], axis=1)
    count = grads.shape[0] // len(ones)
    for k, one in enumerate(ones):
        one[...] = dot_nt(grads[k * count : (k + 1) * count], weight_ref[...]).astype(LOW)
    size, rows, _ = keep.shape
    product = dot_tn(rows_ref[...], grads)
    for block in range(size):
        spot = block ^ f_index
        top = product[2 * block * rows : (2 * block + 1) * rows].astype(LOW)
        bottom = product[(2 * block + 1) * rows : (2 * block + 2) * rows].astype(LOW)
        keep[spot] = jnp.where(core == 0, top, bottom)
        send[spot] = jnp.where(core == 0, bottom, top)


def key_grads(rows, query, own, rest, weight, f_index, core, size):
    count, width = rows.shape
    shape = jax.ShapeDtypeStruct((size, width // size // 2, weight.shape[1]), LOW)
    results = pl.pallas_call(
        key_grads_kernel,
        out_shape=[jax.ShapeDtypeStruct((count // GROUP, width), LOW)] * GROUP + [shape] * 2,
        in_specs=[smem()] + vmem(5),
        out_specs=vmem(GROUP + 2),
        compiler_params=pltpu.CompilerParams(vmem_limit_bytes=VMEM_LIMIT),
        cost_estimate=takes(0.1),
        name="key_grads",
    )(jnp.stack([f_index, core]).astype(jnp.int32), rows, query, own, rest, weight)
    return list(results[:GROUP]), results[GROUP], results[GROUP + 1]


def add_qkv_kernel(index_ref, keep_ref, received_ref, table_ref, *outs):
    rows = keep_ref.shape[1]
    buckets = table_ref.shape[0] // len(outs)
    for k, out in enumerate(outs):
        out[:rows] = add_low(keep_ref[k], received_ref[k])
        here = pl.ds(pl.multiple_of((index_ref[0] ^ k) * buckets, 8), buckets)
        table = table_ref[here]
        spare = out.shape[1] - table.shape[1]
        table = jnp.concatenate([table, jnp.zeros((buckets, spare), WIDE)], axis=1)
        below = jnp.zeros((out.shape[0] - rows - buckets, out.shape[1]), WIDE)
        out[rows:] = jnp.concatenate([table, below]).astype(LOW)


def add_qkv(keep, received, table, f_index):
    size, rows, width = keep.shape
    return list(
        pl.pallas_call(
            add_qkv_kernel,
            out_shape=[jax.ShapeDtypeStruct((rows + 16, width), LOW)] * size,
            in_specs=[smem()] + vmem(3),
            out_specs=vmem(size),
            compiler_params=pltpu.CompilerParams(vmem_limit_bytes=VMEM_LIMIT),
            cost_estimate=takes(2),
            name="add_qkv",
        )(f_index.reshape(1).astype(jnp.int32), keep, received, table)
    )


def qkv_finish_kernel(index_ref, mine_ref, theirs_ref, *refs):
    core = index_ref[0]
    weights, gain_ref, outs, bias_ref, gain_out = refs[:3], refs[3], refs[4:7], refs[7], refs[8]
    own = mine_ref.shape[2] // 3
    rows = outs[0].shape[0] // 2
    product = None
    for which in range(3):
        for source, side in ((mine_ref, core), (theirs_ref, 1 - core)):
            whole = jnp.concatenate(
                [
                    source[g, :rows, which * own : (which + 1) * own].astype(WIDE)
                    for g in range(GROUP)
                ],
                axis=1,
            )
            outs[which][pl.ds(pl.multiple_of(side * rows, 8), rows)] = whole
        one = weights[which][...].astype(WIDE) * outs[which][...]
        product = one if product is None else product + one
    gain_out[...] = row_sums(product) / gain_ref[...].astype(WIDE)
    buckets = bias_ref.shape[0]
    for g in range(GROUP):
        table = mine_ref[g, rows:, :128].astype(WIDE) + theirs_ref[g, rows:, :128].astype(WIDE)
        bias_ref[:, g * OWN_HEADS : (g + 1) * OWN_HEADS] = table[:buckets, :OWN_HEADS]


def finish_qkv(mine, theirs, weights, gain, core, bias_shape):
    shard, width = weights[0].shape
    shapes = [(shard, width)] * 3 + [bias_shape, (1, shard)]
    results = pl.pallas_call(
        qkv_finish_kernel,
        out_shape=[jax.ShapeDtypeStruct(shape, WIDE) for shape in shapes],
        in_specs=[smem()] + vmem(6),
        out_specs=vmem(len(shapes)),
        compiler_params=pltpu.CompilerParams(vmem_limit_bytes=VMEM_LIMIT),
        cost_estimate=takes(2.6),
        name="qkv_finish",
    )(core.reshape(1).astype(jnp.int32), mine, theirs, *weights, gain[None])
    return list(results[:4]) + [results[4][0]]


def head_lanes(head, width):
    first = head // 2 * 128
    return first, min(first + 128, width)


def only_head(rows, head):
    if rows.shape[-1] == HEAD_DIM:
        return rows
    lane = lax.broadcasted_iota(jnp.int32, rows.shape, rows.ndim - 1)
    return jnp.where(lane // HEAD_DIM == head % 2, rows, jnp.zeros_like(rows))


def bias_block(kind_ref, tile_ref, head, step, first_block, width):
    rows = []
    for half in range(2):
        columns = []
        for pair in range(width // 128):
            left = kind_ref[2 * step + half, first_block + 2 * pair]
            right = kind_ref[2 * step + half, first_block + 2 * pair + 1]
            columns.append(tile_ref[0, head, left] + tile_ref[1, head, right])
        rows.append(jnp.concatenate(columns, axis=1))
    return jnp.concatenate(rows, axis=0)


def chunk_scores(query_head, key_ref, lanes, first, width, head, step, kind_ref, tile_ref):
    keys = key_ref[pl.ds(first, width), lanes[0] : lanes[1]]
    scores = lax.dot_general(query_head, keys, NT, preferred_element_type=WIDE)
    if kind_ref is not None:
        scores = scores + bias_block(kind_ref, tile_ref, head, step, first // HEAD_DIM, width)
    return scores


def forward_body(step, kind_ref, tile_ref, query_ref, key_ref, value_ref, out_ref, log_ref):
    width = query_ref.shape[-1]
    key_count = key_ref.shape[0]
    chunk = math.gcd(key_count, 1024)
    rows = query_ref.shape[0]
    lane = lax.broadcasted_iota(jnp.int32, (rows, 128), 1)
    logs = jnp.zeros((rows, 128), WIDE)
    tile_out = None
    for head in range(width // HEAD_DIM):
        lanes = head_lanes(head, width)
        query_head = only_head(query_ref[:, lanes[0] : lanes[1]], head) * jnp.asarray(0.125, LOW)

        def one_chunk(index, running):
            top, total, mixed = running
            first = index * chunk
            scores = chunk_scores(
                query_head, key_ref, lanes, first, chunk, head, step, kind_ref, tile_ref
            )
            values = value_ref[pl.ds(first, chunk), lanes[0] : lanes[1]]
            if key_count == chunk:
                top = jnp.max(scores, axis=1, keepdims=True)
                weights = jnp.exp(scores - top)
                total = jnp.sum(weights, axis=1, keepdims=True)
                return top, total, jnp.dot(weights.astype(LOW), values, preferred_element_type=WIDE)
            new_top = jnp.maximum(top, jnp.max(scores, axis=1, keepdims=True))
            weights = jnp.exp(scores - new_top)
            shrink = jnp.exp(top - new_top)
            total = total * shrink + jnp.sum(weights, axis=1, keepdims=True)
            mixed = mixed * shrink + jnp.dot(
                weights.astype(LOW), values, preferred_element_type=WIDE
            )
            return new_top, total, mixed

        running = (
            jnp.full((rows, 1), -1e29, WIDE),
            jnp.zeros((rows, 1), WIDE),
            jnp.zeros((rows, lanes[1] - lanes[0]), WIDE),
        )
        if key_count == chunk:
            running = one_chunk(0, running)
        else:
            running = lax.fori_loop(0, key_count // chunk, one_chunk, running)
        top, total, mixed = running
        mixed = only_head(mixed / total, head)
        logs = jnp.where(lane == head, top + jnp.log(total), logs)
        tile_out = mixed if head % 2 == 0 else tile_out + mixed
        if head % 2 == 1 or head == width // HEAD_DIM - 1:
            out_ref[:, lanes[0] : lanes[1]] = tile_out.astype(LOW)
    log_ref[...] = logs


def backward_body(
    step, kind_ref, tile_ref, query_ref, up_ref, log_ref, key_ref, value_ref, dq_ref, dk_ref, dv_ref, sums
):
    width = query_ref.shape[-1]
    key_count = key_ref.shape[0]
    chunk = math.gcd(key_count, 1024)
    rows = query_ref.shape[0]
    tile_out = None
    for head in range(width // HEAD_DIM):
        lanes = head_lanes(head, width)
        query_head = only_head(query_ref[:, lanes[0] : lanes[1]], head) * jnp.asarray(0.125, LOW)
        up_head = only_head(up_ref[:, lanes[0] : lanes[1]], head)
        log_head = log_ref[:, head : head + 1]

        def probs_of(first):
            scores = chunk_scores(
                query_head, key_ref, lanes, first, chunk, head, step, kind_ref, tile_ref
            )
            probs = jnp.exp(scores - log_head)
            values = value_ref[pl.ds(first, chunk), lanes[0] : lanes[1]]
            prob_grad = lax.dot_general(up_head, values, NT, preferred_element_type=WIDE)
            return probs, prob_grad

        def finish(first, probs, prob_grad, delta):
            score_grad = probs * (prob_grad - delta)
            if sums is not None:
                for half in range(2):
                    for pair in range(chunk // 128):
                        block = first // HEAD_DIM + 2 * pair
                        left = kind_ref[2 * step + half, block]
                        right = kind_ref[2 * step + half, block + 1]
                        piece = score_grad[
                            half * HEAD_DIM : (half + 1) * HEAD_DIM, pair * 128 : (pair + 1) * 128
                        ]
                        sums[0, head, left] += piece
                        sums[1, head, right] += piece
            score_low = score_grad.astype(LOW)
            here = pl.ds(first, chunk)
            dk_ref[here, lanes[0] : lanes[1]] += lax.dot_general(
                score_low, query_head, TN, preferred_element_type=WIDE
            )
            dv_ref[here, lanes[0] : lanes[1]] += lax.dot_general(
                probs.astype(LOW), up_head, TN, preferred_element_type=WIDE
            )
            keys = key_ref[here, lanes[0] : lanes[1]]
            return jnp.dot(score_low, keys, preferred_element_type=WIDE)

        if key_count == chunk:
            probs, prob_grad = probs_of(0)
            delta = jnp.sum(probs * prob_grad, axis=1, keepdims=True)
            query_grad = finish(0, probs, prob_grad, delta)
        else:

            def add_delta(index, delta):
                probs, prob_grad = probs_of(index * chunk)
                return delta + jnp.sum(probs * prob_grad, axis=1, keepdims=True)

            delta = lax.fori_loop(0, key_count // chunk, add_delta, jnp.zeros((rows, 1), WIDE))

            def add_grad(index, total):
                probs, prob_grad = probs_of(index * chunk)
                return total + finish(index * chunk, probs, prob_grad, delta)

            query_grad = lax.fori_loop(
                0, key_count // chunk, add_grad, jnp.zeros((rows, lanes[1] - lanes[0]), WIDE)
            )
        query_grad = only_head(query_grad * 0.125, head)
        tile_out = query_grad if head % 2 == 0 else tile_out + query_grad
        if head % 2 == 1 or head == width // HEAD_DIM - 1:
            dq_ref[:, lanes[0] : lanes[1]] = tile_out.astype(LOW)


def load_keys(own_ref, rest_ref, key_ref, value_ref):
    own, width = own_ref.shape[0], key_ref.shape[1]
    key_ref[:own] = own_ref[:, :width]
    key_ref[own:] = rest_ref[:, :width]
    value_ref[:own] = own_ref[:, width:]
    value_ref[own:] = rest_ref[:, width:]


def self_forward_kernel(first, kind_ref, tile_ref, query_ref, own_ref, rest_ref, *refs):
    outs, log_ref, out_ref, key_ref, value_ref = refs[:-4], refs[-4], refs[-3], refs[-2], refs[-1]

    @pl.when(pl.program_id(0) == 0)
    def start():
        load_keys(own_ref, rest_ref, key_ref, value_ref)

    forward_body(
        first + pl.program_id(0), kind_ref, tile_ref, query_ref, key_ref, value_ref, out_ref, log_ref
    )
    for k in range(len(outs)):

        @pl.when(pl.program_id(0) == k)
        def store():
            outs[k][...] = out_ref[...]


def self_backward_kernel(first, last, kind_ref, tile_ref, query_ref, up_ref, log_ref, own_ref, rest_ref, *refs):
    if first > 0:
        dk_start, dv_start, sums_start = refs[:3]
        refs = refs[3:]
    dq_ref, outs, (key_ref, value_ref, dk_ref, dv_ref) = refs[0], refs[1:4], refs[4:]
    sums = outs[2]

    @pl.when(pl.program_id(0) == 0)
    def start():
        load_keys(own_ref, rest_ref, key_ref, value_ref)
        if first > 0:
            dk_ref[...] = dk_start[...]
            dv_ref[...] = dv_start[...]
            sums[...] = sums_start[...]
        else:
            dk_ref[...] = jnp.zeros_like(dk_ref)
            dv_ref[...] = jnp.zeros_like(dv_ref)
            sums[...] = jnp.zeros_like(sums)

    backward_body(
        first + pl.program_id(0),
        kind_ref,
        tile_ref,
        query_ref,
        up_ref,
        log_ref,
        key_ref,
        value_ref,
        dq_ref,
        dk_ref,
        dv_ref,
        sums,
    )

    @pl.when(pl.program_id(0) == pl.num_programs(0) - 1)
    def end():
        if last:
            own, width = own_ref.shape[0], key_ref.shape[1]
            for out, here in ((outs[0], slice(0, own)), (outs[1], slice(own, None))):
                out[:, :width] = dk_ref[here].astype(LOW)
                out[:, width:] = dv_ref[here].astype(LOW)
        else:
            outs[0][...] = dk_ref[...]
            outs[1][...] = dv_ref[...]


def cross_forward_kernel(query_ref, key_ref, value_ref, out_ref, log_ref):
    forward_body(0, None, None, query_ref, key_ref, value_ref, out_ref, log_ref)


def cross_backward_kernel(
    query_ref, up_ref, log_ref, key_ref, value_ref, dq_ref, dk_out, dv_out, dk_ref, dv_ref
):
    dk_ref[...] = jnp.zeros_like(dk_ref)
    dv_ref[...] = jnp.zeros_like(dv_ref)
    backward_body(
        0, None, None, query_ref, up_ref, log_ref, key_ref, value_ref, dq_ref, dk_ref, dv_ref, None
    )
    dk_out[...] = dk_ref[...].astype(LOW)
    dv_out[...] = dv_ref[...].astype(LOW)


def whole_block(shape):
    return pl.BlockSpec(shape, lambda *index: (0,) * len(shape))


def row_block(rows, width):
    return pl.BlockSpec((rows, width), lambda i, *rest: (i, 0))


def lane_block(rows):
    return pl.BlockSpec((rows, 128), lambda i, *rest: (0, i))


def self_forward(first, last, kinds, tiles, queries, own, rest):
    width = queries.shape[1]
    rows = 2 * HEAD_DIM
    keys = own.shape[0] + rest.shape[0]
    blocks = last - first
    return pl.pallas_call(
        partial(self_forward_kernel, first),
        grid_spec=pltpu.PrefetchScalarGridSpec(
            num_scalar_prefetch=1,
            grid=(blocks,),
            in_specs=[
                whole_block(tiles.shape),
                pl.BlockSpec((rows, width), lambda i, *refs: (first + i, 0)),
                whole_block(own.shape),
                whole_block(rest.shape),
            ],
            out_specs=[whole_block((rows, width))] * blocks + [row_block(rows, 128)],
            scratch_shapes=[
                pltpu.VMEM((rows, width), LOW),
                pltpu.VMEM((keys, width), LOW),
                pltpu.VMEM((keys, width), LOW),
            ],
        ),
        out_shape=[jax.ShapeDtypeStruct((rows, width), LOW)] * blocks
        + [jax.ShapeDtypeStruct((blocks * rows, 128), WIDE)],
        compiler_params=pltpu.CompilerParams(vmem_limit_bytes=VMEM_LIMIT),
        cost_estimate=takes(2.2 * blocks),
        name="self_forward",
    )(kinds, tiles, queries, own, rest)


def self_backward(first, last, kinds, tiles, queries, up_rows, logs, own, rest, start=()):
    count, width = queries.shape
    rows = 2 * HEAD_DIM
    done = last == count // rows
    keys = own.shape[0] + rest.shape[0]
    if done:
        shapes = [jax.ShapeDtypeStruct(own.shape, LOW), jax.ShapeDtypeStruct(rest.shape, LOW)]
    else:
        shapes = [jax.ShapeDtypeStruct((keys, width), WIDE)] * 2
    shapes.append(jax.ShapeDtypeStruct(tiles.shape, WIDE))

    def rows_at(lanes):
        return pl.BlockSpec((rows, lanes), lambda i, *refs: (first + i, 0))

    return pl.pallas_call(
        partial(self_backward_kernel, first, done),
        grid_spec=pltpu.PrefetchScalarGridSpec(
            num_scalar_prefetch=1,
            grid=(last - first,),
            in_specs=[
                whole_block(tiles.shape),
                rows_at(width),
                rows_at(width),
                rows_at(128),
                whole_block(own.shape),
                whole_block(rest.shape),
            ]
            + [whole_block(array.shape) for array in start],
            out_specs=[row_block(rows, width)] + [whole_block(shape.shape) for shape in shapes],
            scratch_shapes=[pltpu.VMEM((keys, width), LOW)] * 2
            + [pltpu.VMEM((keys, width), WIDE)] * 2,
        ),
        out_shape=[jax.ShapeDtypeStruct(((last - first) * rows, width), LOW)] + shapes,
        compiler_params=pltpu.CompilerParams(vmem_limit_bytes=VMEM_LIMIT),
        cost_estimate=takes(9),
        name="self_backward",
    )(kinds, tiles, queries, up_rows, logs, own, rest, *start)


def cross_forward(queries, keys, values):
    count, width = queries.shape
    key_count = keys.shape[0]
    return pl.pallas_call(
        cross_forward_kernel,
        in_specs=vmem(3),
        out_specs=vmem(2),
        out_shape=[
            jax.ShapeDtypeStruct((count, width), LOW),
            jax.ShapeDtypeStruct((count, 128), WIDE),
        ],
        compiler_params=pltpu.CompilerParams(vmem_limit_bytes=VMEM_LIMIT),
        cost_estimate=takes(6.6),
        name="cross_forward",
    )(queries, keys, values)


def cross_backward(queries, up_rows, logs, keys, values):
    count, width = queries.shape
    key_count = keys.shape[0]
    return pl.pallas_call(
        cross_backward_kernel,
        in_specs=vmem(5),
        out_specs=vmem(3),
        scratch_shapes=[pltpu.VMEM(keys.shape, WIDE), pltpu.VMEM(keys.shape, WIDE)],
        out_shape=[
            jax.ShapeDtypeStruct((count, width), LOW),
            jax.ShapeDtypeStruct(keys.shape, LOW),
            jax.ShapeDtypeStruct(keys.shape, LOW),
        ],
        compiler_params=pltpu.CompilerParams(vmem_limit_bytes=VMEM_LIMIT),
        cost_estimate=takes(8.2),
        name="cross_backward",
    )(queries, up_rows, logs, keys, values)


def tiles_kernel(bound_ref, bias_ref, out_ref):
    shape = (HEAD_DIM, 2 * HEAD_DIM)
    lane = lax.broadcasted_iota(jnp.int32, shape, 1)
    row = lax.broadcasted_iota(jnp.int32, shape, 0)
    left = lane < HEAD_DIM
    offset = row - lane % HEAD_DIM
    for head in range(OWN_HEADS):
        far = jnp.full(shape, bias_ref[BUCKETS - 1, head], WIDE)
        tiles = [jnp.full(shape, MASKED, WIDE)]
        for apart in range(3):
            tile = tiles[0]
            for bucket in range(BUCKETS):
                reached = offset + apart * HEAD_DIM >= bound_ref[bucket]
                tile = jnp.where(reached, bias_ref[bucket, head], tile)
            tiles.append(tile)
        for kind, tile in enumerate(tiles + [far]):
            out_ref[0, head, kind] = jnp.where(left, tile, 0.0)
            out_ref[1, head, kind] = jnp.where(left, 0.0, tile)


def bias_tiles(lower_bounds, own_bias):
    shape = (2, OWN_HEADS, 5, HEAD_DIM, 2 * HEAD_DIM)
    return pl.pallas_call(
        tiles_kernel,
        out_shape=jax.ShapeDtypeStruct(shape, WIDE),
        in_specs=[pl.BlockSpec(memory_space=pltpu.SMEM)] * 2,
        out_specs=pl.BlockSpec(memory_space=pltpu.VMEM),
        cost_estimate=takes(2.7),
        name="bias_tiles",
    )(lower_bounds, own_bias)


def bucket_sums(sums, lower_bounds):
    tiles = sums[0, :, 1:, :, :HEAD_DIM] + sums[1, :, 1:, :, HEAD_DIM:]
    shape = (3, HEAD_DIM, HEAD_DIM, BUCKETS)
    distance = (
        lax.broadcasted_iota(jnp.int32, shape, 0) * HEAD_DIM
        + lax.broadcasted_iota(jnp.int32, shape, 1)
        - lax.broadcasted_iota(jnp.int32, shape, 2)
    )
    upper_bounds = jnp.concatenate([lower_bounds[1:], jnp.full((1,), 1 << 30, jnp.int32)])
    hot = ((distance >= lower_bounds) & (distance < upper_bounds)).astype(LOW)
    near = tiles[:, :3].reshape(OWN_HEADS, -1)
    high = near.astype(LOW)
    low = (near - high.astype(WIDE)).astype(LOW)
    both = jnp.dot(
        jnp.concatenate([high, low]), hot.reshape(-1, BUCKETS), preferred_element_type=WIDE
    )
    table = both[:OWN_HEADS] + both[OWN_HEADS:]
    far = jnp.sum(tiles[:, 3], axis=(1, 2))
    return table + jnp.where(jnp.arange(BUCKETS) == BUCKETS - 1, far[:, None], 0.0)


def rms_of(values):
    return lax.rsqrt(jnp.mean(values * values, axis=-1, keepdims=True) + EPSILON)


def norm_grad(values, inv_rms, gain, upstream):
    scaled = gain * upstream
    inner = jnp.mean(scaled * values, axis=-1, keepdims=True)
    return inv_rms * scaled - values * (inv_rms * inv_rms * inv_rms * inner)


def dot(left, right):
    return jnp.dot(left, right, preferred_element_type=WIDE)


def dot_nt(left, right):
    return lax.dot_general(left, right, NT, preferred_element_type=WIDE)


def dot_tn(left, right):
    return lax.dot_general(left, right, TN, preferred_element_type=WIDE)


def on_device(
    tokens,
    cotangent,
    encoder,
    expert_ids,
    block_order,
    bucket_table,
    first_gain,
    second_gain,
    third_gain,
    position_bias,
    query_weight,
    key_weight,
    value_weight,
    out_weight,
    cross_query,
    cross_key,
    cross_value,
    cross_out,
    router_weight,
    expert_in,
    expert_out,
):
    ctx_size = lax.axis_size("ctx")
    fsdp_size = lax.axis_size("fsdp")
    rests = rest_count()
    f_index = lax.axis_index("fsdp")
    ctx_index = lax.axis_index("ctx")
    core = ctx_index % 2
    group = (ctx_index // 2) % GROUP
    rest = ctx_index // (2 * GROUP)
    seq_count, span, width = tokens.shape
    shard = width // fsdp_size
    own_width = width // GROUP
    half_shard = shard // 2
    half_width = width // 2
    experts = expert_in.shape[0] * ctx_size
    capacity = (5 * seq_count * span + 4 * experts - 1) // (4 * experts)
    hidden_low = tokens.reshape(span, width)
    upstream = cotangent.reshape(span, width).astype(WIDE)

    gains = jnp.concatenate([first_gain, second_gain, third_gain]).reshape(3, shard)
    small = (gains, router_weight.T, position_bias)
    extra = small_rows(small)
    qkv_payload, early, late = pack_weights(
        small,
        (
            query_weight,
            key_weight,
            value_weight,
            out_weight,
            cross_key,
            cross_value,
            cross_query,
            cross_out,
        ),
        3,
        group,
        core,
    )
    first_hops = tie(*gather_group(hidden_low), *gather_fsdp(qkv_payload), early, late)
    own_rows = jnp.concatenate(first_hops[:GROUP])
    own_qkv, small_full = place_qkv(first_hops[GROUP : GROUP + fsdp_size], extra, f_index)
    early, late = first_hops[GROUP + fsdp_size :]
    early_x, early_y = swap_fsdp(early, 1), swap_fsdp(early, 2)
    expert_ids = after(expert_ids, qkv_payload)
    block_order, bucket_table, _ = tie(block_order, bucket_table, qkv_payload)

    gain_one = small_full[:, 0].reshape(width).astype(WIDE)
    gain_two = small_full[:, 1].reshape(width).astype(WIDE)
    gain_three = small_full[:, 2].reshape(width).astype(WIDE)
    router_full = small_full[:, 8 : 8 + experts].transpose(1, 0, 2).reshape(experts, width)
    bias_full = small_full[:, 8 + experts : 8 + experts + position_bias.shape[0], :HEADS]
    bias_full = bias_full.reshape(BUCKETS, HEADS)

    slots = jnp.arange(GROUP, dtype=jnp.int32)
    key_devices = (
        ((rest - jnp.arange(rests, dtype=jnp.int32)) % rests)[:, None, None] * (2 * GROUP)
        + (group ^ slots)[None, None, :] * 2
        + (core ^ jnp.arange(2, dtype=jnp.int32))[None, :, None]
    ).reshape(-1)
    key_blocks = (key_devices[:, None] * 2 + jnp.arange(2, dtype=jnp.int32)[None]).reshape(-1)
    block_count = block_order.shape[0]
    hits = key_blocks[:, None] == jnp.arange(block_count, dtype=jnp.int32)[None]
    key_places = jnp.sum(jnp.where(hits, block_order[None], 0), axis=1)
    query_places = key_places[: 2 * GROUP]
    kinds = jnp.clip(query_places[:, None] - key_places[None], -1, 3) + 1
    lower_bounds = jnp.sum(
        (bucket_table[:, None] < jnp.arange(BUCKETS, dtype=jnp.int32)[None]).astype(jnp.int32),
        axis=0,
    )
    own_bias = lax.dynamic_slice_in_dim(
        bias_full.astype(WIDE), group * OWN_HEADS, OWN_HEADS, 1
    )
    tiles = bias_tiles(lower_bounds, own_bias)

    routes = expert_ids.reshape(-1)
    chosen = routes[:, None] == jnp.arange(experts, dtype=jnp.int32)[None]
    order = jnp.arange(span)
    lower = (order[:, None] > order[None]).astype(LOW)
    earlier = dot(lower, chosen.astype(LOW))
    slot_rank = jnp.sum(jnp.where(chosen, earlier, 0.0), axis=1).astype(jnp.int32)
    block_rows = -(-2 * capacity // 8) * 8
    slot_rows = rests * GROUP * block_rows
    target = (
        (((routes // (2 * GROUP) - rest) % rests) * GROUP + (((routes // 2) % GROUP) ^ group))
        * block_rows
        + core * capacity
        + slot_rank
    )
    code = jnp.where(slot_rank < capacity, (routes % 2) * slot_rows + target, -1)
    own_code = jnp.broadcast_to(code.astype(WIDE)[:, None], (span, 128))
    other_code = swap_core(own_code)
    codes = jnp.concatenate([own_code[:, :1], other_code[:, :1]]).astype(jnp.int32)
    placing = (
        codes == core * slot_rows + jnp.arange(slot_rows, dtype=jnp.int32)[None]
    ).astype(LOW)
    chosen = chosen.astype(WIDE)

    wide_rows = own_rows.astype(WIDE)
    normed_own = (wide_rows * rms_of(wide_rows) * gain_one).astype(LOW)
    own_count = GROUP * span
    queries = dot(normed_own, own_qkv[:, :own_width]).astype(LOW)
    pairs_own = dot(normed_own, own_qkv[:, own_width:]).astype(LOW)
    pairs_rest = swap_core(pairs_own)
    encoder_pieces = gather_group(after(encoder, early).reshape(-1, width))
    pairs_own, pairs_rest, early_x, early_y = tie(pairs_own, pairs_rest, early_x, early_y)
    early_xy = swap_fsdp(early_x, 2)
    late_x, late_y = swap_fsdp(late, 1), swap_fsdp(late, 2)
    if rests > 1:
        near = jnp.concatenate([pairs_own, pairs_rest])
        pairs_rest = jnp.concatenate(
            [pairs_rest] + [shift_rest(near, r) for r in range(1, rests)]
        )
    half_group = GROUP // 2
    *far, far_logs = self_forward(
        half_group, GROUP, kinds, tiles, queries, pairs_own, pairs_rest
    )
    pairs_own, *far = tie(pairs_own, *far)
    far = [swap_group(piece, half_group + k) for k, piece in enumerate(far)]
    *attended, near_logs = self_forward(
        0, half_group, kinds, tiles, queries, pairs_own, pairs_rest
    )
    attended, far, early_xy, late_x, encoder_pieces = tie(
        attended, far, early_xy, late_x, encoder_pieces
    )
    self_logs = jnp.concatenate([near_logs, far_logs])
    attended = [attended[0]] + [swap_group(attended[k], k) for k in range(1, half_group)] + far
    late_xy = swap_fsdp(late_x, 2)
    early_mine = stack_pieces((early, early_x, early_y, early_xy), 1, f_index, group)
    early_theirs = swap_core(early_mine)
    encoder_own = jnp.concatenate(encoder_pieces)
    encoder_other = swap_core(encoder_own)
    *attended, early_theirs, encoder_other = tie(*attended, early_theirs, encoder_other)
    out_full, cross_k_full, cross_v_full = weave_halves(early_mine, early_theirs, core)
    encoder_all = jnp.concatenate([encoder_own, encoder_other])
    if rests > 1:
        encoder_all = jnp.concatenate(
            [encoder_all] + [shift_rest(encoder_all, r) for r in range(1, rests)]
        )
    attended = jnp.concatenate(attended, axis=1)
    hidden = hidden_low.astype(WIDE)
    first_sum = hidden + dot(attended, out_full)
    inv_two = rms_of(first_sum)
    normed_two = (first_sum * inv_two * gain_two).astype(LOW)
    normed_two, late_xy, late_y = tie(normed_two, late_xy, late_y)
    late_mine = stack_pieces((late, late_x, late_y, late_xy), 0, f_index, group)
    late_theirs = swap_core(late_mine)

    cross_keys = dot(after(encoder_all, late_mine), cross_k_full).astype(LOW)
    cross_values = dot(encoder_all, cross_v_full).astype(LOW)
    cross_q_full, cross_o_full = weave_halves(late_mine, late_theirs, core)
    cross_rows = dot(normed_two, cross_q_full).astype(LOW)
    cross_mixed, cross_logs = cross_forward(cross_rows, cross_keys, cross_values)
    second_sum = first_sum + dot(cross_mixed, cross_o_full)
    inv_three = rms_of(second_sum)
    normed_three = (second_sum * inv_three * gain_three).astype(LOW)

    logits = dot_nt(normed_three, router_full)
    router_probs = jax.nn.softmax(logits, axis=-1)
    gate_value = jnp.sum(router_probs * chosen, axis=-1, keepdims=True)
    scaled_up = (gate_value * upstream).astype(LOW)

    sides = jnp.concatenate([normed_three, scaled_up], axis=1)
    sides = jnp.concatenate([sides, swap_core(sides)])
    sent = dot_tn(placing, sides).astype(LOW).reshape(rests, GROUP * block_rows, 2 * width)
    near = jnp.concatenate(
        [sent[0]] + [shift_rest(sent[r], r) for r in range(1, rests)]
    ).reshape(rests, GROUP, block_rows, 2 * width)
    arrived = jnp.concatenate(
        [near[:, 0]] + [swap_group(near[:, k], k) for k in range(1, GROUP)], axis=1
    ).reshape(slot_rows, 2 * width)
    arrivals = list(gather_fsdp(arrived))
    near_count = fsdp_size // 2
    answers, middle = run_experts(arrivals[:near_count], expert_in[0], expert_out[0])
    answers, middle, arrivals[near_count:] = tie(answers, middle, arrivals[near_count:])
    more_answers, more_middle = run_experts(arrivals[near_count:], expert_in[0], expert_out[0])
    answers = answers + more_answers
    answers = tie(answers[0], *[swap_fsdp(answers[k], k) for k in range(1, fsdp_size)])
    answers = sum_home(answers, rests)
    near = [answers[0]] + [swap_group(answers[k], k) for k in range(1, GROUP)]
    near = jnp.concatenate(
        [piece.reshape(rests, block_rows, 2 * width) for piece in near], axis=1
    )
    home = jnp.concatenate([near[0]] + [shift_rest(near[r], -r) for r in range(1, rests)])
    both = dot(placing, home).astype(LOW)
    both = both[:span].astype(WIDE) + swap_core(both[span:]).astype(WIDE)
    moe_rows, dispatch_grad = both[:, :width], both[:, width:]
    grad_expert_in, grad_expert_out = expert_grads(arrivals, (middle, more_middle))
    grad_expert_in, grad_expert_out = grad_expert_in[None], grad_expert_out[None]

    mixed_out = (second_sum + gate_value * moe_rows).astype(LOW).reshape(tokens.shape)
    gate_grad = jnp.sum(upstream * moe_rows, axis=-1, keepdims=True)
    logit_low = (gate_grad * gate_value * (chosen - router_probs)).astype(LOW)
    three_grad = dispatch_grad + dot(logit_low, router_full)
    second_grad = upstream + norm_grad(second_sum, inv_three, gain_three, three_grad)
    gain_three_part = jnp.sum(three_grad * second_sum * inv_three, axis=0, keepdims=True)
    router_part = dot_tn(logit_low, normed_three)
    spread = jnp.concatenate([router_part, gain_three_part])
    spread = jnp.pad(spread, ((0, -spread.shape[0] % 16), (0, 0)))

    branch_two = second_grad.astype(LOW)
    cross_up = dot_nt(branch_two, cross_o_full).astype(LOW)
    cross_q_low, cross_k_part, cross_v_part = cross_backward(
        cross_rows, cross_up, cross_logs, cross_keys, cross_values
    )
    two_grad = dot_nt(cross_q_low, cross_q_full)
    first_grad = second_grad + norm_grad(first_sum, inv_two, gain_two, two_grad)

    branch_one = first_grad.astype(LOW)
    self_up = dot_nt(branch_one, out_full).astype(LOW)
    branch_one, self_up = tie(branch_one, self_up)
    up_pieces = [self_up[:, :own_width]] + [
        swap_group(self_up[:, k * own_width : (k + 1) * own_width], k) for k in range(1, GROUP)
    ]
    extra_rows = -(-spread.shape[0] // 64) * 64
    keep, send = weight_grads(
        (False, False, False, False, True),
        (
            (cross_mixed, branch_two),
            (normed_two, cross_q_low),
            (encoder_all, cross_k_part),
            (encoder_all, cross_v_part),
            (attended, branch_one),
        ),
        spread,
        extra_rows,
        f_index,
        core,
        group,
        fsdp_size,
    )
    *up_pieces, received = tie(*up_pieces, swap_core(send))
    up_own = jnp.concatenate(up_pieces)
    middle = keep.shape[1] // 2
    top = [add_low(keep[k, :middle], received[k, :middle]) for k in range(fsdp_size)]
    up_own, top[1:] = tie(up_own, top[1:])
    top = [top[0]] + [swap_fsdp(top[k], k) for k in range(1, fsdp_size)]
    query_low, pair_own, pair_rest, bias_parts = self_backward(
        0, own_count // span, kinds, tiles, queries, up_own, self_logs, pairs_own, pairs_rest
    )
    query_low, pair_own, pair_rest, bias_parts, top, keep, received = tie(
        query_low, pair_own, pair_rest, bias_parts, top, keep, received
    )
    bottom = [add_low(keep[k, middle:], received[k, middle:]) for k in range(fsdp_size)]
    bottom = [bottom[0]] + [swap_fsdp(bottom[k], k) for k in range(1, fsdp_size)]
    if rests > 1:
        near = jnp.concatenate([pair_own, pair_rest[:own_count]]).astype(WIDE)
        for r in range(1, rests):
            first = (2 * r - 1) * own_count
            piece = pair_rest[first : first + 2 * own_count]
            near = near + shift_rest(piece, -r).astype(WIDE)
        pair_own, pair_rest = near[:own_count].astype(LOW), near[own_count:].astype(LOW)
    one_parts, qkv_keep, qkv_send = key_grads(
        normed_own, query_low, pair_own, swap_core(pair_rest), own_qkv, f_index, core, fsdp_size
    )
    one_parts = [one_parts[0]] + [swap_group(one_parts[k], k) for k in range(1, GROUP)]
    qkv_send, bottom, bias_parts, one_parts[1] = tie(
        swap_core(qkv_send), bottom, bias_parts, one_parts[1]
    )
    qkv_send, *quarters = tie(qkv_send, *sum_quarters(top, bottom, group))
    quarters = [quarters[0]] + [swap_group(quarters[k], k) for k in range(1, GROUP)]

    table = jnp.pad(bucket_sums(bias_parts, lower_bounds).T, ((0, 0), (0, 128 - OWN_HEADS)))
    qkv_parts = add_qkv(qkv_keep, qkv_send, table, f_index)
    qkv_parts = [qkv_parts[0]] + [swap_fsdp(qkv_parts[k], k) for k in range(1, fsdp_size)]
    qkv_parts, one_parts, quarters, grad_expert_in, grad_expert_out = tie(
        qkv_parts, one_parts, quarters, grad_expert_in, grad_expert_out
    )
    dense_shard = sum_rest(sum_low(quarters[0], quarters[1:])).astype(LOW)
    one_grad = sum(one.astype(WIDE) for one in one_parts)
    tokens_grad = first_grad + norm_grad(hidden, rms_of(hidden), gain_one, one_grad)
    tokens_grad = tokens_grad.reshape(tokens.shape)
    qkv_shard = sum_rest(sum_low(qkv_parts[0], qkv_parts[1:])).astype(LOW)
    spots = [group ^ k for k in range(GROUP)]
    qkv_mine = collect(gather_group(qkv_shard), spots)
    query_total, key_total, value_total, bias_total, grad_gain_one = finish_qkv(
        qkv_mine,
        swap_core(qkv_mine),
        (query_weight, key_weight, value_weight),
        first_gain,
        core,
        position_bias.shape,
    )
    dense_pieces, query_total, tokens_grad = tie(
        gather_group(dense_shard), query_total, tokens_grad
    )
    (
        cross_o_total,
        cross_q_total,
        cross_k_total,
        cross_v_total,
        out_total,
        grad_router,
        grad_gain_three,
        grad_gain_two,
    ) = finish_weights(
        dense_pieces,
        [swap_core(piece) for piece in dense_pieces],
        cross_query,
        second_gain,
        group,
        core,
        experts,
    )

    return (
        mixed_out,
        tokens_grad,
        grad_gain_one,
        grad_gain_two,
        grad_gain_three,
        bias_total,
        query_total,
        key_total,
        value_total,
        out_total,
        cross_q_total,
        cross_k_total,
        cross_v_total,
        cross_o_total,
        grad_router,
        grad_expert_in,
        grad_expert_out,
    )


def solution(mesh):
    rows = P("fsdp", "ctx", None)
    vector = P("fsdp")
    matrix = P("fsdp", None)
    expert_specs = (P("ctx", None, "fsdp"), P("ctx", "fsdp", None))
    return jax.shard_map(
        on_device,
        mesh=mesh,
        in_specs=(rows,) * 4 + (P(),) * 2 + (vector,) * 3 + (matrix,) * 10 + expert_specs,
        out_specs=(rows,) * 2 + (vector,) * 3 + (matrix,) * 10 + expert_specs,
        check_vma=False,
    )
```
